32 devices in a mesh: groups: 2 (over x), store: 16 (over z, y, core).
Axes of the slice: x: 2, y: 2, z: 4, core: 2. Of those that a mesh axis runs over, the one named last changes fastest.
Arguments:
- tokens: bfloat16 [24576, 8192], P(('groups', 'store')), parts along dimension 0, may hold values from -400 to 400
- input_norm_gain: bfloat16 [8192], replicated, may hold values from 0.5 to 1.5
- value_matrix: bfloat16 [8192, 1024], P('store'), may hold values from -0.0625 to 0.0625
- adapter_down_factors: bfloat16 [8192, 16, 64], P('store'), may hold values from -0.0625 to 0.0625
- adapter_up_factors: bfloat16 [16, 64, 1024], P(None, None, 'store'), may hold values from -0.75 to 0.75
- document_lengths: int32 [32, 4], P(('groups', 'store')), parts along dimension 0, may hold values from 1 to 384, 768 in all within a row
- document_tenant: int32 [32, 4], P(('groups', 'store')), parts along dimension 0, may hold values from 0 to 15
- tenant_adapter_slot: int32 [16], replicated, may hold values from 0 to 15, each once
Outputs:
- values_out: bfloat16 [24576, 1024], P(('groups', 'store')), parts along dimension 0
The draws below stay inside these ranges and needn't reach their ends.
There are 2 independent parts, one for each index of `groups`. The reference program is written for one: setup_inputs(seed, part) draws one part's arguments, and reference() takes and returns one part's arrays. A program takes and returns all parts, laid end to end along the dimension named above; an argument that names none is the same for every part. Nothing has to cross between parts.
Inputs may be any that keep to these rules, and one draw needn't show every extreme that they name: `document_lengths`: each row sums to 768. `tenant_adapter_slot`: A permutation of the slots.
All inputs are finite; a program needn't handle non-finite values.
Results may differ from the reference program's by a relative error of at most 0.0056.
Values may be sent and summed in bfloat16 or wider, within the bound.
No kernel may reach another device: no remote copies, remote signals or barrier semaphores. Data moves between devices by JAX's collectives and lax.ppermute only.
A program may use at most 128 MiB of HBM per device.

```python
import math
import jax
import jax.numpy as jnp
import numpy as np
from jax import lax

MODEL_WIDTH = 8192
KEY_VALUE_HEADS = 8
HEAD_SIZE = 128
ADAPTER_RANK = 64
TENANT_ADAPTERS = 16
TOK_DEV = 768
DOC_DEV = 4
VALUE_COLUMNS = 1024
MOST = 384
TOKENS = 12288
N_STORE = 16


def draw_tokens(key, part):
    key = jax.random.fold_in(key, 11)
    noise_key, row_key, col_key = jax.random.split(key, 3)
    noise = jnp.clip(jax.random.normal(noise_key, (TOKENS, MODEL_WIDTH), jnp.float32), -4.0, 4.0)
    col_top = math.log(10.0)
    row_scale = jnp.exp(jax.random.uniform(row_key, (TOKENS, 1), jnp.float32, 0.0, math.log(10.0)))
    col_scale = jnp.exp(jax.random.uniform(col_key, (1, MODEL_WIDTH), jnp.float32, 0.0, col_top))
    return jnp.clip(noise * row_scale * col_scale * 0.25, -400.0, 400.0).astype(jnp.bfloat16)


def plant(entries, own_key, least, high):
    index_at = [jax.random.randint(jax.random.fold_in(own_key, axis), (), 0, length) for axis, length in enumerate(entries.shape)]
    widest = entries.shape.index(max(entries.shape))
    beside = index_at[:widest] + [(index_at[widest] + 1) % entries.shape[widest]] + index_at[widest + 1:]
    return entries.at[tuple(index_at)].set(least).at[tuple(beside)].set(high)


def block_scale(own_key, dims, pieces, low, top_value):
    gain = 1.0
    for dim, parts in pieces:
        steps = jax.random.uniform(jax.random.fold_in(jax.random.fold_in(own_key, 6), dim), (parts,), jnp.float32, low / len(pieces), top_value / len(pieces))
        gain = gain * jnp.repeat(jnp.exp(steps), dims[dim] // parts).reshape((-1,) + (1,) * (len(dims) - 1 - dim))
    return gain


def length_profile(number_of, total, most, lean):
    loads = [(1 << 20) // math.isqrt(standing ** lean) + 1 for standing in range(2, number_of + 1)]
    surplus, given = total - most - (number_of - 1), [1] * (number_of - 1)
    while surplus > 0:
        movable = [i for i in range(number_of - 1) if given[i] < most]
        pool, left = sum([loads[i] for i in movable]), surplus
        for i in movable:
            more = min(most - given[i], max(1, left * loads[i] // pool), surplus)
            given[i] = given[i] + more
            surplus = surplus - more
    return np.array([most] + given)


def uneven_parts(stream_key, number_of, total, most, skew):
    if number_of == 2:
        one = jax.random.randint(stream_key, (), max(1, total - most), min(most, total - 1) + 1)
        return jnp.stack([one, total - one])
    tallies = jnp.asarray(length_profile(number_of, total, most, skew), jnp.int32)
    couples = (number_of - 1) // 2
    donor, receiver = tallies[1:1 + 2 * couples:2], tallies[2:2 + 2 * couples:2]
    margin = jnp.minimum(donor - 1, most - receiver)
    moved = jax.random.randint(jax.random.fold_in(stream_key, 1), (couples,), 0, 1 << 20) % (margin + 1)
    tallies = tallies.at[1:1 + 2 * couples:2].set(donor - moved).at[2:2 + 2 * couples:2].set(receiver + moved)
    return tallies[jax.random.permutation(jax.random.fold_in(stream_key, 2), number_of)]


def scatter_about(stream_key, dims, spread, bound, cuts=(), kind=jnp.bfloat16):
    array = jax.random.normal(stream_key, dims, jnp.float32) * spread
    if len(cuts) > 0:
        array = block_scale(stream_key, dims, cuts, -0.22, 0.18) * array
    return jnp.clip(array, min=-bound, max=bound).astype(kind)


def setup_inputs(seed: int = 0, part: int = 0) -> dict:
    key_list = jax.random.split(jax.random.key(seed), 9)
    part_keys = jax.random.split(jax.random.fold_in(key_list[8], part), 9)
    return {
        "tokens": draw_tokens(jax.random.fold_in(jax.random.fold_in(key_list[8], part), 71), part),
        "input_norm_gain": jnp.clip(1.0 + 0.1 * jax.random.normal(key_list[1], (MODEL_WIDTH,), jnp.float32), 0.5, 1.5).astype(jnp.bfloat16),
        "value_matrix": scatter_about(key_list[2], (MODEL_WIDTH, VALUE_COLUMNS), MODEL_WIDTH ** -0.5, 0.0625, ((0, 16),)),
        "adapter_down_factors": scatter_about(key_list[3], (MODEL_WIDTH, TENANT_ADAPTERS, ADAPTER_RANK), MODEL_WIDTH ** -0.5, 0.0625, ((0, 16),)),
        "adapter_up_factors": scatter_about(key_list[4], (TENANT_ADAPTERS, ADAPTER_RANK, VALUE_COLUMNS), ADAPTER_RANK ** -0.5, 0.75, ((2, 16),)),
        "document_lengths": jax.vmap(lambda own: uneven_parts(own, DOC_DEV, TOK_DEV, MOST, 2))(jax.random.split(part_keys[5], N_STORE)).reshape((N_STORE, DOC_DEV)).astype(jnp.int32),
        "document_tenant": plant(jax.random.randint(part_keys[6], (N_STORE, DOC_DEV), 0, TENANT_ADAPTERS), jax.random.fold_in(part_keys[6], 1), 0, TENANT_ADAPTERS - 1).astype(jnp.int32),
        "tenant_adapter_slot": jax.random.permutation(key_list[7], TENANT_ADAPTERS).astype(jnp.int32),
    }


adapter_scale = 2.0

def token_slots(lengths, tenants, tenant_adapter_slot, row_count):
    ends = jnp.cumsum(lengths).astype(jnp.int32)
    position = jnp.arange(row_count, dtype=jnp.int32)
    doc_index = lax.optimization_barrier(jnp.sum((position[:, None] >= ends[None, :]).astype(jnp.int32), axis=1))
    doc_pick = (doc_index[:, None] == jnp.arange(lengths.shape[0], dtype=jnp.int32)[None, :]).astype(jnp.int32)
    tenant = lax.optimization_barrier(jnp.sum(doc_pick * tenants[None, :], axis=1))
    tenant_pick = (tenant[:, None] == jnp.arange(tenant_adapter_slot.shape[0], dtype=jnp.int32)[None, :]).astype(jnp.int32)
    return lax.optimization_barrier(jnp.sum(tenant_pick * tenant_adapter_slot[None, :], axis=1)).astype(jnp.int32)

def normalize(tokens, input_norm_gain):
    wide = tokens.astype(jnp.float32)
    meansq = lax.optimization_barrier(jnp.mean(wide * wide, axis=1, keepdims=True))
    return (wide * lax.rsqrt(meansq + 1e-05) * input_norm_gain.astype(jnp.float32)).astype(jnp.bfloat16)

def reference(tokens, input_norm_gain, value_matrix, adapter_down_factors, adapter_up_factors, document_lengths, document_tenant, tenant_adapter_slot):
    normed_input = normalize(tokens, input_norm_gain)
    base_output = jnp.dot(normed_input, value_matrix, preferred_element_type=jnp.float32)
    slots = jax.vmap(lambda lens, tens: token_slots(lens, tens, tenant_adapter_slot, TOK_DEV))(document_lengths, document_tenant)
    slots = slots.reshape(TOKENS)
    select = (slots[:, None] == jnp.arange(TENANT_ADAPTERS, dtype=jnp.int32)[None, :]).astype(jnp.float32)
    rank_total_rows = jnp.dot(normed_input, adapter_down_factors.reshape(MODEL_WIDTH, TENANT_ADAPTERS * ADAPTER_RANK), preferred_element_type=jnp.float32)
    mid = lax.optimization_barrier(jnp.sum(rank_total_rows.reshape(TOKENS, TENANT_ADAPTERS, ADAPTER_RANK) * select[:, :, None], axis=1)).astype(jnp.bfloat16)
    expanded_rows = (mid[:, None, :] * select.astype(jnp.bfloat16)[:, :, None]).reshape(TOKENS, TENANT_ADAPTERS * ADAPTER_RANK)
    adapter_update = jnp.dot(expanded_rows, adapter_up_factors.reshape(TENANT_ADAPTERS * ADAPTER_RANK, KEY_VALUE_HEADS * HEAD_SIZE), preferred_element_type=jnp.float32)
    return (base_output + adapter_scale * adapter_update).astype(jnp.bfloat16)
```

```python
import functools

import jax
import jax.numpy as jnp
from jax import lax
from jax.experimental import pallas as pl
from jax.experimental.pallas import tpu as pltpu
from jax.sharding import PartitionSpec as P

adapter_scale = 2.0
cores, rows_y, lane = 2, 2, 128
nt = (((1,), (1,)), ((), ()))


def token_slots(lengths, tenants, tenant_adapter_slot, row_count):
    ends = jnp.cumsum(lengths)
    position = jnp.arange(row_count, dtype=jnp.int32)
    doc_index = jnp.sum((position[:, None] >= ends[None, :]).astype(jnp.int32), axis=1)
    doc_pick = (
        doc_index[:, None] == jnp.arange(lengths.shape[0], dtype=jnp.int32)[None, :]
    ).astype(jnp.int32)
    tenant = jnp.sum(doc_pick * tenants[None, :], axis=1)
    tenant_pick = (
        tenant[:, None] == jnp.arange(tenant_adapter_slot.shape[0], dtype=jnp.int32)[None, :]
    ).astype(jnp.int32)
    return jnp.sum(tenant_pick * tenant_adapter_slot[None, :], axis=1)


def pick_rank(rank_total_rows, slots, count_of_adapters, rank_span_width):
    select = (slots[:, None] == jnp.arange(count_of_adapters, dtype=jnp.int32)[None, :]).astype(
        jnp.float32
    )
    shaped = rank_total_rows.reshape(slots.shape[0], count_of_adapters, rank_span_width)
    return jnp.sum(shaped * select[:, :, None], axis=1)


def plain(
    tokens,
    input_norm_gain,
    value_matrix,
    adapter_down_factors,
    adapter_up_factors,
    document_lengths,
    document_tenant,
    tenant_adapter_slot,
):
    row_count = tokens.shape[0]
    count_of_adapters = adapter_down_factors.shape[1]
    rank_span_width = adapter_down_factors.shape[2]
    flat_width = count_of_adapters * rank_span_width
    wide = tokens.astype(jnp.float32)
    meansq = jnp.mean(wide * wide, axis=1, keepdims=True)
    normed = (wide * lax.rsqrt(meansq + 1e-05) * input_norm_gain.astype(jnp.float32)).astype(
        jnp.bfloat16
    )
    slots = token_slots(document_lengths[0], document_tenant[0], tenant_adapter_slot, row_count)
    base_output = jnp.dot(
        normed,
        lax.all_gather(value_matrix, "store", axis=0, tiled=True),
        preferred_element_type=jnp.float32,
    )
    down = lax.all_gather(adapter_down_factors, "store", axis=0, tiled=True)
    rank_total_rows = jnp.dot(
        normed, down.reshape(down.shape[0], flat_width), preferred_element_type=jnp.float32
    )
    mid = pick_rank(rank_total_rows, slots, count_of_adapters, rank_span_width)
    mid = mid.astype(jnp.bfloat16)
    select = (slots[:, None] == jnp.arange(count_of_adapters, dtype=jnp.int32)[None, :]).astype(
        jnp.bfloat16
    )
    expanded_rows = (mid[:, None, :] * select[:, :, None]).reshape(row_count, flat_width)
    up = lax.all_gather(adapter_up_factors, "store", axis=2, tiled=True)
    adapter_update = jnp.dot(
        expanded_rows, up.reshape(flat_width, up.shape[2]), preferred_element_type=jnp.float32
    )
    return (base_output + adapter_scale * adapter_update).astype(jnp.bfloat16)


def norm_kernel(source_ref, tokens_ref, gain_ref, own_ref, other_ref):
    width = tokens_ref.shape[1]
    half = width // 2
    total = jnp.zeros((tokens_ref.shape[0], lane), jnp.float32)
    for i in range(width // lane):
        part = tokens_ref[:, i * lane : (i + 1) * lane].astype(jnp.float32)
        total += part * part
    scale = lax.rsqrt(jnp.sum(total, axis=1, keepdims=True) / width + 1e-05)
    for out_ref, first in ((own_ref, 0), (other_ref, half // lane)):
        for i in range(half // lane):
            start = pl.multiple_of(source_ref[first + i], lane)
            part = tokens_ref[:, pl.ds(start, lane)].astype(jnp.float32)
            gain = gain_ref[:, pl.ds(start, lane)].astype(jnp.float32)
            out_ref[:, i * lane : (i + 1) * lane] = (part * scale * gain).astype(jnp.bfloat16)


def norm_in_order(tokens, gain, source):
    rows, width = tokens.shape
    block = 64
    half = jax.ShapeDtypeStruct((rows, width // 2), jnp.bfloat16)
    return pl.pallas_call(
        norm_kernel,
        out_shape=(half, half),
        grid_spec=pltpu.PrefetchScalarGridSpec(
            num_scalar_prefetch=1,
            grid=(rows // block,),
            in_specs=[
                pl.BlockSpec((block, width), lambda i, *_: (i, 0)),
                pl.BlockSpec((1, width), lambda i, *_: (0, 0)),
            ],
            out_specs=[pl.BlockSpec((block, width // 2), lambda i, *_: (i, 0))] * 2,
        ),
        compiler_params=pltpu.CompilerParams(vmem_limit_bytes=16 << 20),
        cost_estimate=pl.CostEstimate(
            flops=6 * rows * width, bytes_accessed=4 * rows * width, transcendentals=rows
        ),
    )(source, tokens, gain.reshape(1, width))


def fixed(array):
    return pl.BlockSpec(array.shape, lambda i, *_: (0,) * array.ndim, pipeline_mode=pl.Buffered(1))


def tiled(array, tile):
    return pl.BlockSpec((tile,) + array.shape[1:], lambda i, *_: (i, 0))


def mid_kernel(docs, rank, pieces, ends_ref, slots_ref, *refs):
    token_refs, down_refs, out_refs = refs[:2], refs[2:-2], refs[-2:]
    tile = token_refs[0].shape[0]
    shard = sum(down_refs[i].shape[1] for i in pieces[0])
    row = pl.program_id(0) * tile + lax.broadcasted_iota(jnp.int32, (tile, rank), 0)
    for side in range(2):
        acc = jnp.zeros((tile, docs * rank), jnp.float32)
        for at, parts in enumerate(pieces):
            slabs = []
            for doc in range(docs):
                start = pl.multiple_of(slots_ref[side, doc] * rank, rank)
                slabs.append(
                    jnp.concatenate([down_refs[i][pl.ds(start, rank), :] for i in parts], 1)
                )
            acc += lax.dot_general(
                token_refs[side][:, at * shard : (at + 1) * shard],
                jnp.concatenate(slabs, 0),
                nt,
                preferred_element_type=jnp.float32,
            )
        mid = jnp.zeros((tile, rank), jnp.float32)
        for doc in range(docs):
            low = 0 if doc == 0 else ends_ref[side, doc - 1]
            inside = (row >= low) & (row < ends_ref[side, doc])
            mid = jnp.where(inside, acc[:, doc * rank : (doc + 1) * rank], mid)
        out_refs[side][...] = mid


def mid_partials(own, other, pieces, ends, slots, rank):
    rows = own.shape[0]
    tile = 256 if rows % 256 == 0 else rows
    arrays, places = [], []
    for parts in pieces:
        places.append(tuple(range(len(arrays), len(arrays) + len(parts))))
        arrays += parts
    docs = slots.shape[1]
    out = jax.ShapeDtypeStruct((rows, rank), jnp.float32)
    return pl.pallas_call(
        functools.partial(mid_kernel, docs, rank, tuple(places)),
        out_shape=(out, out),
        grid_spec=pltpu.PrefetchScalarGridSpec(
            num_scalar_prefetch=2,
            grid=(rows // tile,),
            in_specs=[tiled(own, tile), tiled(other, tile)] + [fixed(a) for a in arrays],
            out_specs=[pl.BlockSpec((tile, rank), lambda i, *_: (i, 0))] * 2,
        ),
        compiler_params=pltpu.CompilerParams(vmem_limit_bytes=32 << 20),
        cost_estimate=pl.CostEstimate(
            flops=4 * rows * own.shape[1] * docs * rank,
            bytes_accessed=4 * own.size + sum(2 * a.size for a in arrays),
            transcendentals=0,
        ),
    )(ends, slots, own, other, *arrays)


def shard_rows(refs, parts, cols):
    return jnp.concatenate([refs[i][a:b, cols] for i, a, b in parts], 0)


def part_kernel(pieces, columns, *refs):
    token_refs, value_refs, out_refs = refs[:2], refs[2:-2], refs[-2:]
    for n in range(0, out_refs[0].shape[1], columns):
        cols = slice(n, n + columns)
        acc = [None, None]
        for at, parts in pieces:
            rhs = shard_rows(value_refs, parts, cols)
            for side in range(2):
                term = jnp.dot(
                    token_refs[side][:, at : at + rhs.shape[0]],
                    rhs,
                    preferred_element_type=jnp.float32,
                )
                acc[side] = term if acc[side] is None else acc[side] + term
        for side in range(2):
            out_refs[side][:, cols] = acc[side]


def value_partials(own, other, arrays, pieces, width):
    rows = own.shape[0]
    tile = 256 if rows % 256 == 0 else rows
    out = jax.ShapeDtypeStruct((rows, width), jnp.float32)
    depth = sum(b - a for _, parts in pieces for _, a, b in parts)
    return pl.pallas_call(
        functools.partial(part_kernel, pieces, 256),
        out_shape=(out, out),
        grid=(rows // tile,),
        in_specs=[tiled(own, tile), tiled(other, tile)] + [fixed(a) for a in arrays],
        out_specs=[tiled(out, tile)] * 2,
        compiler_params=pltpu.CompilerParams(vmem_limit_bytes=40 << 20),
        cost_estimate=pl.CostEstimate(
            flops=4 * rows * depth * width,
            bytes_accessed=4 * own.size + 8 * out.size + sum(2 * a.size for a in arrays),
            transcendentals=0,
        ),
    )(own, other, *arrays)


def last_kernel(pieces, columns, spans, slots_ref, ends_ref, *refs):
    token_refs, sum_refs, mid_refs, up_ref = refs[:2], refs[2:4], refs[4:6], refs[6]
    value_refs, out_ref = refs[7:-1], refs[-1]
    docs = slots_ref.shape[0]
    tile, rank = mid_refs[0].shape
    row = pl.program_id(0) * tile + lax.broadcasted_iota(jnp.int32, (tile, rank), 0)
    mid = (mid_refs[0][...] + mid_refs[1][...]).astype(jnp.bfloat16)
    nothing = jnp.zeros_like(mid)
    spread = []
    for doc in range(docs):
        low = 0 if doc == 0 else ends_ref[doc - 1]
        spread.append(jnp.where((row >= low) & (row < ends_ref[doc]), mid, nothing))
    spread = jnp.concatenate(spread, 1)
    for n in range(0, out_ref.shape[1], columns):
        cols = slice(n, n + columns)
        up = [
            up_ref[pl.ds(pl.multiple_of(slots_ref[doc] * rank, rank), rank), cols]
            for doc in range(docs)
        ]
        acc = adapter_scale * jnp.dot(
            spread, jnp.concatenate(up, 0), preferred_element_type=jnp.float32
        )
        acc += sum_refs[0][:, cols] + sum_refs[1][:, cols]
        for side, at, parts in pieces:
            rhs = shard_rows(value_refs, parts, cols)
            acc += jnp.dot(
                token_refs[side][:, at - spans[side] : at - spans[side] + rhs.shape[0]],
                rhs,
                preferred_element_type=jnp.float32,
            )
        out_ref[:, cols] = acc.astype(out_ref.dtype)


def last_values(own, other, sums, mids, up, slots, ends, arrays, pieces):
    rows, width = sums[0].shape
    tile = 256 if rows % 256 == 0 else rows
    depth = sum(b - a for _, _, parts in pieces for _, a, b in parts)
    return pl.pallas_call(
        functools.partial(last_kernel, pieces, 256, (0, 0)),
        out_shape=jax.ShapeDtypeStruct((rows, width), jnp.bfloat16),
        grid_spec=pltpu.PrefetchScalarGridSpec(
            num_scalar_prefetch=2,
            grid=(rows // tile,),
            in_specs=[tiled(a, tile) for a in (own, other, *sums, *mids)]
            + [fixed(a) for a in (up, *arrays)],
            out_specs=pl.BlockSpec((tile, width), lambda i, *_: (i, 0)),
        ),
        compiler_params=pltpu.CompilerParams(vmem_limit_bytes=40 << 20),
        cost_estimate=pl.CostEstimate(
            flops=2 * rows * depth * width,
            bytes_accessed=4 * own.size + 10 * rows * width + sum(2 * a.size for a in arrays),
            transcendentals=0,
        ),
    )(slots, ends, own, other, *sums, *mids, up, *arrays)


def after(value, *earlier):
    return lax.optimization_barrier((value, *earlier))[0]


def make(groups, store):
    depth = store // (rows_y * cores)

    def index(z, y, c):
        return (z * rows_y + y) * cores + c

    def pairs(move):
        return [
            (index(z, y, c), index(*move(z, y, c)))
            for z in range(depth)
            for y in range(rows_y)
            for c in range(cores)
        ]

    def along_z(value, k):
        return lax.ppermute(value, "store", pairs(lambda z, y, c: ((z + k) % depth, y, c)))

    def along_y(value):
        return lax.ppermute(value, "store", pairs(lambda z, y, c: (z, 1 - y, c)))

    def across(value):
        return lax.ppermute(value, "store", pairs(lambda z, y, c: (z, y, 1 - c)))

    def along_x(value):
        return lax.ppermute(value, "groups", [(g, g ^ 1) for g in range(groups)])

    class Line:
        def __init__(self, send):
            self.send, self.sent = send, []

        def __call__(self, value, *args):
            if len(self.sent) >= 2:
                value = after(value, self.sent[-2])
            self.sent.append(self.send(value, *args))
            return self.sent[-1]

    def per_device(
        tokens,
        input_norm_gain,
        value_matrix,
        adapter_down_factors,
        adapter_up_factors,
        document_lengths,
        document_tenant,
        tenant_adapter_slot,
    ):
        shard, adapters, rank = adapter_down_factors.shape
        flat = adapters * rank
        width = value_matrix.shape[1]
        quarter, half = shard // 4, shard // 2
        me = lax.axis_index("store")
        side = lax.axis_index("groups") % 2
        mz, my, mc = me // (rows_y * cores), (me // cores) % rows_y, me % cores

        down = adapter_down_factors.reshape(shard, flat).T
        take = lax.dynamic_slice_in_dim
        d_have = {(0, 0): take(down, side * half, half, 1)}
        d_miss = {(0, 0): take(down, half - side * half, half, 1)}
        v_have = {
            (0, 0): jnp.concatenate(
                [
                    take(value_matrix, side * half, half, 0),
                    take(value_matrix, 3 * quarter - side * half, quarter, 0),
                ],
                0,
            )
        }
        v_miss = {(0, 0): (take(value_matrix, half - side * half, quarter, 0), 0)}
        up = adapter_up_factors.reshape(flat, -1).T
        up_all = lax.all_gather(up, "store", axis=0, tiled=True).T

        source = []
        for lane_at in (mc, 1 - mc):
            for dy in range(rows_y):
                for k in range(depth):
                    s = index((mz - k) % depth, my ^ dy, lane_at)
                    for c in range(shard // lane):
                        piece = c * lane + jnp.where(c * lane < half, 1, -1) * side * half
                        source.append(s * shard + piece)
        ks = []
        for k in range(1, depth // 2 + 1):
            ks += [k, depth - k] if k != depth - k else [k]
        last = ks[-1]
        z, y, x = Line(along_z), Line(along_y), Line(along_x)

        def x_values(names):
            got = x(jnp.concatenate([v_have[name][:quarter] for name in names], 0))
            for i, name in enumerate(names):
                v_miss[name] = (got, i * quarter)

        d_have[1, 0] = y(d_have[0, 0])
        for k in ks:
            d_have[0, k] = z(d_have[0, 0], k)
        v_have[1, 0] = y(v_have[0, 0])
        for k in ks:
            v_have[0, k] = z(v_have[0, 0], k)
        d_miss[1, 0] = x(d_have[1, 0])
        own, other = norm_in_order(
            after(tokens, d_have[1, 0]), input_norm_gain, jnp.stack(source).astype(jnp.int32))
        for k in ks:
            d_have[1, k] = y(d_have[0, k])
        for k in ks:
            d_miss[0, k] = x(d_have[0, k])
            d_miss[1, k] = x(d_have[1, k])
        for k in ks:
            v_have[1, k] = y(v_have[0, k])
        early = [k for k in ks if k != last]
        x_values([(1, 0)] + [(0, k) for k in early])
        x_values([(1, k) for k in early])
        x_values([(0, last)])
        x_values([(1, last)])

        partner = across(other)

        ends = jnp.cumsum(document_lengths, axis=1).astype(jnp.int32)
        slots = jnp.sum(
            (document_tenant[0][:, None] == jnp.arange(adapters, dtype=jnp.int32)[None, :])
            * tenant_adapter_slot[None, :],
            axis=1,
        ).astype(jnp.int32)[None, :]
        near = jnp.concatenate([ends, slots], 0)
        far = across(near)
        ends_both = jnp.concatenate([ends, far[:1]], 0)
        slots_both = jnp.concatenate([slots, far[1:]], 0)

        names = [(dy, k) for dy in range(rows_y) for k in range(depth)]
        mid_own, mid_far = mid_partials(
            after(own, up_all), partner, [[d_have[n], d_miss[n]] for n in names], ends_both, slots_both, rank
        )
        mids = (mid_own, across(mid_far))

        def lay(names, have, miss):
            arrays, pieces = [], []

            def place(array):
                for i, known in enumerate(arrays):
                    if known is array:
                        return i
                arrays.append(array)
                return len(arrays) - 1

            for name in names:
                h = place(have[name])
                m, row = miss[name]
                m = place(m)
                pieces.append(
                    (
                        (name[0] * depth + name[1]) * shard,
                        ((h, 0, half), (m, row, row + quarter), (h, half, half + quarter)),
                    )
                )
            return arrays, pieces

        arrays, pieces = lay([n for n in names if n[1] != last], v_have, v_miss)
        arrays[0] = after(arrays[0], v_have[0, last])
        sum_own, sum_far = value_partials(own, partner, arrays, tuple(pieces), width)
        sums = (sum_own, across(sum_far))

        final = [(dy, last) for dy in range(rows_y)]
        arrays, pieces = lay(final, v_have, v_miss)
        far_have = {n: across(v_have[n]) for n in final}
        far_miss = {n: (across(v_miss[n][0]), v_miss[n][1]) for n in final}
        far_arrays, far_pieces = lay(final, far_have, far_miss)
        pieces = [(0, at, parts) for at, parts in pieces] + [
            (1, at, tuple((i + len(arrays), a, b) for i, a, b in parts))
            for at, parts in far_pieces
        ]
        return last_values(
            own, other, sums, mids, up_all, slots[0], ends[0], arrays + far_arrays, tuple(pieces)
        )

    return per_device


def solution(mesh):
    in_specs = (
        P(("groups", "store"), None),
        P(),
        P("store", None),
        P("store", None, None),
        P(None, None, "store"),
        P(("groups", "store"), None),
        P(("groups", "store"), None),
        P(),
    )
    out_specs = P(("groups", "store"), None)
    groups, store = mesh.shape["groups"], mesh.shape["store"]

    def run(*args):
        shard = args[2].shape[0]
        cut = shard % (4 * lane) == 0 and store % (rows_y * cores) == 0 and groups % 2 == 0
        return (make(groups, store) if cut else plain)(*args)

    return jax.shard_map(
        run, mesh=mesh, in_specs=in_specs, out_specs=out_specs, check_vma=False
    )
```

```python
import functools

import jax
import jax.numpy as jnp
from jax import lax
from jax.experimental import pallas as pl
from jax.experimental.pallas import tpu as pltpu
from jax.sharding import PartitionSpec as P

adapter_scale = 2.0
cores, rows_y, lane = 2, 2, 128
nt = (((1,), (1,)), ((), ()))
vmem = 58 << 20


def token_slots(lengths, tenants, tenant_adapter_slot, row_count):
    ends = jnp.cumsum(lengths)
    position = jnp.arange(row_count, dtype=jnp.int32)
    doc_index = jnp.sum((position[:, None] >= ends[None, :]).astype(jnp.int32), axis=1)
    doc_pick = (
        doc_index[:, None] == jnp.arange(lengths.shape[0], dtype=jnp.int32)[None, :]
    ).astype(jnp.int32)
    tenant = jnp.sum(doc_pick * tenants[None, :], axis=1)
    tenant_pick = (
        tenant[:, None] == jnp.arange(tenant_adapter_slot.shape[0], dtype=jnp.int32)[None, :]
    ).astype(jnp.int32)
    return jnp.sum(tenant_pick * tenant_adapter_slot[None, :], axis=1)


def pick_rank(rank_total_rows, slots, count_of_adapters, rank_span_width):
    select = (slots[:, None] == jnp.arange(count_of_adapters, dtype=jnp.int32)[None, :]).astype(
        jnp.float32
    )
    shaped = rank_total_rows.reshape(slots.shape[0], count_of_adapters, rank_span_width)
    return jnp.sum(shaped * select[:, :, None], axis=1)


def plain(
    tokens,
    input_norm_gain,
    value_matrix,
    adapter_down_factors,
    adapter_up_factors,
    document_lengths,
    document_tenant,
    tenant_adapter_slot,
):
    row_count = tokens.shape[0]
    count_of_adapters = adapter_down_factors.shape[1]
    rank_span_width = adapter_down_factors.shape[2]
    flat_width = count_of_adapters * rank_span_width
    wide = tokens.astype(jnp.float32)
    meansq = jnp.mean(wide * wide, axis=1, keepdims=True)
    normed = (wide * lax.rsqrt(meansq + 1e-05) * input_norm_gain.astype(jnp.float32)).astype(
        jnp.bfloat16
    )
    slots = token_slots(document_lengths[0], document_tenant[0], tenant_adapter_slot, row_count)
    base_output = jnp.dot(
        normed,
        lax.all_gather(value_matrix, "store", axis=0, tiled=True),
        preferred_element_type=jnp.float32,
    )
    down = lax.all_gather(adapter_down_factors, "store", axis=0, tiled=True)
    rank_total_rows = jnp.dot(
        normed, down.reshape(down.shape[0], flat_width), preferred_element_type=jnp.float32
    )
    mid = pick_rank(rank_total_rows, slots, count_of_adapters, rank_span_width)
    mid = mid.astype(jnp.bfloat16)
    select = (slots[:, None] == jnp.arange(count_of_adapters, dtype=jnp.int32)[None, :]).astype(
        jnp.bfloat16
    )
    expanded_rows = (mid[:, None, :] * select[:, :, None]).reshape(row_count, flat_width)
    up = lax.all_gather(adapter_up_factors, "store", axis=2, tiled=True)
    adapter_update = jnp.dot(
        expanded_rows, up.reshape(flat_width, up.shape[2]), preferred_element_type=jnp.float32
    )
    return (base_output + adapter_scale * adapter_update).astype(jnp.bfloat16)


def norm_kernel(source_ref, tokens_ref, gain_ref, *out_refs):
    width = tokens_ref.shape[1]
    total = jnp.zeros((tokens_ref.shape[0], lane), jnp.float32)
    for i in range(width // lane):
        part = tokens_ref[:, i * lane : (i + 1) * lane].astype(jnp.float32)
        total += part * part
    scale = lax.rsqrt(jnp.sum(total, axis=1, keepdims=True) / width + 1e-05)
    first = 0
    for out_ref in out_refs:
        for i in range(out_ref.shape[1] // lane):
            start = pl.multiple_of(source_ref[first + i], lane)
            part = tokens_ref[:, pl.ds(start, lane)].astype(jnp.float32)
            gain = gain_ref[:, pl.ds(start, lane)].astype(jnp.float32)
            out_ref[:, i * lane : (i + 1) * lane] = (part * scale * gain).astype(jnp.bfloat16)
        first += out_ref.shape[1] // lane


def norm_in_order(tokens, gain, source, widths):
    rows, width = tokens.shape
    block = 64
    return pl.pallas_call(
        norm_kernel,
        out_shape=[jax.ShapeDtypeStruct((rows, w), jnp.bfloat16) for w in widths],
        grid_spec=pltpu.PrefetchScalarGridSpec(
            num_scalar_prefetch=1,
            grid=(rows // block,),
            in_specs=[
                pl.BlockSpec((block, width), lambda i, *_: (i, 0)),
                pl.BlockSpec((1, width), lambda i, *_: (0, 0)),
            ],
            out_specs=[pl.BlockSpec((block, w), lambda i, *_: (i, 0)) for w in widths],
        ),
        compiler_params=pltpu.CompilerParams(vmem_limit_bytes=vmem),
        cost_estimate=pl.CostEstimate(
            flops=6 * rows * width, bytes_accessed=4 * rows * width, transcendentals=rows
        ),
    )(source, tokens, gain.reshape(1, width))


def far_memory():
    return pl.BlockSpec(memory_space=pltpu.HBM)


def held(arrays):
    return [pltpu.VMEM(a.shape, a.dtype) for a in arrays] + [
        pltpu.SemaphoreType.DMA((len(arrays),))
    ]


def load(array_refs, held_refs):
    *held_refs, sem = held_refs
    copies = [
        pltpu.make_async_copy(a, h, sem.at[i])
        for i, (a, h) in enumerate(zip(array_refs, held_refs))
    ]

    @pl.when(pl.program_id(0) == 0)
    def _():
        for copy in copies:
            copy.start()
        for copy in copies:
            copy.wait()

    return held_refs


def tiled(array, tile, block=None):
    if block is None:
        return pl.BlockSpec((tile,) + array.shape[1:], lambda i, *_: (i, 0))
    at, width = block
    return pl.BlockSpec((tile, width), lambda i, *_: (i, at))


def pick_kernel(rank, slots_ref, *refs):
    piece_refs, out_ref, sem = refs[:-2], refs[-2], refs[-1]
    count = slots_ref.shape[0] * slots_ref.shape[1]
    docs = slots_ref.shape[1]
    copies = []
    for j, piece in enumerate(piece_refs):
        for i in range(count):
            start = pl.multiple_of(slots_ref[i // docs, i % docs] * rank, rank)
            copies.append(
                pltpu.make_async_copy(
                    piece.at[pl.ds(start, rank), :],
                    out_ref.at[pl.ds((j * count + i) * rank, rank), :],
                    sem.at[j * count + i],
                )
            )
    for copy in copies:
        copy.start()
    for copy in copies:
        copy.wait()


def pick_adapters(pieces, slots, rank):
    count = slots.shape[0] * slots.shape[1] * len(pieces)
    columns = pieces[0].shape[1]
    return pl.pallas_call(
        functools.partial(pick_kernel, rank),
        out_shape=jax.ShapeDtypeStruct((count * rank, columns), jnp.bfloat16),
        grid_spec=pltpu.PrefetchScalarGridSpec(
            num_scalar_prefetch=1,
            in_specs=[far_memory()] * len(pieces),
            out_specs=far_memory(),
            scratch_shapes=[pltpu.SemaphoreType.DMA((count,))],
        ),
        compiler_params=pltpu.CompilerParams(vmem_limit_bytes=vmem),
        cost_estimate=pl.CostEstimate(
            flops=0, bytes_accessed=4 * count * rank * columns, transcendentals=0
        ),
    )(slots, *pieces)


def slab(rank, slot, have, miss, at):
    start = pl.multiple_of(slot * rank, rank)
    miss_ref, first = miss
    at = first + at * rank
    return jnp.concatenate([have[pl.ds(start, rank), :], miss_ref[at : at + rank, :]], 1)


def by_document(acc, ends, tile, rank):
    row = pl.program_id(0) * tile + lax.broadcasted_iota(jnp.int32, (tile, rank), 0)
    mid = jnp.zeros((tile, rank), jnp.float32)
    low = 0
    for doc, end in enumerate(ends):
        mid = jnp.where((row >= low) & (row < end), acc[:, doc * rank : (doc + 1) * rank], mid)
        low = end
    return mid


def mid_kernel(rank, plan, blocks, arrays, ends_ref, slots_ref, *refs):
    block_refs, array_refs = refs[:blocks], refs[blocks : blocks + arrays]
    out_refs = refs[blocks + arrays : blocks + arrays + 2]
    refs = list(block_refs) + load(array_refs, refs[blocks + arrays + 2 :])
    docs = slots_ref.shape[1]
    tile = out_refs[0].shape[0]
    for side in range(2):
        acc = None
        for block, column, have, rest, row in plan[side]:
            rhs = jnp.concatenate(
                [
                    slab(rank, slots_ref[side, d], refs[have], (refs[rest], row), side * docs + d)
                    for d in range(docs)
                ],
                0,
            )
            term = lax.dot_general(
                refs[block][:, column : column + rhs.shape[1]],
                rhs,
                nt,
                preferred_element_type=jnp.float32,
            )
            acc = term if acc is None else acc + term
        ends = [ends_ref[side, d] for d in range(docs)]
        out_refs[side][...] = by_document(acc, ends, tile, rank)


def mid_partials(blocks, arrays, plan, ends, slots, rank):
    rows = blocks[0].shape[0]
    tile = 256 if rows % 256 == 0 else rows
    out = jax.ShapeDtypeStruct((rows, rank), jnp.float32)
    return pl.pallas_call(
        functools.partial(mid_kernel, rank, plan, len(blocks), len(arrays)),
        out_shape=(out, out),
        grid_spec=pltpu.PrefetchScalarGridSpec(
            num_scalar_prefetch=2,
            grid=(rows // tile,),
            in_specs=[tiled(b, tile) for b in blocks] + [far_memory()] * len(arrays),
            out_specs=[pl.BlockSpec((tile, rank), lambda i, *_: (i, 0))] * 2,
            scratch_shapes=held(arrays),
        ),
        compiler_params=pltpu.CompilerParams(vmem_limit_bytes=vmem),
        cost_estimate=pl.CostEstimate(
            flops=2 * sum(b.size for b in blocks) * slots.shape[1] * rank,
            bytes_accessed=2 * sum(a.size for a in (*blocks, *arrays)),
            transcendentals=0,
        ),
    )(ends, slots, *blocks, *arrays)


def value_kernel(plan, columns, blocks, arrays, has_sum, *refs):
    block_refs, sum_refs = refs[:blocks], refs[blocks : blocks + has_sum]
    refs = refs[blocks + has_sum :]
    array_refs, out_ref = refs[:arrays], refs[arrays]
    refs = list(block_refs) + load(array_refs, refs[arrays + 1 :])
    for n in range(0, out_ref.shape[1], columns):
        cols = slice(n, n + columns)
        acc = sum_refs[0][:, cols] if has_sum else None
        for block, at, parts in plan:
            rhs = jnp.concatenate([refs[i][a:b, cols] for i, a, b in parts], 0)
            term = jnp.dot(
                refs[block][:, at : at + rhs.shape[0]], rhs, preferred_element_type=jnp.float32
            )
            acc = term if acc is None else acc + term
        out_ref[:, cols] = acc


def value_sums(blocks, arrays, plan, width, start=None):
    rows = blocks[0].shape[0]
    tile = 256 if rows % 256 == 0 else rows
    out = jax.ShapeDtypeStruct((rows, width), jnp.float32)
    extra = [] if start is None else [start]
    size = sum(b.size for b in blocks)
    return pl.pallas_call(
        functools.partial(value_kernel, plan, 256, len(blocks), len(arrays), len(extra)),
        out_shape=out,
        grid=(rows // tile,),
        in_specs=[tiled(b, tile) for b in (*blocks, *extra)] + [far_memory()] * len(arrays),
        out_specs=tiled(out, tile),
        scratch_shapes=held(arrays),
        compiler_params=pltpu.CompilerParams(vmem_limit_bytes=vmem),
        cost_estimate=pl.CostEstimate(
            flops=2 * size * width,
            bytes_accessed=2 * size + 4 * out.size + sum(2 * a.size for a in arrays),
            transcendentals=0,
        ),
    )(*blocks, *extra, *arrays)


def last_kernel(rank, plan, blocks, arrays, slots_ref, ends_ref, *refs):
    sum_ref, mid_refs, refs = refs[0], refs[1:3], refs[3:]
    block_refs, array_refs, out_ref = refs[:blocks], refs[blocks:-arrays - 2], refs[-arrays - 2]
    *refs, up_ref = load(array_refs, refs[-arrays - 1 :])
    refs = list(block_refs) + refs
    docs = slots_ref.shape[0]
    tile = out_ref.shape[0]
    acc = None
    for block, have, rest, row, first in plan:
        rhs = jnp.concatenate(
            [
                slab(rank, slots_ref[d], refs[have], (refs[rest], row), first + d)
                for d in range(docs)
            ],
            0,
        )
        term = lax.dot_general(refs[block][...], rhs, nt, preferred_element_type=jnp.float32)
        acc = term if acc is None else acc + term
    ends = [ends_ref[d] for d in range(docs)]
    mid = by_document(acc, ends, tile, rank) + mid_refs[0][...] + mid_refs[1][...]
    row = pl.program_id(0) * tile + lax.broadcasted_iota(jnp.int32, (tile, rank), 0)
    spread, low = [], 0
    for end in ends:
        spread.append(jnp.where((row >= low) & (row < end), mid, 0.0).astype(jnp.bfloat16))
        low = end
    spread = jnp.concatenate(spread, 1)
    columns = 256
    for n in range(0, out_ref.shape[1], columns):
        cols = slice(n, n + columns)
        up = [
            up_ref[pl.ds(pl.multiple_of(slots_ref[d] * rank, rank), rank), cols]
            for d in range(docs)
        ]
        delta = jnp.dot(spread, jnp.concatenate(up, 0), preferred_element_type=jnp.float32)
        out_ref[:, cols] = (sum_ref[:, cols] + adapter_scale * delta).astype(out_ref.dtype)


def last_values(base, mids, up, blocks, arrays, plan, slots, ends):
    rows, width = base.shape
    rank = mids[0].shape[1]
    tile = 256 if rows % 256 == 0 else rows
    return pl.pallas_call(
        functools.partial(last_kernel, rank, plan, len(blocks), len(arrays) + 1),
        out_shape=jax.ShapeDtypeStruct((rows, width), jnp.bfloat16),
        grid_spec=pltpu.PrefetchScalarGridSpec(
            num_scalar_prefetch=2,
            grid=(rows // tile,),
            in_specs=[tiled(a, tile) for a in (base, *mids)]
            + [tiled(b, tile, (at, w)) for b, at, w in blocks]
            + [far_memory()] * (len(arrays) + 1),
            out_specs=pl.BlockSpec((tile, width), lambda i, *_: (i, 0)),
            scratch_shapes=held([*arrays, up]),
        ),
        compiler_params=pltpu.CompilerParams(vmem_limit_bytes=vmem),
        cost_estimate=pl.CostEstimate(
            flops=2 * rows * width * 256,
            bytes_accessed=8 * rows * width + sum(2 * a.size for a in arrays),
            transcendentals=0,
        ),
    )(slots, ends, base, *mids, *[b for b, _, _ in blocks], *arrays, up)


def after(value, *earlier):
    return lax.optimization_barrier((value, *earlier))[0]


def make(groups, store):
    depth = store // (rows_y * cores)

    def index(z, y, c):
        return (z * rows_y + y) * cores + c

    def pairs(move):
        return [
            (index(z, y, c), index(*move(z, y, c)))
            for z in range(depth)
            for y in range(rows_y)
            for c in range(cores)
        ]

    def along_z(value, k):
        return lax.ppermute(value, "store", pairs(lambda z, y, c: ((z + k) % depth, y, c)))

    def along_y(value):
        return lax.ppermute(value, "store", pairs(lambda z, y, c: (z, 1 - y, c)))

    def across(value):
        return lax.ppermute(value, "store", pairs(lambda z, y, c: (z, y, 1 - c)))

    def along_x(value):
        return lax.ppermute(value, "groups", [(g, g ^ 1) for g in range(groups)])

    class Line:
        def __init__(self, send):
            self.send, self.sent = send, []

        def __call__(self, value, *args):
            if len(self.sent) >= 2:
                value = after(value, self.sent[-2])
            self.sent.append(self.send(value, *args))
            return self.sent[-1]

    def per_device(
        tokens,
        input_norm_gain,
        value_matrix,
        adapter_down_factors,
        adapter_up_factors,
        document_lengths,
        document_tenant,
        tenant_adapter_slot,
    ):
        shard, adapters, rank = adapter_down_factors.shape
        flat = adapters * rank
        width = value_matrix.shape[1]
        half, part = shard // 2, 3 * shard // 8
        me = lax.axis_index("store")
        side = lax.axis_index("groups") % 2
        mz, my, mc = me // (rows_y * cores), (me // cores) % rows_y, me % cores
        take = lax.dynamic_slice_in_dim

        down = adapter_down_factors.reshape(shard, flat).T
        v_have = {
            (0, 0): jnp.concatenate(
                [
                    take(value_matrix, side * half, half, 0),
                    take(value_matrix, half + part - side * half, half - part, 0),
                ],
                0,
            )
        }
        v_miss = {(0, 0): (take(value_matrix, half - side * half, part, 0), 0)}
        d_have = {(0, 0): take(down, side * half, half, 1)}
        d_rest = take(down, half - side * half, half, 1)
        up = adapter_up_factors.reshape(flat, -1).T
        up_all = lax.all_gather(up, "store", axis=0, tiled=True).T

        ends = jnp.cumsum(document_lengths, axis=1).astype(jnp.int32)
        slots = jnp.sum(
            (document_tenant[0][:, None] == jnp.arange(adapters, dtype=jnp.int32)[None, :])
            * tenant_adapter_slot[None, :],
            axis=1,
        ).astype(jnp.int32)[None, :]
        near = jnp.concatenate([ends, slots], 0)
        far = across(near)
        ends_both = jnp.concatenate([ends, far[:1]], 0)
        slots_both = jnp.concatenate([slots, far[1:]], 0)
        slots_there = along_x(slots_both)
        d_miss = {(0, 0): (pick_adapters([d_rest], slots_both, rank), 0)}
        chosen = slots_both.size * rank

        ks = []
        for k in range(1, depth // 2 + 1):
            ks += [k, depth - k] if k != depth - k else [k]
        last = ks[-1]
        early = [k for k in ks if k != last]
        z, y, x = Line(along_z), Line(along_y), Line(along_x)

        def x_values(names, *earlier):
            got = x(after(jnp.concatenate([v_have[name][:part] for name in names], 0), *earlier))
            for i, name in enumerate(names):
                v_miss[name] = (got, i * part)

        def x_down(names):
            got = x(pick_adapters([d_have[name] for name in names], slots_there, rank))
            for i, name in enumerate(names):
                d_miss[name] = (got, i * chosen)

        for k in ks:
            v_have[0, k] = z(v_have[0, 0], k)
        for k in ks:
            d_have[0, k] = z(d_have[0, 0], k)
        v_have[1, 0] = y(v_have[0, 0])
        d_have[1, 0] = y(d_have[0, 0])
        x_values([(1, 0)])
        for k in early:
            v_have[1, k] = y(v_have[0, k])
        x_values([(0, k) for k in early])
        x_values([(1, k) for k in early])
        v_have[1, last] = y(v_have[0, last])
        x_values([(0, last)])
        x_values([(1, last)], *[d_have[0, k] for k in early])
        x_down([(1, 0)])
        for k in early:
            d_have[1, k] = y(d_have[0, k])
        x_down([(0, k) for k in early])
        x_down([(1, k) for k in early])
        d_have[1, last] = y(d_have[0, last])
        x_down([(0, last)])
        x_down([(1, last)])

        source = []
        for lane_at in (mc, 1 - mc):
            for dy in range(rows_y):
                for k in range(depth):
                    s = index((mz - k) % depth, my ^ dy, lane_at)
                    for c in range(shard // lane):
                        piece = c * lane + jnp.where(c * lane < half, 1, -1) * side * half
                        source.append(s * shard + piece)
        span = rows_y * depth * shard
        chunk = span // 4
        ready = [v_have[0, k] for k in early] + [v_miss[1, 0][0], d_miss[1, 0][0], up_all]
        own, *other = norm_in_order(
            after(tokens, *ready),
            input_norm_gain,
            jnp.stack(source).astype(jnp.int32),
            [span] + [chunk] * 4,
        )
        partner = [across(o) for o in other]

        names = [(dy, k) for dy in range(rows_y) for k in range(depth)]

        def column(name):
            return (name[0] * depth + name[1]) * shard

        def lay(blocks):
            arrays = []

            def place(array):
                for i, known in enumerate(arrays):
                    if known is array:
                        return blocks + i
                arrays.append(array)
                return blocks + len(arrays) - 1

            return arrays, place

        def values(blocks, start=None):
            arrays, place = lay(len(blocks))
            width_of = blocks[0].shape[1]
            plan = []
            for name in names:
                h = place(v_have[name])
                m, row = v_miss[name]
                m = place(m)
                parts = ((h, 0, half), (m, row, row + part), (h, half, shard - part))
                plan.append((column(name) // width_of, column(name) % width_of, parts))
            return value_sums(blocks, arrays, tuple(plan), width, start)

        ready = [d_have[1, k] for k in early] + [d_have[0, last]]
        partner[0] = after(partner[0], *ready)
        base = values([own], across(values(partner)))

        arrays, place = lay(5)
        plan = ([], [])
        for name in names:
            if name[1] != last:
                miss, row = d_miss[name]
                entry = (place(d_have[name]), place(miss), row)
                at = column(name)
                plan[0].append((0, at, *entry))
                plan[1].append((1 + at // chunk, at % chunk, *entry))
        mid_own, mid_far = mid_partials(
            [own, *partner], arrays, tuple(map(tuple, plan)), ends_both, slots_both, rank
        )
        mids = (mid_own, across(mid_far))

        final = [(dy, last) for dy in range(rows_y)]
        blocks, pieces = [], []
        for name in final:
            blocks.append((own, column(name) // shard, shard))
            pieces.append((d_have[name], *d_miss[name], 0))
        for name in final:
            at = column(name)
            blocks.append((other[at // chunk], at % chunk // shard, shard))
            miss, row = d_miss[name]
            pieces.append((across(d_have[name]), across(miss), row, slots.shape[1]))
        arrays, place = lay(len(blocks))
        plan = [
            (i, place(have), place(miss), row, first)
            for i, (have, miss, row, first) in enumerate(pieces)
        ]
        return last_values(base, mids, up_all, blocks, arrays, tuple(plan), slots[0], ends[0])

    return per_device


def solution(mesh):
    in_specs = (
        P(("groups", "store"), None),
        P(),
        P("store", None),
        P("store", None, None),
        P(None, None, "store"),
        P(("groups", "store"), None),
        P(("groups", "store"), None),
        P(),
    )
    out_specs = P(("groups", "store"), None)
    groups, store = mesh.shape["groups"], mesh.shape["store"]

    def run(*args):
        shard = args[2].shape[0]
        cut = shard % (4 * lane) == 0 and store > 4 and store % (rows_y * cores) == 0 and groups % 2 == 0
        return (make(groups, store) if cut else plain)(*args)

    return jax.shard_map(
        run, mesh=mesh, in_specs=in_specs, out_specs=out_specs, check_vma=False
    )
```

```python
import functools

import jax
import jax.numpy as jnp
from jax import lax
from jax.experimental import pallas as pl
from jax.experimental.pallas import tpu as pltpu
from jax.sharding import PartitionSpec as P

adapter_scale = 2.0
cores, rows_y, lane = 2, 2, 128
nt = (((1,), (1,)), ((), ()))
vmem = 58 << 20
light = pl.CostEstimate(flops=0, bytes_accessed=0, transcendentals=0)


def token_slots(lengths, tenants, tenant_adapter_slot, row_count):
    ends = jnp.cumsum(lengths)
    position = jnp.arange(row_count, dtype=jnp.int32)
    doc_index = jnp.sum((position[:, None] >= ends[None, :]).astype(jnp.int32), axis=1)
    doc_pick = (
        doc_index[:, None] == jnp.arange(lengths.shape[0], dtype=jnp.int32)[None, :]
    ).astype(jnp.int32)
    tenant = jnp.sum(doc_pick * tenants[None, :], axis=1)
    tenant_pick = (
        tenant[:, None] == jnp.arange(tenant_adapter_slot.shape[0], dtype=jnp.int32)[None, :]
    ).astype(jnp.int32)
    return jnp.sum(tenant_pick * tenant_adapter_slot[None, :], axis=1)


def pick_rank(rank_total_rows, slots, count_of_adapters, rank_span_width):
    select = (slots[:, None] == jnp.arange(count_of_adapters, dtype=jnp.int32)[None, :]).astype(
        jnp.float32
    )
    shaped = rank_total_rows.reshape(slots.shape[0], count_of_adapters, rank_span_width)
    return jnp.sum(shaped * select[:, :, None], axis=1)


def plain(
    tokens,
    input_norm_gain,
    value_matrix,
    adapter_down_factors,
    adapter_up_factors,
    document_lengths,
    document_tenant,
    tenant_adapter_slot,
):
    row_count = tokens.shape[0]
    count_of_adapters = adapter_down_factors.shape[1]
    rank_span_width = adapter_down_factors.shape[2]
    flat_width = count_of_adapters * rank_span_width
    wide = tokens.astype(jnp.float32)
    meansq = jnp.mean(wide * wide, axis=1, keepdims=True)
    normed = (wide * lax.rsqrt(meansq + 1e-05) * input_norm_gain.astype(jnp.float32)).astype(
        jnp.bfloat16
    )
    slots = token_slots(document_lengths[0], document_tenant[0], tenant_adapter_slot, row_count)
    base_output = jnp.dot(
        normed,
        lax.all_gather(value_matrix, "store", axis=0, tiled=True),
        preferred_element_type=jnp.float32,
    )
    down = lax.all_gather(adapter_down_factors, "store", axis=0, tiled=True)
    rank_total_rows = jnp.dot(
        normed, down.reshape(down.shape[0], flat_width), preferred_element_type=jnp.float32
    )
    mid = pick_rank(rank_total_rows, slots, count_of_adapters, rank_span_width)
    mid = mid.astype(jnp.bfloat16)
    select = (slots[:, None] == jnp.arange(count_of_adapters, dtype=jnp.int32)[None, :]).astype(
        jnp.bfloat16
    )
    expanded_rows = (mid[:, None, :] * select[:, :, None]).reshape(row_count, flat_width)
    up = lax.all_gather(adapter_up_factors, "store", axis=2, tiled=True)
    adapter_update = jnp.dot(
        expanded_rows, up.reshape(flat_width, up.shape[2]), preferred_element_type=jnp.float32
    )
    return (base_output + adapter_scale * adapter_update).astype(jnp.bfloat16)


def norm_kernel(source_ref, tokens_ref, gain_ref, *out_refs):
    width = tokens_ref.shape[1]
    total = jnp.zeros((tokens_ref.shape[0], lane), jnp.float32)
    for i in range(width // lane):
        part = tokens_ref[:, i * lane : (i + 1) * lane].astype(jnp.float32)
        total += part * part
    scale = lax.rsqrt(jnp.sum(total, axis=1, keepdims=True) / width + 1e-05)
    first = 0
    for out_ref in out_refs:
        for i in range(out_ref.shape[1] // lane):
            start = pl.multiple_of(source_ref[first + i], lane)
            part = tokens_ref[:, pl.ds(start, lane)].astype(jnp.float32)
            gain = gain_ref[:, pl.ds(start, lane)].astype(jnp.float32)
            out_ref[:, i * lane : (i + 1) * lane] = (part * scale * gain).astype(jnp.bfloat16)
        first += out_ref.shape[1] // lane


def norm_in_order(tokens, gain, source, widths):
    rows, width = tokens.shape
    block = 64
    return pl.pallas_call(
        norm_kernel,
        out_shape=[jax.ShapeDtypeStruct((rows, w), jnp.bfloat16) for w in widths],
        grid_spec=pltpu.PrefetchScalarGridSpec(
            num_scalar_prefetch=1,
            grid=(rows // block,),
            in_specs=[
                pl.BlockSpec((block, width), lambda i, *_: (i, 0)),
                pl.BlockSpec((1, width), lambda i, *_: (0, 0)),
            ],
            out_specs=[pl.BlockSpec((block, w), lambda i, *_: (i, 0)) for w in widths],
        ),
        compiler_params=pltpu.CompilerParams(vmem_limit_bytes=vmem),
        cost_estimate=light,
    )(source, tokens, gain.reshape(1, width))


def far_memory():
    return pl.BlockSpec(memory_space=pltpu.HBM)


def tiled(array, tile):
    return pl.BlockSpec((tile,) + array.shape[1:], lambda i, *_: (i, 0))


def rows_tile(rows):
    return 256 if rows % 256 == 0 else rows


def pick_kernel(rank, slots_ref, *refs):
    piece_refs, out_ref = refs[:-1], refs[-1]
    sides, docs = slots_ref.shape
    at = 0
    for piece in piece_refs:
        for i in range(sides * docs):
            start = pl.multiple_of(slots_ref[i // docs, i % docs] * rank, rank)
            out_ref[at : at + rank, :] = piece[pl.ds(start, rank), :]
            at += rank


def pick_adapters(pieces, slots, rank):
    count = slots.shape[0] * slots.shape[1] * len(pieces)
    columns = pieces[0].shape[1]
    whole = [pl.BlockSpec(p.shape, lambda i, *_: (0, 0)) for p in pieces]
    return pl.pallas_call(
        functools.partial(pick_kernel, rank),
        out_shape=jax.ShapeDtypeStruct((count * rank, columns), jnp.bfloat16),
        grid_spec=pltpu.PrefetchScalarGridSpec(
            num_scalar_prefetch=1,
            grid=(1,),
            in_specs=whole,
            out_specs=pl.BlockSpec((count * rank, columns), lambda i, *_: (0, 0)),
        ),
        compiler_params=pltpu.CompilerParams(vmem_limit_bytes=12 << 20),
        cost_estimate=light,
    )(slots, *pieces)


def value_kernel(plan, columns, has_sum, arrays, *refs):
    own_ref, far_ref, refs = refs[0], refs[1], refs[2:]
    sum_refs, refs = refs[:has_sum], refs[has_sum:]
    array_refs, out_refs, held_ref, sem = refs[:arrays], refs[arrays:-2], refs[-2], refs[-1]

    @pl.when(pl.program_id(0) == 0)
    def _():
        copies = [
            pltpu.make_async_copy(
                array_refs[i].at[a:b, :], held_ref.at[row : row + b - a, :], sem.at[j]
            )
            for j, (i, a, b, row) in enumerate(plan)
        ]
        for copy in copies:
            copy.start()
        for copy in copies:
            copy.wait()

    tile = own_ref.shape[0]
    both = jnp.concatenate([own_ref[...], far_ref[...]], 0)
    for n in range(0, held_ref.shape[1], columns):
        cols = slice(n, n + columns)
        acc = jnp.dot(both, held_ref[:, cols], preferred_element_type=jnp.float32)
        for side in range(2):
            term = acc[side * tile : (side + 1) * tile]
            if has_sum:
                term += sum_refs[side][:, cols]
            out_refs[side][:, cols] = term


def value_sums(own, far, arrays, plan, width, sums=()):
    rows, depth = own.shape
    tile = rows_tile(rows)
    out = jax.ShapeDtypeStruct((rows, width), jnp.float32)
    return pl.pallas_call(
        functools.partial(value_kernel, plan, 256, len(sums), len(arrays)),
        out_shape=(out, out),
        grid=(rows // tile,),
        in_specs=[tiled(b, tile) for b in (own, far, *sums)] + [far_memory()] * len(arrays),
        out_specs=[tiled(out, tile)] * 2,
        scratch_shapes=[
            pltpu.VMEM((depth, width), jnp.bfloat16),
            pltpu.SemaphoreType.DMA((len(plan),)),
        ],
        compiler_params=pltpu.CompilerParams(vmem_limit_bytes=vmem),
        cost_estimate=light,
    )(own, far, *sums, *arrays)


def load_all(array_refs, held_refs, sem, first=0):
    copies = [
        pltpu.make_async_copy(a, h, sem.at[first + i])
        for i, (a, h) in enumerate(zip(array_refs, held_refs))
    ]
    for copy in copies:
        copy.start()
    return copies


def lay_slabs(rank, parts, slots, first, held_refs, rhs_ref):
    for at, have, miss, row in parts:
        for d, slot in enumerate(slots):
            rows = slice(d * rank, (d + 1) * rank)
            start = pl.multiple_of(slot * rank, rank)
            half = held_refs[have].shape[1]
            rhs_ref[rows, at : at + half] = held_refs[have][pl.ds(start, rank), :]
            low = row + (first + d) * rank
            rhs_ref[rows, at + half : at + 2 * half] = held_refs[miss][low : low + rank, :]


def by_document(acc, ends, tile, rank):
    row = pl.program_id(0) * tile + lax.broadcasted_iota(jnp.int32, (tile, rank), 0)
    mid = jnp.zeros((tile, rank), jnp.float32)
    low = 0
    for doc, end in enumerate(ends):
        mid = jnp.where((row >= low) & (row < end), acc[:, doc * rank : (doc + 1) * rank], mid)
        low = end
    return mid


def mid_kernel(rank, parts, arrays, ends_ref, slots_ref, *refs):
    token_refs, array_refs, out_refs = refs[:2], refs[2 : 2 + arrays], refs[2 + arrays : 4 + arrays]
    held_refs, rhs_refs, sem = refs[4 + arrays : -3], refs[-3:-1], refs[-1]
    docs = slots_ref.shape[1]
    tile = out_refs[0].shape[0]

    @pl.when(pl.program_id(0) == 0)
    def _():
        for copy in load_all(array_refs, held_refs, sem):
            copy.wait()
        for side in range(2):
            slots = [slots_ref[side, d] for d in range(docs)]
            lay_slabs(rank, parts, slots, side * docs, held_refs, rhs_refs[side])

    for side in range(2):
        acc = lax.dot_general(
            token_refs[side][...], rhs_refs[side][...], nt, preferred_element_type=jnp.float32
        )
        ends = [ends_ref[side, d] for d in range(docs)]
        out_refs[side][...] = by_document(acc, ends, tile, rank)


def mid_partials(own, far, arrays, parts, ends, slots, rank):
    rows, depth = own.shape
    tile = rows_tile(rows)
    docs = slots.shape[1]
    out = jax.ShapeDtypeStruct((rows, rank), jnp.float32)
    return pl.pallas_call(
        functools.partial(mid_kernel, rank, parts, len(arrays)),
        out_shape=(out, out),
        grid_spec=pltpu.PrefetchScalarGridSpec(
            num_scalar_prefetch=2,
            grid=(rows // tile,),
            in_specs=[tiled(own, tile), tiled(far, tile)] + [far_memory()] * len(arrays),
            out_specs=[pl.BlockSpec((tile, rank), lambda i, *_: (i, 0))] * 2,
            scratch_shapes=[pltpu.VMEM(a.shape, a.dtype) for a in arrays]
            + [pltpu.VMEM((docs * rank, depth), jnp.bfloat16)] * 2
            + [pltpu.SemaphoreType.DMA((len(arrays),))],
        ),
        compiler_params=pltpu.CompilerParams(vmem_limit_bytes=vmem),
        cost_estimate=light,
    )(ends, slots, own, far, *arrays)


def last_kernel(rank, parts, arrays, slots_ref, ends_ref, at_ref, *refs):
    sum_refs, mid_refs, token_refs, refs = refs[:2], refs[2:4], refs[4:6], refs[6:]
    up_refs, array_refs, out_ref = refs[:2], refs[2 : 2 + arrays], refs[2 + arrays]
    held_refs, rhs_refs, up_ref, sem = refs[3 + arrays : -4], refs[-4:-2], refs[-2], refs[-1]
    docs = slots_ref.shape[0]
    tile, width = out_ref.shape
    ends = [ends_ref[d] for d in range(docs)]

    @pl.when(pl.program_id(0) == 0)
    def _():
        copies = load_all(array_refs, held_refs, sem)
        count = at_ref.shape[1]
        span = up_refs[0].shape[0] // count
        for i in range(2):
            for j in range(count):
                start = pl.multiple_of(at_ref[i, j], span)
                copies.append(
                    pltpu.make_async_copy(
                        up_refs[i].at[pl.ds(j * span, span), :],
                        up_ref.at[pl.ds(start, span), :],
                        sem.at[arrays + i * count + j],
                    )
                )
                copies[-1].start()
        for copy in copies:
            copy.wait()
        slots = [slots_ref[d] for d in range(docs)]
        for i, (first, part) in enumerate(parts):
            lay_slabs(rank, part, slots, first, held_refs, rhs_refs[i])

    acc = lax.dot_general(
        token_refs[0][...], rhs_refs[0][...], nt, preferred_element_type=jnp.float32
    )
    acc += lax.dot_general(
        token_refs[1][...], rhs_refs[1][...], nt, preferred_element_type=jnp.float32
    )
    mid = by_document(acc, ends, tile, rank) + mid_refs[0][...] + mid_refs[1][...]
    flat = up_ref.shape[1]
    row = pl.program_id(0) * tile + lax.broadcasted_iota(jnp.int32, (tile, flat), 0)
    slot, low = jnp.zeros((tile, flat), jnp.int32), 0
    for d, end in enumerate(ends):
        slot = jnp.where((row >= low) & (row < end), slots_ref[d], slot)
        low = end
    adapter = lax.broadcasted_iota(jnp.int32, (tile, flat), 1) // rank
    spread = jnp.where(slot == adapter, jnp.concatenate([mid] * (flat // rank), 1), 0.0)
    spread = spread.astype(jnp.bfloat16)
    columns = 256
    for n in range(0, width, columns):
        cols = slice(n, n + columns)
        delta = lax.dot_general(spread, up_ref[cols, :], nt, preferred_element_type=jnp.float32)
        base = sum_refs[0][:, cols] + sum_refs[1][:, cols]
        out_ref[:, cols] = (base + adapter_scale * delta).astype(out_ref.dtype)


def last_values(sums, mids, tokens, ups, up_at, arrays, parts, slots, ends):
    rows, width = sums[0].shape
    rank = mids[0].shape[1]
    flat = ups[0].shape[1]
    tile = rows_tile(rows)
    docs = slots.shape[0]
    return pl.pallas_call(
        functools.partial(last_kernel, rank, parts, len(arrays)),
        out_shape=jax.ShapeDtypeStruct((rows, width), jnp.bfloat16),
        grid_spec=pltpu.PrefetchScalarGridSpec(
            num_scalar_prefetch=3,
            grid=(rows // tile,),
            in_specs=[tiled(a, tile) for a in (*sums, *mids, *tokens)]
            + [far_memory()] * (2 + len(arrays)),
            out_specs=pl.BlockSpec((tile, width), lambda i, *_: (i, 0)),
            scratch_shapes=[pltpu.VMEM(a.shape, a.dtype) for a in arrays]
            + [pltpu.VMEM((docs * rank, tokens[0].shape[1]), jnp.bfloat16)] * 2
            + [pltpu.VMEM((width, flat), jnp.bfloat16)]
            + [pltpu.SemaphoreType.DMA((len(arrays) + up_at.size,))],
        ),
        compiler_params=pltpu.CompilerParams(vmem_limit_bytes=vmem),
        cost_estimate=light,
    )(slots, ends, up_at, *sums, *mids, *tokens, *ups, *arrays)


def after(value, *earlier):
    return lax.optimization_barrier((value, *earlier))[0]


def make(groups, store):
    depth = store // (rows_y * cores)

    def index(z, y, c):
        return (z * rows_y + y) * cores + c

    def pairs(move):
        return [
            (index(z, y, c), index(*move(z, y, c)))
            for z in range(depth)
            for y in range(rows_y)
            for c in range(cores)
        ]

    def along_z(value, k):
        return lax.ppermute(value, "store", pairs(lambda z, y, c: ((z + k) % depth, y, c)))

    def along_y(value):
        return lax.ppermute(value, "store", pairs(lambda z, y, c: (z, 1 - y, c)))

    def across(value):
        return lax.ppermute(value, "store", pairs(lambda z, y, c: (z, y, 1 - c)))

    def along_x(value):
        return lax.ppermute(value, "groups", [(g, g ^ 1) for g in range(groups)])

    class Line:
        def __init__(self, send):
            self.send, self.sent = send, []

        def __call__(self, value, *args):
            if len(self.sent) >= 2:
                value = after(value, self.sent[-2])
            self.sent.append(self.send(value, *args))
            return self.sent[-1]

    def per_device(
        tokens,
        input_norm_gain,
        value_matrix,
        adapter_down_factors,
        adapter_up_factors,
        document_lengths,
        document_tenant,
        tenant_adapter_slot,
    ):
        shard, adapters, rank = adapter_down_factors.shape
        flat = adapters * rank
        width = value_matrix.shape[1]
        half, part = shard // 2, 3 * shard // 8
        me = lax.axis_index("store")
        side = lax.axis_index("groups") % 2
        mz, my, mc = me // (rows_y * cores), (me // cores) % rows_y, me % cores
        take = lax.dynamic_slice_in_dim

        down = adapter_down_factors.reshape(shard, flat).T
        up = adapter_up_factors.reshape(flat, -1).T
        bit = up.shape[0] // 2
        cut = part + bit
        v_have = {
            (0, 0): jnp.concatenate(
                [
                    take(value_matrix, side * half, part, 0),
                    take(up, side * bit, bit, 0),
                    take(value_matrix, side * half + part, half - part, 0),
                    take(value_matrix, half + part - side * half, half - part, 0),
                ],
                0,
            )
        }
        v_miss = {
            (0, 0): (
                jnp.concatenate(
                    [
                        take(value_matrix, half - side * half, part, 0),
                        take(up, bit - side * bit, bit, 0),
                    ],
                    0,
                ),
                0,
            )
        }
        d_have = {(0, 0): take(down, side * half, half, 1)}
        d_rest = take(down, half - side * half, half, 1)

        ends = jnp.cumsum(document_lengths, axis=1).astype(jnp.int32)
        slots = jnp.sum(
            (document_tenant[0][:, None] == jnp.arange(adapters, dtype=jnp.int32)[None, :])
            * tenant_adapter_slot[None, :],
            axis=1,
        ).astype(jnp.int32)[None, :]
        near = jnp.concatenate([ends, slots], 0)
        far = across(near)
        ends_both = jnp.concatenate([ends, far[:1]], 0)
        slots_both = jnp.concatenate([slots, far[1:]], 0)
        slots_there = along_x(slots_both)
        d_miss = {(0, 0): (pick_adapters([d_rest], slots_both, rank), 0)}
        chosen = slots_both.size * rank

        ks = []
        for k in range(1, depth // 2 + 1):
            ks += [k, depth - k] if k != depth - k else [k]
        last = ks[-1]
        early = [k for k in ks if k != last]
        z, y, x = Line(along_z), Line(along_y), Line(along_x)

        def x_values(names, *earlier):
            got = x(after(jnp.concatenate([v_have[name][:cut] for name in names], 0), *earlier))
            for i, name in enumerate(names):
                v_miss[name] = (got, i * cut)

        def x_down(names):
            got = x(pick_adapters([d_have[name] for name in names], slots_there, rank))
            for i, name in enumerate(names):
                d_miss[name] = (got, i * chosen)

        names = [(k, dy) for k in [0] + ks for dy in range(rows_y)]
        source, up_at = [], []
        for lane_at in (mc, 1 - mc):
            for k, dy in names:
                s = index((mz - k) % depth, my ^ dy, lane_at)
                for c in range(shard // lane):
                    piece = c * lane + jnp.where(c * lane < half, 1, -1) * side * half
                    source.append(s * shard + piece)
                up_at += [(2 * s + side) * bit, (2 * s + 1 - side) * bit]
        up_at = jnp.stack(up_at).astype(jnp.int32).reshape(2, -1)
        bulk = (len(names) - rows_y) * shard
        rest = rows_y * shard
        own, own_rest, other, other_rest = norm_in_order(
            tokens,
            input_norm_gain,
            jnp.stack(source).astype(jnp.int32),
            [bulk, rest] * 2,
        )
        partner, partner_rest = across(other), across(other_rest)

        for k in ks:
            v_have[k, 0] = z(v_have[0, 0], k)
        for k in ks:
            d_have[k, 0] = z(d_have[0, 0], k)
        v_have[0, 1] = y(v_have[0, 0])
        d_have[0, 1] = y(d_have[0, 0])
        x_values([(0, 1)], slots_there)
        for k in early:
            v_have[k, 1] = y(after(v_have[k, 0], partner, v_miss[0, 1][0]))
        x_values([(k, 0) for k in early])
        x_values([(k, 1) for k in early])
        v_have[last, 1] = y(v_have[last, 0])
        x_values([(last, 0)])
        x_down([(0, 1)])
        for k in early:
            d_have[k, 1] = y(d_have[k, 0])
        x_values([(last, 1)])
        x_down([(k, 0) for k in early])
        x_down([(k, 1) for k in early])
        d_have[last, 1] = y(d_have[last, 0])
        x_down([(last, 0)])
        x_down([(last, 1)])

        def lay():
            arrays = []

            def place(array):
                for i, known in enumerate(arrays):
                    if known is array:
                        return i
                arrays.append(array)
                return len(arrays) - 1

            return arrays, place

        def values(names, *args):
            arrays, place = lay()
            plan = []
            for i, name in enumerate(names):
                h, (m, row) = place(v_have[name]), v_miss[name]
                m, at = place(m), i * shard
                plan += [
                    (h, 0, part, at),
                    (h, cut, cut + half - part, at + part),
                    (m, row, row + part, at + half),
                    (h, cut + half - part, cut + 2 * (half - part), at + half + part),
                ]
            return arrays, tuple(plan)

        arrays, plan = values(names[:-rows_y])
        sums = value_sums(own, partner, arrays, plan, width)
        arrays, plan = values(names[-rows_y:])
        sum_own, sum_far = value_sums(own_rest, partner_rest, arrays, plan, width, sums)
        sums = (sum_own, across(sum_far))

        up_lane = []
        for name in names:
            miss, row = v_miss[name]
            up_lane += [v_have[name][part:cut], miss[row + part : row + cut]]
        up_lane = jnp.concatenate(up_lane, 0)
        ups = (up_lane, across(up_lane))

        def slabs(place, names, have, miss):
            out = []
            for i, name in enumerate(names):
                m, row = miss[name]
                out.append((i * shard, place(have[name]), place(m), row))
            return tuple(out)

        arrays, place = lay()
        parts = slabs(place, names[:-rows_y], d_have, d_miss)
        mid_own, mid_far = mid_partials(own, partner, arrays, parts, ends_both, slots_both, rank)
        mids = (mid_own, across(mid_far))

        final = names[-rows_y:]
        arrays, place = lay()
        parts = [(0, slabs(place, final, d_have, d_miss))]
        far_have = {n: across(d_have[n]) for n in final}
        far_miss = {n: (across(d_miss[n][0]), d_miss[n][1]) for n in final}
        parts.append((slots.shape[1], slabs(place, final, far_have, far_miss)))
        return last_values(
            sums,
            mids,
            (own_rest, other_rest),
            ups,
            up_at,
            arrays,
            tuple(parts),
            slots[0],
            ends[0],
        )

    return per_device


def solution(mesh):
    in_specs = (
        P(("groups", "store"), None),
        P(),
        P("store", None),
        P("store", None, None),
        P(None, None, "store"),
        P(("groups", "store"), None),
        P(("groups", "store"), None),
        P(),
    )
    out_specs = P(("groups", "store"), None)
    groups, store = mesh.shape["groups"], mesh.shape["store"]

    def run(*args):
        shard = args[2].shape[0]
        cut = shard % (4 * lane) == 0 and args[4].shape[2] % 32 == 0 and store > 4 and store % (rows_y * cores) == 0 and groups % 2 == 0
        return (make(groups, store) if cut else plain)(*args)

    return jax.shard_map(
        run, mesh=mesh, in_specs=in_specs, out_specs=out_specs, check_vma=False
    )
```

```python
import functools

import jax
import jax.numpy as jnp
from jax import lax
from jax.experimental import pallas as pl
from jax.experimental.pallas import tpu as pltpu
from jax.sharding import PartitionSpec as P

adapter_scale = 2.0
cores, rows_y, lane = 2, 2, 128
nt = (((1,), (1,)), ((), ()))
vmem = 58 << 20
light = pl.CostEstimate(flops=0, bytes_accessed=0, transcendentals=0)


def token_slots(lengths, tenants, tenant_adapter_slot, row_count):
    ends = jnp.cumsum(lengths)
    position = jnp.arange(row_count, dtype=jnp.int32)
    doc_index = jnp.sum((position[:, None] >= ends[None, :]).astype(jnp.int32), axis=1)
    doc_pick = (
        doc_index[:, None] == jnp.arange(lengths.shape[0], dtype=jnp.int32)[None, :]
    ).astype(jnp.int32)
    tenant = jnp.sum(doc_pick * tenants[None, :], axis=1)
    tenant_pick = (
        tenant[:, None] == jnp.arange(tenant_adapter_slot.shape[0], dtype=jnp.int32)[None, :]
    ).astype(jnp.int32)
    return jnp.sum(tenant_pick * tenant_adapter_slot[None, :], axis=1)


def pick_rank(rank_total_rows, slots, count_of_adapters, rank_span_width):
    select = (slots[:, None] == jnp.arange(count_of_adapters, dtype=jnp.int32)[None, :]).astype(
        jnp.float32
    )
    shaped = rank_total_rows.reshape(slots.shape[0], count_of_adapters, rank_span_width)
    return jnp.sum(shaped * select[:, :, None], axis=1)


def plain(
    tokens,
    input_norm_gain,
    value_matrix,
    adapter_down_factors,
    adapter_up_factors,
    document_lengths,
    document_tenant,
    tenant_adapter_slot,
):
    row_count = tokens.shape[0]
    count_of_adapters = adapter_down_factors.shape[1]
    rank_span_width = adapter_down_factors.shape[2]
    flat_width = count_of_adapters * rank_span_width
    wide = tokens.astype(jnp.float32)
    meansq = jnp.mean(wide * wide, axis=1, keepdims=True)
    normed = (wide * lax.rsqrt(meansq + 1e-05) * input_norm_gain.astype(jnp.float32)).astype(
        jnp.bfloat16
    )
    slots = token_slots(document_lengths[0], document_tenant[0], tenant_adapter_slot, row_count)
    base_output = jnp.dot(
        normed,
        lax.all_gather(value_matrix, "store", axis=0, tiled=True),
        preferred_element_type=jnp.float32,
    )
    down = lax.all_gather(adapter_down_factors, "store", axis=0, tiled=True)
    rank_total_rows = jnp.dot(
        normed, down.reshape(down.shape[0], flat_width), preferred_element_type=jnp.float32
    )
    mid = pick_rank(rank_total_rows, slots, count_of_adapters, rank_span_width)
    mid = mid.astype(jnp.bfloat16)
    select = (slots[:, None] == jnp.arange(count_of_adapters, dtype=jnp.int32)[None, :]).astype(
        jnp.bfloat16
    )
    expanded_rows = (mid[:, None, :] * select[:, :, None]).reshape(row_count, flat_width)
    up = lax.all_gather(adapter_up_factors, "store", axis=2, tiled=True)
    adapter_update = jnp.dot(
        expanded_rows, up.reshape(flat_width, up.shape[2]), preferred_element_type=jnp.float32
    )
    return (base_output + adapter_scale * adapter_update).astype(jnp.bfloat16)


def norm_kernel(source_ref, tokens_ref, gain_ref, *out_refs):
    width = tokens_ref.shape[1]
    total = jnp.zeros((tokens_ref.shape[0], lane), jnp.float32)
    for i in range(width // lane):
        part = tokens_ref[:, i * lane : (i + 1) * lane].astype(jnp.float32)
        total += part * part
    scale = lax.rsqrt(jnp.sum(total, axis=1, keepdims=True) / width + 1e-05)
    first = 0
    for out_ref in out_refs:
        for i in range(out_ref.shape[1] // lane):
            start = pl.multiple_of(source_ref[first + i], lane)
            part = tokens_ref[:, pl.ds(start, lane)].astype(jnp.float32)
            gain = gain_ref[:, pl.ds(start, lane)].astype(jnp.float32)
            out_ref[:, i * lane : (i + 1) * lane] = (part * scale * gain).astype(jnp.bfloat16)
        first += out_ref.shape[1] // lane


def norm_in_order(tokens, gain, source, widths):
    rows, width = tokens.shape
    block = 128
    return pl.pallas_call(
        norm_kernel,
        out_shape=[jax.ShapeDtypeStruct((rows, w), jnp.bfloat16) for w in widths],
        grid_spec=pltpu.PrefetchScalarGridSpec(
            num_scalar_prefetch=1,
            grid=(rows // block,),
            in_specs=[
                pl.BlockSpec((block, width), lambda i, *_: (i, 0)),
                pl.BlockSpec((1, width), lambda i, *_: (0, 0)),
            ],
            out_specs=[pl.BlockSpec((block, w), lambda i, *_: (i, 0)) for w in widths],
        ),
        compiler_params=pltpu.CompilerParams(vmem_limit_bytes=vmem),
        cost_estimate=light,
    )(source, tokens, gain.reshape(1, width))


def far_memory():
    return pl.BlockSpec(memory_space=pltpu.HBM)


def tiled(array, tile):
    return pl.BlockSpec((tile,) + array.shape[1:], lambda i, *_: (i, 0))


def rows_tile(rows):
    return 256 if rows % 256 == 0 else rows


def pick_kernel(rank, slots_ref, *refs):
    piece_refs, out_ref = refs[:-1], refs[-1]
    sides, docs = slots_ref.shape
    at = 0
    for piece in piece_refs:
        for i in range(sides * docs):
            start = pl.multiple_of(slots_ref[i // docs, i % docs] * rank, rank)
            out_ref[at : at + rank, :] = piece[pl.ds(start, rank), :]
            at += rank


def pick_adapters(pieces, slots, rank):
    count = slots.shape[0] * slots.shape[1] * len(pieces)
    columns = pieces[0].shape[1]
    whole = [pl.BlockSpec(p.shape, lambda i, *_: (0, 0)) for p in pieces]
    return pl.pallas_call(
        functools.partial(pick_kernel, rank),
        out_shape=jax.ShapeDtypeStruct((count * rank, columns), jnp.bfloat16),
        grid_spec=pltpu.PrefetchScalarGridSpec(
            num_scalar_prefetch=1,
            grid=(1,),
            in_specs=whole,
            out_specs=pl.BlockSpec((count * rank, columns), lambda i, *_: (0, 0)),
        ),
        compiler_params=pltpu.CompilerParams(vmem_limit_bytes=12 << 20),
        cost_estimate=light,
    )(slots, *pieces)


def value_kernel(plan, columns, has_sum, arrays, *refs):
    own_ref, far_ref, refs = refs[0], refs[1], refs[2:]
    sum_refs, refs = refs[:has_sum], refs[has_sum:]
    array_refs, out_refs, held_ref, sem = refs[:arrays], refs[arrays:-2], refs[-2], refs[-1]

    @pl.when(pl.program_id(0) == 0)
    def _():
        copies = [
            pltpu.make_async_copy(
                array_refs[i].at[a:b, :], held_ref.at[row : row + b - a, :], sem.at[j]
            )
            for j, (i, a, b, row) in enumerate(plan)
        ]
        for copy in copies:
            copy.start()
        for copy in copies:
            copy.wait()

    tile = own_ref.shape[0]
    both = jnp.concatenate([own_ref[...], far_ref[...]], 0)
    for n in range(0, held_ref.shape[1], columns):
        cols = slice(n, n + columns)
        acc = jnp.dot(both, held_ref[:, cols], preferred_element_type=jnp.float32)
        terms = [acc[:tile], acc[tile:]]
        if has_sum:
            terms[0] += sum_refs[0][:, cols]
            terms[1] += sum_refs[1 + n // columns][...]
        out_refs[0][:, cols] = terms[0]
        out_refs[1 + n // columns][...] = terms[1]


def value_sums(own, far, arrays, plan, width, sums=()):
    rows, depth = own.shape
    tile, columns = rows_tile(rows), 256
    outs = [jax.ShapeDtypeStruct((rows, width), jnp.float32)]
    outs += [jax.ShapeDtypeStruct((rows, columns), jnp.float32)] * (width // columns)
    return pl.pallas_call(
        functools.partial(value_kernel, plan, columns, len(sums), len(arrays)),
        out_shape=outs,
        grid=(rows // tile,),
        in_specs=[tiled(b, tile) for b in (own, far, *sums)] + [far_memory()] * len(arrays),
        out_specs=[tiled(o, tile) for o in outs],
        scratch_shapes=[
            pltpu.VMEM((depth, width), jnp.bfloat16),
            pltpu.SemaphoreType.DMA((len(plan),)),
        ],
        compiler_params=pltpu.CompilerParams(vmem_limit_bytes=vmem),
        cost_estimate=light,
    )(own, far, *sums, *arrays)


def gather_kernel(plan, *refs):
    array_refs, out_ref, sem = refs[:-2], refs[-2], refs[-1]
    copies = [
        pltpu.make_async_copy(array_refs[i].at[a:b, :], out_ref.at[row : row + b - a, :], sem.at[j])
        for j, (i, a, b, row) in enumerate(plan)
    ]
    for copy in copies:
        copy.start()
    for copy in copies:
        copy.wait()


def gather_rows(arrays, plan):
    rows = sum(b - a for _, a, b, _ in plan)
    return pl.pallas_call(
        functools.partial(gather_kernel, plan),
        out_shape=jax.ShapeDtypeStruct((rows, arrays[0].shape[1]), arrays[0].dtype),
        in_specs=[far_memory()] * len(arrays),
        out_specs=pl.BlockSpec(memory_space=pltpu.VMEM),
        scratch_shapes=[pltpu.SemaphoreType.DMA((len(plan),))],
        compiler_params=pltpu.CompilerParams(vmem_limit_bytes=12 << 20),
        cost_estimate=light,
    )(*arrays)


def load_all(array_refs, held_refs, sem, first=0):
    copies = [
        pltpu.make_async_copy(a, h, sem.at[first + i])
        for i, (a, h) in enumerate(zip(array_refs, held_refs))
    ]
    for copy in copies:
        copy.start()
    return copies


def lay_slabs(rank, parts, slots, first, held_refs, rhs_ref):
    for at, have, miss, row in parts:
        for d, slot in enumerate(slots):
            rows = slice(d * rank, (d + 1) * rank)
            start = pl.multiple_of(slot * rank, rank)
            half = held_refs[have].shape[1]
            rhs_ref[rows, at : at + half] = held_refs[have][pl.ds(start, rank), :]
            low = row + (first + d) * rank
            rhs_ref[rows, at + half : at + 2 * half] = held_refs[miss][low : low + rank, :]


def by_document(acc, ends, tile, rank):
    row = pl.program_id(0) * tile + lax.broadcasted_iota(jnp.int32, (tile, rank), 0)
    mid = jnp.zeros((tile, rank), jnp.float32)
    low = 0
    for doc, end in enumerate(ends):
        mid = jnp.where((row >= low) & (row < end), acc[:, doc * rank : (doc + 1) * rank], mid)
        low = end
    return mid


def mid_kernel(rank, parts, arrays, ends_ref, slots_ref, *refs):
    token_refs, array_refs, out_refs = refs[:2], refs[2 : 2 + arrays], refs[2 + arrays : 4 + arrays]
    held_refs, rhs_refs, sem = refs[4 + arrays : -3], refs[-3:-1], refs[-1]
    docs = slots_ref.shape[1]
    tile = out_refs[0].shape[0]

    @pl.when(pl.program_id(0) == 0)
    def _():
        for copy in load_all(array_refs, held_refs, sem):
            copy.wait()
        for side in range(2):
            slots = [slots_ref[side, d] for d in range(docs)]
            lay_slabs(rank, parts, slots, side * docs, held_refs, rhs_refs[side])

    for side in range(2):
        acc = lax.dot_general(
            token_refs[side][...], rhs_refs[side][...], nt, preferred_element_type=jnp.float32
        )
        ends = [ends_ref[side, d] for d in range(docs)]
        out_refs[side][...] = by_document(acc, ends, tile, rank)


def mid_partials(own, far, arrays, parts, ends, slots, rank):
    rows, depth = own.shape
    tile = rows_tile(rows)
    docs = slots.shape[1]
    out = jax.ShapeDtypeStruct((rows, rank), jnp.float32)
    return pl.pallas_call(
        functools.partial(mid_kernel, rank, parts, len(arrays)),
        out_shape=(out, out),
        grid_spec=pltpu.PrefetchScalarGridSpec(
            num_scalar_prefetch=2,
            grid=(rows // tile,),
            in_specs=[tiled(own, tile), tiled(far, tile)] + [far_memory()] * len(arrays),
            out_specs=[pl.BlockSpec((tile, rank), lambda i, *_: (i, 0))] * 2,
            scratch_shapes=[pltpu.VMEM(a.shape, a.dtype) for a in arrays]
            + [pltpu.VMEM((docs * rank, depth), jnp.bfloat16)] * 2
            + [pltpu.SemaphoreType.DMA((len(arrays),))],
        ),
        compiler_params=pltpu.CompilerParams(vmem_limit_bytes=vmem),
        cost_estimate=light,
    )(ends, slots, own, far, *arrays)


def last_kernel(rank, parts, sums, arrays, slots_ref, ends_ref, at_ref, *refs):
    sum_refs, refs = refs[:sums], refs[sums:]
    mid_refs, token_refs, refs = refs[:2], refs[2:4], refs[4:]
    up_refs, array_refs, out_ref = refs[:2], refs[2 : 2 + arrays], refs[2 + arrays]
    held_refs, rhs_refs, up_ref, sem = refs[3 + arrays : -4], refs[-4:-2], refs[-2], refs[-1]
    docs = slots_ref.shape[0]
    tile, width = out_ref.shape
    ends = [ends_ref[d] for d in range(docs)]

    @pl.when(pl.program_id(0) == 0)
    def _():
        copies = load_all(array_refs, held_refs, sem)
        count = at_ref.shape[1]
        span = up_refs[0].shape[0] // count
        for i in range(2):
            for j in range(count):
                start = pl.multiple_of(at_ref[i, j], span)
                copies.append(
                    pltpu.make_async_copy(
                        up_refs[i].at[pl.ds(j * span, span), :],
                        up_ref.at[pl.ds(start, span), :],
                        sem.at[arrays + i * count + j],
                    )
                )
                copies[-1].start()
        for copy in copies:
            copy.wait()
        slots = [slots_ref[d] for d in range(docs)]
        for i, (first, part) in enumerate(parts):
            lay_slabs(rank, part, slots, first, held_refs, rhs_refs[i])

    acc = lax.dot_general(
        token_refs[0][...], rhs_refs[0][...], nt, preferred_element_type=jnp.float32
    )
    acc += lax.dot_general(
        token_refs[1][...], rhs_refs[1][...], nt, preferred_element_type=jnp.float32
    )
    mid = by_document(acc, ends, tile, rank) + mid_refs[0][...] + mid_refs[1][...]
    flat = up_ref.shape[1]
    row = pl.program_id(0) * tile + lax.broadcasted_iota(jnp.int32, (tile, flat), 0)
    slot, low = jnp.zeros((tile, flat), jnp.int32), 0
    for d, end in enumerate(ends):
        slot = jnp.where((row >= low) & (row < end), slots_ref[d], slot)
        low = end
    adapter = lax.broadcasted_iota(jnp.int32, (tile, flat), 1) // rank
    spread = jnp.where(slot == adapter, jnp.concatenate([mid] * (flat // rank), 1), 0.0)
    spread = spread.astype(jnp.bfloat16)
    columns = sum_refs[1].shape[1]
    for n in range(0, width, columns):
        cols = slice(n, n + columns)
        delta = lax.dot_general(spread, up_ref[cols, :], nt, preferred_element_type=jnp.float32)
        base = sum_refs[0][:, cols] + sum_refs[1 + n // columns][...]
        out_ref[:, cols] = (base + adapter_scale * delta).astype(out_ref.dtype)


def last_values(sums, mids, tokens, ups, up_at, arrays, parts, slots, ends):
    rows, width = sums[0].shape
    rank = mids[0].shape[1]
    flat = ups[0].shape[1]
    tile = rows_tile(rows)
    docs = slots.shape[0]
    return pl.pallas_call(
        functools.partial(last_kernel, rank, parts, len(sums), len(arrays)),
        out_shape=jax.ShapeDtypeStruct((rows, width), jnp.bfloat16),
        grid_spec=pltpu.PrefetchScalarGridSpec(
            num_scalar_prefetch=3,
            grid=(rows // tile,),
            in_specs=[tiled(a, tile) for a in (*sums, *mids, *tokens)]
            + [far_memory()] * (2 + len(arrays)),
            out_specs=pl.BlockSpec((tile, width), lambda i, *_: (i, 0)),
            scratch_shapes=[pltpu.VMEM(a.shape, a.dtype) for a in arrays]
            + [pltpu.VMEM((docs * rank, tokens[0].shape[1]), jnp.bfloat16)] * 2
            + [pltpu.VMEM((width, flat), jnp.bfloat16)]
            + [pltpu.SemaphoreType.DMA((len(arrays) + up_at.size,))],
        ),
        compiler_params=pltpu.CompilerParams(vmem_limit_bytes=vmem),
        cost_estimate=light,
    )(slots, ends, up_at, *sums, *mids, *tokens, *ups, *arrays)


def after(value, *earlier):
    return lax.optimization_barrier((value, *earlier))[0]


def make(groups, store):
    depth = store // (rows_y * cores)

    def index(z, y, c):
        return (z * rows_y + y) * cores + c

    def pairs(move):
        return [
            (index(z, y, c), index(*move(z, y, c)))
            for z in range(depth)
            for y in range(rows_y)
            for c in range(cores)
        ]

    def along_z(value, k):
        return lax.ppermute(value, "store", pairs(lambda z, y, c: ((z + k) % depth, y, c)))

    def along_y(value):
        return lax.ppermute(value, "store", pairs(lambda z, y, c: (z, 1 - y, c)))

    def across(value):
        return lax.ppermute(value, "store", pairs(lambda z, y, c: (z, y, 1 - c)))

    def along_x(value):
        return lax.ppermute(value, "groups", [(g, g ^ 1) for g in range(groups)])

    class Line:
        def __init__(self, send, most=2):
            self.send, self.most, self.sent = send, most, []

        def __call__(self, value, *args):
            if len(self.sent) >= self.most:
                value = after(value, self.sent[-self.most])
            self.sent.append(self.send(value, *args))
            return self.sent[-1]

    def per_device(
        tokens,
        input_norm_gain,
        value_matrix,
        adapter_down_factors,
        adapter_up_factors,
        document_lengths,
        document_tenant,
        tenant_adapter_slot,
    ):
        shard, adapters, rank = adapter_down_factors.shape
        flat = adapters * rank
        width = value_matrix.shape[1]
        half, part = shard // 2, 3 * shard // 8
        me = lax.axis_index("store")
        side = lax.axis_index("groups") % 2
        mz, my, mc = me // (rows_y * cores), (me // cores) % rows_y, me % cores
        take = lax.dynamic_slice_in_dim

        down = adapter_down_factors.reshape(shard, flat).T
        up = adapter_up_factors.reshape(flat, -1).T
        bit = up.shape[0] // 2
        cut = part + bit
        v_have = {
            (0, 0): jnp.concatenate(
                [
                    take(value_matrix, side * half, part, 0),
                    take(up, side * bit, bit, 0),
                    take(value_matrix, side * half + part, half - part, 0),
                    take(value_matrix, half + part - side * half, half - part, 0),
                ],
                0,
            )
        }
        v_miss = {
            (0, 0): (
                jnp.concatenate(
                    [
                        take(value_matrix, half - side * half, part, 0),
                        take(up, bit - side * bit, bit, 0),
                    ],
                    0,
                ),
                0,
            )
        }
        d_have = {(0, 0): take(down, side * half, half, 1)}
        d_rest = take(down, half - side * half, half, 1)

        ends = jnp.cumsum(document_lengths, axis=1).astype(jnp.int32)
        slots = jnp.sum(
            (document_tenant[0][:, None] == jnp.arange(adapters, dtype=jnp.int32)[None, :])
            * tenant_adapter_slot[None, :],
            axis=1,
        ).astype(jnp.int32)[None, :]
        near = jnp.concatenate([ends, slots], 0)
        far = across(near)
        ends_both = jnp.concatenate([ends, far[:1]], 0)
        slots_both = jnp.concatenate([slots, far[1:]], 0)
        slots_there = along_x(slots_both)
        d_miss = {(0, 0): (pick_adapters([d_rest], slots_both, rank), 0)}
        chosen = slots_both.size * rank

        order = [0]
        for k in range(1, depth // 2 + 1):
            order += [k, depth - k] if k != depth - k else [k]
        names = [(k, dy) for k in order for dy in range(rows_y)]
        z, y, x = Line(along_z), Line(along_y, 2), Line(along_x)

        def x_values(names, *earlier):
            got = x(after(jnp.concatenate([v_have[name][:cut] for name in names], 0), *earlier))
            for i, name in enumerate(names):
                v_miss[name] = (got, i * cut)

        def x_down(names, *earlier):
            pieces = [d_have[name] for name in names]
            pieces[0] = after(pieces[0], *earlier)
            got = x(pick_adapters(pieces, slots_there, rank))
            for i, name in enumerate(names):
                d_miss[name] = (got, i * slots_both.size * rank)

        source, up_at = [], []
        for lane_at in (mc, 1 - mc):
            for k, dy in names:
                s = index((mz - k) % depth, my ^ dy, lane_at)
                for c in range(shard // lane):
                    piece = c * lane + jnp.where(c * lane < half, 1, -1) * side * half
                    source.append(s * shard + piece)
                up_at += [(2 * s + side) * bit, (2 * s + 1 - side) * bit]
        source = jnp.stack(source).astype(jnp.int32)
        up_at = jnp.stack(up_at).astype(jnp.int32).reshape(2, -1)
        first, second = names[: len(names) // 2], names[len(names) // 2 :]
        span = len(first) * shard

        def lay():
            arrays = []

            def place(array):
                for i, known in enumerate(arrays):
                    if known is array:
                        return i
                arrays.append(array)
                return len(arrays) - 1

            return arrays, place

        def values(names):
            arrays, place = lay()
            plan = []
            for i, name in enumerate(names):
                h, (m, row) = place(v_have[name]), v_miss[name]
                m, at = place(m), i * shard
                plan += [
                    (h, 0, part, at),
                    (h, cut, cut + half - part, at + part),
                    (m, row, row + part, at + half),
                    (h, cut + half - part, cut + 2 * (half - part), at + half + part),
                ]
            return arrays, tuple(plan)

        def ups(names):
            arrays, place = lay()
            plan = []
            for i, name in enumerate(names):
                h, (m, row) = place(v_have[name]), v_miss[name]
                plan.append((h, part, cut, 2 * i * bit))
                plan.append((place(m), row + part, row + cut, (2 * i + 1) * bit))
            return gather_rows(arrays, tuple(plan))

        def slabs(place, names, have, miss):
            out = []
            for i, name in enumerate(names):
                m, row = miss[name]
                out.append((i * shard, place(have[name]), place(m), row))
            return tuple(out)

        ks = order[1:]
        early, last = ks[:-1], ks[-1]
        own, own_rest, other, other_rest = norm_in_order(
            tokens, input_norm_gain, source, [span] * 4
        )
        partner, partner_rest = across(other), across(other_rest)
        for k in ks:
            v_have[k, 0] = z(v_have[0, 0], k)
        for k in ks:
            d_have[k, 0] = z(d_have[0, 0], k)
        v_have[0, 1] = y(v_have[0, 0])
        d_have[0, 1] = y(d_have[0, 0])
        x_values([(0, 1)], slots_there)
        for k in early:
            v_have[k, 1] = y(after(v_have[k, 0], partner, v_miss[0, 1][0]))
        x_values([(k, 0) for k in early])
        x_values([(k, 1) for k in early])
        v_have[last, 1] = y(v_have[last, 0])
        x_values([(last, 0)])
        x_down([(0, 1)])
        for k in early:
            d_have[k, 1] = y(d_have[k, 0])
        arrays, plan = values(first)
        sums = value_sums(after(own, v_have[last, 1]), partner, arrays, plan, width)
        x_values([(last, 1)], sums[0])
        x_down([(k, 0) for k in early])
        x_down([(k, 1) for k in early])
        d_have[last, 1] = y(d_have[last, 0])
        x_down([(last, 0)])

        arrays, plan = values(second)
        ready = [d_have[k, 0] for k in ks]
        sum_own, *sum_far = value_sums(
            after(own_rest, *ready), partner_rest, arrays, plan, width, sums
        )
        sums = (sum_own, *[across(part) for part in sum_far])
        up_lane = ups(names)
        up_both = (up_lane, across(up_lane))

        arrays, place = lay()
        parts = slabs(place, first, d_have, d_miss)
        mid_own, mid_far = mid_partials(own, partner, arrays, parts, ends_both, slots_both, rank)
        mids = (mid_own, across(mid_far))
        x_down([(last, 1)], mids[1], up_both[1])

        arrays, place = lay()
        parts = [(0, slabs(place, second, d_have, d_miss))]
        done = d_have[last, 1]
        far_have = {n: across(after(d_have[n], done)) for n in second}
        far_miss = {n: (across(after(d_miss[n][0], done)), d_miss[n][1]) for n in second}
        parts.append((slots.shape[1], slabs(place, second, far_have, far_miss)))
        return last_values(
            sums,
            mids,
            (own_rest, other_rest),
            up_both,
            up_at,
            arrays,
            tuple(parts),
            slots[0],
            ends[0],
        )

    return per_device


def solution(mesh):
    in_specs = (
        P(("groups", "store"), None),
        P(),
        P("store", None),
        P("store", None, None),
        P(None, None, "store"),
        P(("groups", "store"), None),
        P(("groups", "store"), None),
        P(),
    )
    out_specs = P(("groups", "store"), None)
    groups, store = mesh.shape["groups"], mesh.shape["store"]

    def run(*args):
        shard = args[2].shape[0]
        cut = shard % (4 * lane) == 0 and args[4].shape[2] % 32 == 0 and store > 4 and store % (rows_y * cores) == 0 and groups % 2 == 0
        return (make(groups, store) if cut else plain)(*args)

    return jax.shard_map(
        run, mesh=mesh, in_specs=in_specs, out_specs=out_specs, check_vma=False
    )
```

```python
import functools

import jax
import jax.numpy as jnp
from jax import lax
from jax.experimental import pallas as pl
from jax.experimental.pallas import tpu as pltpu
from jax.sharding import PartitionSpec as P

adapter_scale = 2.0
cores, rows_y, lane = 2, 2, 128
nt = (((1,), (1,)), ((), ()))
light = pl.CostEstimate(flops=0, bytes_accessed=0, transcendentals=0)


def token_slots(lengths, tenants, tenant_adapter_slot, row_count):
    ends = jnp.cumsum(lengths)
    position = jnp.arange(row_count, dtype=jnp.int32)
    doc_index = jnp.sum((position[:, None] >= ends[None, :]).astype(jnp.int32), axis=1)
    doc_pick = (
        doc_index[:, None] == jnp.arange(lengths.shape[0], dtype=jnp.int32)[None, :]
    ).astype(jnp.int32)
    tenant = jnp.sum(doc_pick * tenants[None, :], axis=1)
    tenant_pick = (
        tenant[:, None] == jnp.arange(tenant_adapter_slot.shape[0], dtype=jnp.int32)[None, :]
    ).astype(jnp.int32)
    return jnp.sum(tenant_pick * tenant_adapter_slot[None, :], axis=1)


def pick_rank(rank_total_rows, slots, count_of_adapters, rank_span_width):
    select = (slots[:, None] == jnp.arange(count_of_adapters, dtype=jnp.int32)[None, :]).astype(
        jnp.float32
    )
    shaped = rank_total_rows.reshape(slots.shape[0], count_of_adapters, rank_span_width)
    return jnp.sum(shaped * select[:, :, None], axis=1)


def plain(
    tokens,
    input_norm_gain,
    value_matrix,
    adapter_down_factors,
    adapter_up_factors,
    document_lengths,
    document_tenant,
    tenant_adapter_slot,
):
    row_count = tokens.shape[0]
    count_of_adapters = adapter_down_factors.shape[1]
    rank_span_width = adapter_down_factors.shape[2]
    flat_width = count_of_adapters * rank_span_width
    wide = tokens.astype(jnp.float32)
    meansq = jnp.mean(wide * wide, axis=1, keepdims=True)
    normed = (wide * lax.rsqrt(meansq + 1e-05) * input_norm_gain.astype(jnp.float32)).astype(
        jnp.bfloat16
    )
    slots = token_slots(document_lengths[0], document_tenant[0], tenant_adapter_slot, row_count)
    base_output = jnp.dot(
        normed,
        lax.all_gather(value_matrix, "store", axis=0, tiled=True),
        preferred_element_type=jnp.float32,
    )
    down = lax.all_gather(adapter_down_factors, "store", axis=0, tiled=True)
    rank_total_rows = jnp.dot(
        normed, down.reshape(down.shape[0], flat_width), preferred_element_type=jnp.float32
    )
    mid = pick_rank(rank_total_rows, slots, count_of_adapters, rank_span_width)
    mid = mid.astype(jnp.bfloat16)
    select = (slots[:, None] == jnp.arange(count_of_adapters, dtype=jnp.int32)[None, :]).astype(
        jnp.bfloat16
    )
    expanded_rows = (mid[:, None, :] * select[:, :, None]).reshape(row_count, flat_width)
    up = lax.all_gather(adapter_up_factors, "store", axis=2, tiled=True)
    adapter_update = jnp.dot(
        expanded_rows, up.reshape(flat_width, up.shape[2]), preferred_element_type=jnp.float32
    )
    return (base_output + adapter_scale * adapter_update).astype(jnp.bfloat16)


def norm_kernel(source_ref, tokens_ref, gain_ref, *out_refs):
    width = tokens_ref.shape[1]
    total = jnp.zeros((tokens_ref.shape[0], lane), jnp.float32)
    for i in range(width // lane):
        part = tokens_ref[:, i * lane : (i + 1) * lane].astype(jnp.float32)
        total += part * part
    scale = lax.rsqrt(jnp.sum(total, axis=1, keepdims=True) / width + 1e-05)
    first = 0
    for out_ref in out_refs:
        for i in range(out_ref.shape[1] // lane):
            start = pl.multiple_of(source_ref[first + i], lane)
            part = tokens_ref[:, pl.ds(start, lane)].astype(jnp.float32)
            gain = gain_ref[:, pl.ds(start, lane)].astype(jnp.float32)
            out_ref[:, i * lane : (i + 1) * lane] = (part * scale * gain).astype(jnp.bfloat16)
        first += out_ref.shape[1] // lane


def norm_in_order(tokens, gain, source, widths):
    rows, width = tokens.shape
    block = 128
    return pl.pallas_call(
        norm_kernel,
        out_shape=[jax.ShapeDtypeStruct((rows, w), jnp.bfloat16) for w in widths],
        grid_spec=pltpu.PrefetchScalarGridSpec(
            num_scalar_prefetch=1,
            grid=(rows // block,),
            in_specs=[
                pl.BlockSpec((block, width), lambda i, *_: (i, 0)),
                pl.BlockSpec((1, width), lambda i, *_: (0, 0)),
            ],
            out_specs=[pl.BlockSpec((block, w), lambda i, *_: (i, 0)) for w in widths],
        ),
        compiler_params=pltpu.CompilerParams(vmem_limit_bytes=20 << 20),
        cost_estimate=light,
    )(source, tokens, gain.reshape(1, width))


def far_memory():
    return pl.BlockSpec(memory_space=pl.ANY)


def tiled(array, tile):
    return pl.BlockSpec((tile,) + array.shape[1:], lambda i, *_: (i, 0))


def rows_tile(rows):
    return 256 if rows % 256 == 0 else rows


def pick_kernel(rank, slots_ref, *refs):
    piece_refs, out_ref = refs[:-1], refs[-1]
    sides, docs = slots_ref.shape
    at = 0
    for piece in piece_refs:
        for i in range(sides * docs):
            start = pl.multiple_of(slots_ref[i // docs, i % docs] * rank, rank)
            out_ref[at : at + rank, :] = piece[pl.ds(start, rank), :]
            at += rank


def pick_adapters(pieces, slots, rank):
    count = slots.shape[0] * slots.shape[1] * len(pieces)
    columns = pieces[0].shape[1]
    whole = [pl.BlockSpec(p.shape, lambda i, *_: (0, 0)) for p in pieces]
    return pl.pallas_call(
        functools.partial(pick_kernel, rank),
        out_shape=jax.ShapeDtypeStruct((count * rank, columns), jnp.bfloat16),
        grid_spec=pltpu.PrefetchScalarGridSpec(
            num_scalar_prefetch=1,
            grid=(1,),
            in_specs=whole,
            out_specs=pl.BlockSpec((count * rank, columns), lambda i, *_: (0, 0)),
        ),
        compiler_params=pltpu.CompilerParams(vmem_limit_bytes=12 << 20),
        cost_estimate=light,
    )(slots, *pieces)


def value_kernel(plan, columns, has_sum, arrays, *refs):
    own_ref, far_ref, refs = refs[0], refs[1], refs[2:]
    sum_refs, refs = refs[:has_sum], refs[has_sum:]
    array_refs, out_refs, held_ref, sem = refs[:arrays], refs[arrays:-2], refs[-2], refs[-1]

    @pl.when(pl.program_id(0) == 0)
    def _():
        copies = [
            pltpu.make_async_copy(
                array_refs[i].at[a:b, :], held_ref.at[row : row + b - a, :], sem.at[j]
            )
            for j, (i, a, b, row) in enumerate(plan)
        ]
        for copy in copies:
            copy.start()
        for copy in copies:
            copy.wait()

    tile = own_ref.shape[0]
    both = jnp.concatenate([own_ref[...], far_ref[...]], 0)
    for n in range(0, held_ref.shape[1], columns):
        cols = slice(n, n + columns)
        acc = jnp.dot(both, held_ref[:, cols], preferred_element_type=jnp.float32)
        terms = [acc[:tile], acc[tile:]]
        if has_sum:
            terms[0] += sum_refs[0][:, cols]
            terms[1] += sum_refs[1 + n // columns][...]
        out_refs[0][:, cols] = terms[0]
        out_refs[1 + n // columns][...] = terms[1]


def value_sums(own, far, arrays, plan, width, sums=()):
    rows, depth = own.shape
    tile, columns = rows_tile(rows), 256
    outs = [jax.ShapeDtypeStruct((rows, width), jnp.float32)]
    outs += [jax.ShapeDtypeStruct((rows, columns), jnp.float32)] * (width // columns)
    return pl.pallas_call(
        functools.partial(value_kernel, plan, columns, len(sums), len(arrays)),
        out_shape=outs,
        grid=(rows // tile,),
        in_specs=[tiled(b, tile) for b in (own, far, *sums)] + [far_memory()] * len(arrays),
        out_specs=[tiled(o, tile) for o in outs],
        scratch_shapes=[
            pltpu.VMEM((depth, width), jnp.bfloat16),
            pltpu.SemaphoreType.DMA((len(plan),)),
        ],
        compiler_params=pltpu.CompilerParams(vmem_limit_bytes=24 << 20),
        cost_estimate=light,
    )(own, far, *sums, *arrays)


def gather_kernel(plan, *refs):
    array_refs, out_ref, sem = refs[:-2], refs[-2], refs[-1]
    copies = [
        pltpu.make_async_copy(array_refs[i].at[a:b, :], out_ref.at[row : row + b - a, :], sem.at[j])
        for j, (i, a, b, row) in enumerate(plan)
    ]
    for copy in copies:
        copy.start()
    for copy in copies:
        copy.wait()


def gather_rows(arrays, plan):
    rows = sum(b - a for _, a, b, _ in plan)
    return pl.pallas_call(
        functools.partial(gather_kernel, plan),
        out_shape=jax.ShapeDtypeStruct((rows, arrays[0].shape[1]), arrays[0].dtype),
        in_specs=[far_memory()] * len(arrays),
        out_specs=pl.BlockSpec(memory_space=pltpu.VMEM),
        scratch_shapes=[pltpu.SemaphoreType.DMA((len(plan),))],
        compiler_params=pltpu.CompilerParams(vmem_limit_bytes=12 << 20),
        cost_estimate=light,
    )(*arrays)


def load_all(array_refs, held_refs, sem, first=0):
    copies = [
        pltpu.make_async_copy(a, h, sem.at[first + i])
        for i, (a, h) in enumerate(zip(array_refs, held_refs))
    ]
    for copy in copies:
        copy.start()
    return copies


def lay_slabs(rank, parts, slots, first, held_refs, rhs_ref):
    for at, have, miss, row in parts:
        for d, slot in enumerate(slots):
            rows = slice(d * rank, (d + 1) * rank)
            start = pl.multiple_of(slot * rank, rank)
            half = held_refs[have].shape[1]
            rhs_ref[rows, at : at + half] = held_refs[have][pl.ds(start, rank), :]
            low = row + (first + d) * rank
            rhs_ref[rows, at + half : at + 2 * half] = held_refs[miss][low : low + rank, :]


def by_document(acc, ends, tile, rank):
    row = pl.program_id(0) * tile + lax.broadcasted_iota(jnp.int32, (tile, rank), 0)
    mid = jnp.zeros((tile, rank), jnp.float32)
    low = 0
    for doc, end in enumerate(ends):
        mid = jnp.where((row >= low) & (row < end), acc[:, doc * rank : (doc + 1) * rank], mid)
        low = end
    return mid


def mid_kernel(rank, parts, arrays, ends_ref, slots_ref, *refs):
    token_refs, array_refs, out_refs = refs[:2], refs[2 : 2 + arrays], refs[2 + arrays : 4 + arrays]
    held_refs, rhs_refs, sem = refs[4 + arrays : -3], refs[-3:-1], refs[-1]
    docs = slots_ref.shape[1]
    tile = out_refs[0].shape[0]

    @pl.when(pl.program_id(0) == 0)
    def _():
        for copy in load_all(array_refs, held_refs, sem):
            copy.wait()
        for side in range(2):
            slots = [slots_ref[side, d] for d in range(docs)]
            lay_slabs(rank, parts, slots, side * docs, held_refs, rhs_refs[side])

    for side in range(2):
        acc = lax.dot_general(
            token_refs[side][...], rhs_refs[side][...], nt, preferred_element_type=jnp.float32
        )
        ends = [ends_ref[side, d] for d in range(docs)]
        out_refs[side][...] = by_document(acc, ends, tile, rank)


def mid_partials(own, far, arrays, parts, ends, slots, rank):
    rows, depth = own.shape
    tile = rows_tile(rows)
    docs = slots.shape[1]
    out = jax.ShapeDtypeStruct((rows, rank), jnp.float32)
    return pl.pallas_call(
        functools.partial(mid_kernel, rank, parts, len(arrays)),
        out_shape=(out, out),
        grid_spec=pltpu.PrefetchScalarGridSpec(
            num_scalar_prefetch=2,
            grid=(rows // tile,),
            in_specs=[tiled(own, tile), tiled(far, tile)] + [far_memory()] * len(arrays),
            out_specs=[pl.BlockSpec((tile, rank), lambda i, *_: (i, 0))] * 2,
            scratch_shapes=[pltpu.VMEM(a.shape, a.dtype) for a in arrays]
            + [pltpu.VMEM((docs * rank, depth), jnp.bfloat16)] * 2
            + [pltpu.SemaphoreType.DMA((len(arrays),))],
        ),
        compiler_params=pltpu.CompilerParams(vmem_limit_bytes=20 << 20),
        cost_estimate=light,
    )(ends, slots, own, far, *arrays)


def last_kernel(rank, parts, sums, arrays, slots_ref, ends_ref, at_ref, *refs):
    sum_refs, refs = refs[:sums], refs[sums:]
    mid_refs, token_refs, refs = refs[:2], refs[2:4], refs[4:]
    up_refs, array_refs, out_ref = refs[:2], refs[2 : 2 + arrays], refs[2 + arrays]
    held_refs, rhs_refs, up_ref, sem = refs[3 + arrays : -4], refs[-4:-2], refs[-2], refs[-1]
    docs = slots_ref.shape[0]
    tile, width = out_ref.shape
    ends = [ends_ref[d] for d in range(docs)]

    @pl.when(pl.program_id(0) == 0)
    def _():
        copies = load_all(array_refs, held_refs, sem)
        count = at_ref.shape[1]
        span = up_refs[0].shape[0] // count
        for i in range(2):
            for j in range(count):
                start = pl.multiple_of(at_ref[i, j], span)
                copies.append(
                    pltpu.make_async_copy(
                        up_refs[i].at[pl.ds(j * span, span), :],
                        up_ref.at[pl.ds(start, span), :],
                        sem.at[arrays + i * count + j],
                    )
                )
                copies[-1].start()
        for copy in copies:
            copy.wait()
        slots = [slots_ref[d] for d in range(docs)]
        for i, (first, part) in enumerate(parts):
            lay_slabs(rank, part, slots, first, held_refs, rhs_refs[i])

    acc = lax.dot_general(
        token_refs[0][...], rhs_refs[0][...], nt, preferred_element_type=jnp.float32
    )
    acc += lax.dot_general(
        token_refs[1][...], rhs_refs[1][...], nt, preferred_element_type=jnp.float32
    )
    mid = by_document(acc, ends, tile, rank) + mid_refs[0][...] + mid_refs[1][...]
    flat = up_ref.shape[1]
    row = pl.program_id(0) * tile + lax.broadcasted_iota(jnp.int32, (tile, flat), 0)
    slot, low = jnp.zeros((tile, flat), jnp.int32), 0
    for d, end in enumerate(ends):
        slot = jnp.where((row >= low) & (row < end), slots_ref[d], slot)
        low = end
    adapter = lax.broadcasted_iota(jnp.int32, (tile, flat), 1) // rank
    spread = jnp.where(slot == adapter, jnp.concatenate([mid] * (flat // rank), 1), 0.0)
    spread = spread.astype(jnp.bfloat16)
    columns = sum_refs[1].shape[1]
    for n in range(0, width, columns):
        cols = slice(n, n + columns)
        delta = lax.dot_general(spread, up_ref[cols, :], nt, preferred_element_type=jnp.float32)
        base = sum_refs[0][:, cols] + sum_refs[1 + n // columns][...]
        out_ref[:, cols] = (base + adapter_scale * delta).astype(out_ref.dtype)


def last_values(sums, mids, tokens, ups, up_at, arrays, parts, slots, ends):
    rows, width = sums[0].shape
    rank = mids[0].shape[1]
    flat = ups[0].shape[1]
    tile = rows_tile(rows)
    docs = slots.shape[0]
    return pl.pallas_call(
        functools.partial(last_kernel, rank, parts, len(sums), len(arrays)),
        out_shape=jax.ShapeDtypeStruct((rows, width), jnp.bfloat16),
        grid_spec=pltpu.PrefetchScalarGridSpec(
            num_scalar_prefetch=3,
            grid=(rows // tile,),
            in_specs=[tiled(a, tile) for a in (*sums, *mids, *tokens)]
            + [far_memory()] * (2 + len(arrays)),
            out_specs=pl.BlockSpec((tile, width), lambda i, *_: (i, 0)),
            scratch_shapes=[pltpu.VMEM(a.shape, a.dtype) for a in arrays]
            + [pltpu.VMEM((docs * rank, tokens[0].shape[1]), jnp.bfloat16)] * 2
            + [pltpu.VMEM((width, flat), jnp.bfloat16)]
            + [pltpu.SemaphoreType.DMA((len(arrays) + up_at.size,))],
        ),
        compiler_params=pltpu.CompilerParams(vmem_limit_bytes=34 << 20),
        cost_estimate=light,
    )(slots, ends, up_at, *sums, *mids, *tokens, *ups, *arrays)


def after(value, *earlier):
    return lax.optimization_barrier((value, *earlier))[0]


def make(groups, store):
    depth = store // (rows_y * cores)

    def index(z, y, c):
        return (z * rows_y + y) * cores + c

    def pairs(move):
        return [
            (index(z, y, c), index(*move(z, y, c)))
            for z in range(depth)
            for y in range(rows_y)
            for c in range(cores)
        ]

    def along_z(value, k):
        return lax.ppermute(value, "store", pairs(lambda z, y, c: ((z + k) % depth, y, c)))

    def along_y(value):
        return lax.ppermute(value, "store", pairs(lambda z, y, c: (z, 1 - y, c)))

    def across(value):
        return lax.ppermute(value, "store", pairs(lambda z, y, c: (z, y, 1 - c)))

    def along_x(value):
        return lax.ppermute(value, "groups", [(g, g ^ 1) for g in range(groups)])

    class Line:
        def __init__(self, send, most=2):
            self.send, self.most, self.sent = send, most, []

        def __call__(self, value, *args):
            if len(self.sent) >= self.most:
                value = after(value, self.sent[-self.most])
            self.sent.append(self.send(value, *args))
            return self.sent[-1]

    def per_device(
        tokens,
        input_norm_gain,
        value_matrix,
        adapter_down_factors,
        adapter_up_factors,
        document_lengths,
        document_tenant,
        tenant_adapter_slot,
    ):
        shard, adapters, rank = adapter_down_factors.shape
        flat = adapters * rank
        width = value_matrix.shape[1]
        half, part = shard // 2, 3 * shard // 8
        me = lax.axis_index("store")
        side = lax.axis_index("groups") % 2
        mz, my, mc = me // (rows_y * cores), (me // cores) % rows_y, me % cores
        take = lax.dynamic_slice_in_dim

        down = adapter_down_factors.reshape(shard, flat).T
        up = adapter_up_factors.reshape(flat, -1).T
        bit = up.shape[0] // 2
        cut = part + bit
        v_have = {
            (0, 0): jnp.concatenate(
                [
                    take(value_matrix, side * half, part, 0),
                    take(up, side * bit, bit, 0),
                    take(value_matrix, side * half + part, half - part, 0),
                    take(value_matrix, half + part - side * half, half - part, 0),
                ],
                0,
            )
        }
        v_miss = {
            (0, 0): (
                jnp.concatenate(
                    [
                        take(value_matrix, half - side * half, part, 0),
                        take(up, bit - side * bit, bit, 0),
                    ],
                    0,
                ),
                0,
            )
        }
        d_have = {(0, 0): take(down, side * half, half, 1)}
        d_rest = take(down, half - side * half, half, 1)

        ends = jnp.cumsum(document_lengths, axis=1).astype(jnp.int32)
        slots = jnp.sum(
            (document_tenant[0][:, None] == jnp.arange(adapters, dtype=jnp.int32)[None, :])
            * tenant_adapter_slot[None, :],
            axis=1,
        ).astype(jnp.int32)[None, :]
        near = jnp.concatenate([ends, slots], 0)
        far = across(near)
        ends_both = jnp.concatenate([ends, far[:1]], 0)
        slots_both = jnp.concatenate([slots, far[1:]], 0)
        slots_there = along_x(slots_both)
        d_miss = {(0, 0): (pick_adapters([d_rest], slots_both, rank), 0)}
        chosen = slots_both.size * rank

        order = [0]
        for k in range(1, depth // 2 + 1):
            order += [k, depth - k] if k != depth - k else [k]
        names = [(k, dy) for k in order for dy in range(rows_y)]
        z, y, x = Line(along_z), Line(along_y, 2), Line(along_x)

        def x_values(names, *earlier):
            got = x(after(jnp.concatenate([v_have[name][:cut] for name in names], 0), *earlier))
            for i, name in enumerate(names):
                v_miss[name] = (got, i * cut)

        def x_down(names, *earlier):
            pieces = [d_have[name] for name in names]
            pieces[0] = after(pieces[0], *earlier)
            got = x(pick_adapters(pieces, slots_there, rank))
            for i, name in enumerate(names):
                d_miss[name] = (got, i * slots_both.size * rank)

        source, up_at = [], []
        for lane_at in (mc, 1 - mc):
            for k, dy in names:
                s = index((mz - k) % depth, my ^ dy, lane_at)
                for c in range(shard // lane):
                    piece = c * lane + jnp.where(c * lane < half, 1, -1) * side * half
                    source.append(s * shard + piece)
                up_at += [(2 * s + side) * bit, (2 * s + 1 - side) * bit]
        source = jnp.stack(source).astype(jnp.int32)
        up_at = jnp.stack(up_at).astype(jnp.int32).reshape(2, -1)
        first, second = names[: len(names) // 2], names[len(names) // 2 :]
        span = len(first) * shard

        def lay():
            arrays = []

            def place(array):
                for i, known in enumerate(arrays):
                    if known is array:
                        return i
                arrays.append(array)
                return len(arrays) - 1

            return arrays, place

        def values(names):
            arrays, place = lay()
            plan = []
            for i, name in enumerate(names):
                h, (m, row) = place(v_have[name]), v_miss[name]
                m, at = place(m), i * shard
                plan += [
                    (h, 0, part, at),
                    (h, cut, cut + half - part, at + part),
                    (m, row, row + part, at + half),
                    (h, cut + half - part, cut + 2 * (half - part), at + half + part),
                ]
            return arrays, tuple(plan)

        def ups(names):
            arrays, place = lay()
            plan = []
            for i, name in enumerate(names):
                h, (m, row) = place(v_have[name]), v_miss[name]
                plan.append((h, part, cut, 2 * i * bit))
                plan.append((place(m), row + part, row + cut, (2 * i + 1) * bit))
            return gather_rows(arrays, tuple(plan))

        def slabs(place, names, have, miss):
            out = []
            for i, name in enumerate(names):
                m, row = miss[name]
                out.append((i * shard, place(have[name]), place(m), row))
            return tuple(out)

        ks = order[1:]
        early, last = ks[:-1], ks[-1]
        own, own_rest, other, other_rest = norm_in_order(
            tokens, input_norm_gain, source, [span] * 4
        )
        partner, partner_rest = across(other), across(other_rest)
        for k in ks:
            v_have[k, 0] = z(v_have[0, 0], k)
        for k in ks:
            d_have[k, 0] = z(d_have[0, 0], k)
        v_have[0, 1] = y(v_have[0, 0])
        d_have[0, 1] = y(d_have[0, 0])
        x_values([(0, 1)], slots_there)
        x_down([(0, 1)])
        for i, k in enumerate(early):
            pins = [partner, partner_rest][: i + 1] + [d_miss[0, 1][0]] * i
            v_have[k, 1] = y(after(v_have[k, 0], *pins))
            x_values([(k, 0)])
        for k in early:
            x_values([(k, 1)])
        v_have[last, 1] = y(v_have[last, 0])
        x_values([(last, 0)])
        for k in early:
            d_have[k, 1] = y(d_have[k, 0])
        arrays, plan = values(first)
        sums = value_sums(after(own, v_have[last, 1]), partner, arrays, plan, width)
        x_values([(last, 1)], sums[0])
        for k in early:
            x_down([(k, 0)])
        for k in early:
            x_down([(k, 1)])
        d_have[last, 1] = y(d_have[last, 0])
        x_down([(last, 0)])

        arrays, plan = values(second)
        ready = [d_have[k, 0] for k in ks]
        sum_own, *sum_far = value_sums(
            after(own_rest, *ready), partner_rest, arrays, plan, width, sums
        )
        sums = (sum_own, *[across(part) for part in sum_far])
        up_lane = ups(names)
        up_both = (up_lane, across(up_lane))

        arrays, place = lay()
        parts = slabs(place, first, d_have, d_miss)
        mid_own, mid_far = mid_partials(own, partner, arrays, parts, ends_both, slots_both, rank)
        mids = (mid_own, across(mid_far))
        x_down([(last, 1)], mids[1], up_both[1])

        arrays, place = lay()
        parts = [(0, slabs(place, second, d_have, d_miss))]
        done = d_have[last, 1]
        far_have = {n: across(after(d_have[n], done)) for n in second}
        far_miss = {n: (across(after(d_miss[n][0], done)), d_miss[n][1]) for n in second}
        parts.append((slots.shape[1], slabs(place, second, far_have, far_miss)))
        return last_values(
            sums,
            mids,
            (own_rest, other_rest),
            up_both,
            up_at,
            arrays,
            tuple(parts),
            slots[0],
            ends[0],
        )

    return per_device


def solution(mesh):
    in_specs = (
        P(("groups", "store"), None),
        P(),
        P("store", None),
        P("store", None, None),
        P(None, None, "store"),
        P(("groups", "store"), None),
        P(("groups", "store"), None),
        P(),
    )
    out_specs = P(("groups", "store"), None)
    groups, store = mesh.shape["groups"], mesh.shape["store"]

    def run(*args):
        shard = args[2].shape[0]
        cut = shard % (4 * lane) == 0 and args[4].shape[2] % 32 == 0 and store > 4 and store % (rows_y * cores) == 0 and groups % 2 == 0
        return (make(groups, store) if cut else plain)(*args)

    return jax.shard_map(
        run, mesh=mesh, in_specs=in_specs, out_specs=out_specs, check_vma=False
    )
```

```python
import functools

import jax
import jax.numpy as jnp
from jax import lax
from jax.experimental import pallas as pl
from jax.experimental.pallas import tpu as pltpu
from jax.sharding import PartitionSpec as P

adapter_scale = 2.0
cores, rows_y, lane = 2, 2, 128
nt = (((1,), (1,)), ((), ()))
light = pl.CostEstimate(flops=0, bytes_accessed=0, transcendentals=0)


def token_slots(lengths, tenants, tenant_adapter_slot, row_count):
    ends = jnp.cumsum(lengths)
    position = jnp.arange(row_count, dtype=jnp.int32)
    doc_index = jnp.sum((position[:, None] >= ends[None, :]).astype(jnp.int32), axis=1)
    doc_pick = (
        doc_index[:, None] == jnp.arange(lengths.shape[0], dtype=jnp.int32)[None, :]
    ).astype(jnp.int32)
    tenant = jnp.sum(doc_pick * tenants[None, :], axis=1)
    tenant_pick = (
        tenant[:, None] == jnp.arange(tenant_adapter_slot.shape[0], dtype=jnp.int32)[None, :]
    ).astype(jnp.int32)
    return jnp.sum(tenant_pick * tenant_adapter_slot[None, :], axis=1)


def pick_rank(rank_total_rows, slots, count_of_adapters, rank_span_width):
    select = (slots[:, None] == jnp.arange(count_of_adapters, dtype=jnp.int32)[None, :]).astype(
        jnp.float32
    )
    shaped = rank_total_rows.reshape(slots.shape[0], count_of_adapters, rank_span_width)
    return jnp.sum(shaped * select[:, :, None], axis=1)


def plain(
    tokens,
    input_norm_gain,
    value_matrix,
    adapter_down_factors,
    adapter_up_factors,
    document_lengths,
    document_tenant,
    tenant_adapter_slot,
):
    row_count = tokens.shape[0]
    count_of_adapters = adapter_down_factors.shape[1]
    rank_span_width = adapter_down_factors.shape[2]
    flat_width = count_of_adapters * rank_span_width
    wide = tokens.astype(jnp.float32)
    meansq = jnp.mean(wide * wide, axis=1, keepdims=True)
    normed = (wide * lax.rsqrt(meansq + 1e-05) * input_norm_gain.astype(jnp.float32)).astype(
        jnp.bfloat16
    )
    slots = token_slots(document_lengths[0], document_tenant[0], tenant_adapter_slot, row_count)
    base_output = jnp.dot(
        normed,
        lax.all_gather(value_matrix, "store", axis=0, tiled=True),
        preferred_element_type=jnp.float32,
    )
    down = lax.all_gather(adapter_down_factors, "store", axis=0, tiled=True)
    rank_total_rows = jnp.dot(
        normed, down.reshape(down.shape[0], flat_width), preferred_element_type=jnp.float32
    )
    mid = pick_rank(rank_total_rows, slots, count_of_adapters, rank_span_width)
    mid = mid.astype(jnp.bfloat16)
    select = (slots[:, None] == jnp.arange(count_of_adapters, dtype=jnp.int32)[None, :]).astype(
        jnp.bfloat16
    )
    expanded_rows = (mid[:, None, :] * select[:, :, None]).reshape(row_count, flat_width)
    up = lax.all_gather(adapter_up_factors, "store", axis=2, tiled=True)
    adapter_update = jnp.dot(
        expanded_rows, up.reshape(flat_width, up.shape[2]), preferred_element_type=jnp.float32
    )
    return (base_output + adapter_scale * adapter_update).astype(jnp.bfloat16)


def norm_kernel(source_ref, tokens_ref, gain_ref, *out_refs):
    width = tokens_ref.shape[1]
    total = jnp.zeros((tokens_ref.shape[0], lane), jnp.float32)
    for i in range(width // lane):
        part = tokens_ref[:, i * lane : (i + 1) * lane].astype(jnp.float32)
        total += part * part
    scale = lax.rsqrt(jnp.sum(total, axis=1, keepdims=True) / width + 1e-05)
    first = 0
    for out_ref in out_refs:
        for i in range(out_ref.shape[1] // lane):
            start = pl.multiple_of(source_ref[first + i], lane)
            part = tokens_ref[:, pl.ds(start, lane)].astype(jnp.float32)
            gain = gain_ref[:, pl.ds(start, lane)].astype(jnp.float32)
            out_ref[:, i * lane : (i + 1) * lane] = (part * scale * gain).astype(jnp.bfloat16)
        first += out_ref.shape[1] // lane


def norm_in_order(tokens, gain, source, widths):
    rows, width = tokens.shape
    block = 128
    return pl.pallas_call(
        norm_kernel,
        out_shape=[jax.ShapeDtypeStruct((rows, w), jnp.bfloat16) for w in widths],
        grid_spec=pltpu.PrefetchScalarGridSpec(
            num_scalar_prefetch=1,
            grid=(rows // block,),
            in_specs=[
                pl.BlockSpec((block, width), lambda i, *_: (i, 0)),
                pl.BlockSpec((1, width), lambda i, *_: (0, 0)),
            ],
            out_specs=[pl.BlockSpec((block, w), lambda i, *_: (i, 0)) for w in widths],
        ),
        compiler_params=pltpu.CompilerParams(vmem_limit_bytes=20 << 20),
        cost_estimate=light,
    )(source, tokens, gain.reshape(1, width))


def far_memory():
    return pl.BlockSpec(memory_space=pl.ANY)


def tiled(array, tile):
    return pl.BlockSpec((tile,) + array.shape[1:], lambda i, *_: (i, 0))


def rows_tile(rows):
    return 256 if rows % 256 == 0 else rows


def pick_kernel(rank, slots_ref, *refs):
    piece_refs, out_ref = refs[:-1], refs[-1]
    sides, docs = slots_ref.shape
    at = 0
    for piece in piece_refs:
        for i in range(sides * docs):
            start = pl.multiple_of(slots_ref[i // docs, i % docs] * rank, rank)
            out_ref[at : at + rank, :] = piece[pl.ds(start, rank), :]
            at += rank


def pick_adapters(pieces, slots, rank):
    count = slots.shape[0] * slots.shape[1] * len(pieces)
    columns = pieces[0].shape[1]
    whole = [pl.BlockSpec(p.shape, lambda i, *_: (0, 0)) for p in pieces]
    return pl.pallas_call(
        functools.partial(pick_kernel, rank),
        out_shape=jax.ShapeDtypeStruct((count * rank, columns), jnp.bfloat16),
        grid_spec=pltpu.PrefetchScalarGridSpec(
            num_scalar_prefetch=1,
            grid=(1,),
            in_specs=whole,
            out_specs=pl.BlockSpec((count * rank, columns), lambda i, *_: (0, 0)),
        ),
        compiler_params=pltpu.CompilerParams(vmem_limit_bytes=12 << 20),
        cost_estimate=light,
    )(slots, *pieces)


def value_kernel(plan, columns, has_sum, arrays, *refs):
    own_ref, far_ref, refs = refs[0], refs[1], refs[2:]
    sum_refs, refs = refs[:has_sum], refs[has_sum:]
    array_refs, out_refs, held_ref, sem = refs[:arrays], refs[arrays:-2], refs[-2], refs[-1]

    @pl.when(pl.program_id(0) == 0)
    def _():
        copies = [
            pltpu.make_async_copy(
                array_refs[i].at[a:b, :], held_ref.at[row : row + b - a, :], sem.at[j]
            )
            for j, (i, a, b, row) in enumerate(plan)
        ]
        for copy in copies:
            copy.start()
        for copy in copies:
            copy.wait()

    tile = own_ref.shape[0]
    both = jnp.concatenate([own_ref[...], far_ref[...]], 0)
    for n in range(0, held_ref.shape[1], columns):
        cols = slice(n, n + columns)
        acc = jnp.dot(both, held_ref[:, cols], preferred_element_type=jnp.float32)
        terms = [acc[:tile], acc[tile:]]
        if has_sum:
            terms[0] += sum_refs[0][:, cols]
            terms[1] += sum_refs[1 + n // columns][...]
        out_refs[0][:, cols] = terms[0]
        out_refs[1 + n // columns][...] = terms[1].astype(out_refs[1].dtype)


def value_sums(own, far, arrays, plan, width, sums=(), far_type=jnp.float32):
    rows, depth = own.shape
    tile, columns = rows_tile(rows), 256
    outs = [jax.ShapeDtypeStruct((rows, width), jnp.float32)]
    outs += [jax.ShapeDtypeStruct((rows, columns), far_type)] * (width // columns)
    return pl.pallas_call(
        functools.partial(value_kernel, plan, columns, len(sums), len(arrays)),
        out_shape=outs,
        grid=(rows // tile,),
        in_specs=[tiled(b, tile) for b in (own, far, *sums)] + [far_memory()] * len(arrays),
        out_specs=[tiled(o, tile) for o in outs],
        scratch_shapes=[
            pltpu.VMEM((depth, width), jnp.bfloat16),
            pltpu.SemaphoreType.DMA((len(plan),)),
        ],
        compiler_params=pltpu.CompilerParams(vmem_limit_bytes=24 << 20),
        cost_estimate=light,
    )(own, far, *sums, *arrays)


def cut_kernel(plan, side_ref, *refs):
    arrays = 1 + max(p[0] for p in plan)
    array_refs, out_refs, sem = refs[:arrays], refs[arrays:-1], refs[-1]
    copies = []
    for j, (i, o, axis, length, even, odd, at) in enumerate(plan):
        start = pl.multiple_of(even + side_ref[0] * (odd - even), 16 if axis == 0 else lane)
        src, dst = [slice(None)] * 2, [slice(None)] * 2
        src[axis], dst[axis] = pl.ds(start, length), slice(at, at + length)
        copies.append(
            pltpu.make_async_copy(
                array_refs[i].at[tuple(src)], out_refs[o].at[tuple(dst)], sem.at[j]
            )
        )
        copies[-1].start()
    for copy in copies:
        copy.wait()


def cut_shards(arrays, shapes, plan, side):
    return pl.pallas_call(
        functools.partial(cut_kernel, plan),
        out_shape=[jax.ShapeDtypeStruct(s, jnp.bfloat16) for s in shapes],
        grid_spec=pltpu.PrefetchScalarGridSpec(
            num_scalar_prefetch=1,
            in_specs=[far_memory()] * len(arrays),
            out_specs=[pl.BlockSpec(memory_space=pltpu.VMEM)] * len(shapes),
            scratch_shapes=[pltpu.SemaphoreType.DMA((len(plan),))],
        ),
        compiler_params=pltpu.CompilerParams(vmem_limit_bytes=12 << 20),
        cost_estimate=light,
    )(side.reshape(1).astype(jnp.int32), *arrays)


def gather_kernel(plan, *refs):
    array_refs, out_ref, sem = refs[:-2], refs[-2], refs[-1]
    copies = [
        pltpu.make_async_copy(array_refs[i].at[a:b, :], out_ref.at[row : row + b - a, :], sem.at[j])
        for j, (i, a, b, row) in enumerate(plan)
    ]
    for copy in copies:
        copy.start()
    for copy in copies:
        copy.wait()


def gather_rows(arrays, plan):
    rows = sum(b - a for _, a, b, _ in plan)
    return pl.pallas_call(
        functools.partial(gather_kernel, plan),
        out_shape=jax.ShapeDtypeStruct((rows, arrays[0].shape[1]), arrays[0].dtype),
        in_specs=[far_memory()] * len(arrays),
        out_specs=pl.BlockSpec(memory_space=pltpu.VMEM),
        scratch_shapes=[pltpu.SemaphoreType.DMA((len(plan),))],
        compiler_params=pltpu.CompilerParams(vmem_limit_bytes=12 << 20),
        cost_estimate=light,
    )(*arrays)


def load_all(array_refs, held_refs, sem, first=0):
    copies = [
        pltpu.make_async_copy(a, h, sem.at[first + i])
        for i, (a, h) in enumerate(zip(array_refs, held_refs))
    ]
    for copy in copies:
        copy.start()
    return copies


def lay_slabs(rank, parts, slots, first, held_refs, rhs_ref):
    for at, have, miss, row in parts:
        for d, slot in enumerate(slots):
            rows = slice(d * rank, (d + 1) * rank)
            start = pl.multiple_of(slot * rank, rank)
            half = held_refs[have].shape[1]
            rhs_ref[rows, at : at + half] = held_refs[have][pl.ds(start, rank), :]
            low = row + (first + d) * rank
            rhs_ref[rows, at + half : at + 2 * half] = held_refs[miss][low : low + rank, :]


def by_document(acc, ends, tile, rank):
    row = pl.program_id(0) * tile + lax.broadcasted_iota(jnp.int32, (tile, rank), 0)
    mid = jnp.zeros((tile, rank), jnp.float32)
    low = 0
    for doc, end in enumerate(ends):
        mid = jnp.where((row >= low) & (row < end), acc[:, doc * rank : (doc + 1) * rank], mid)
        low = end
    return mid


def mid_kernel(rank, parts, arrays, ends_ref, slots_ref, *refs):
    token_refs, array_refs, out_refs = refs[:2], refs[2 : 2 + arrays], refs[2 + arrays : 4 + arrays]
    held_refs, rhs_refs, sem = refs[4 + arrays : -3], refs[-3:-1], refs[-1]
    docs = slots_ref.shape[1]
    tile = out_refs[0].shape[0]

    @pl.when(pl.program_id(0) == 0)
    def _():
        for copy in load_all(array_refs, held_refs, sem):
            copy.wait()
        for side in range(2):
            slots = [slots_ref[side, d] for d in range(docs)]
            lay_slabs(rank, parts, slots, side * docs, held_refs, rhs_refs[side])

    for side in range(2):
        acc = lax.dot_general(
            token_refs[side][...], rhs_refs[side][...], nt, preferred_element_type=jnp.float32
        )
        ends = [ends_ref[side, d] for d in range(docs)]
        out_refs[side][...] = by_document(acc, ends, tile, rank)


def mid_partials(own, far, arrays, parts, ends, slots, rank):
    rows, depth = own.shape
    tile = rows_tile(rows)
    docs = slots.shape[1]
    out = jax.ShapeDtypeStruct((rows, rank), jnp.float32)
    return pl.pallas_call(
        functools.partial(mid_kernel, rank, parts, len(arrays)),
        out_shape=(out, out),
        grid_spec=pltpu.PrefetchScalarGridSpec(
            num_scalar_prefetch=2,
            grid=(rows // tile,),
            in_specs=[tiled(own, tile), tiled(far, tile)] + [far_memory()] * len(arrays),
            out_specs=[pl.BlockSpec((tile, rank), lambda i, *_: (i, 0))] * 2,
            scratch_shapes=[pltpu.VMEM(a.shape, a.dtype) for a in arrays]
            + [pltpu.VMEM((docs * rank, depth), jnp.bfloat16)] * 2
            + [pltpu.SemaphoreType.DMA((len(arrays),))],
        ),
        compiler_params=pltpu.CompilerParams(vmem_limit_bytes=20 << 20),
        cost_estimate=light,
    )(ends, slots, own, far, *arrays)


def last_kernel(rank, parts, sums, arrays, slots_ref, ends_ref, at_ref, *refs):
    sum_refs, refs = refs[:sums], refs[sums:]
    mid_refs, token_refs, refs = refs[:2], refs[2:4], refs[4:]
    up_refs, array_refs, out_ref = refs[:2], refs[2 : 2 + arrays], refs[2 + arrays]
    held_refs, rhs_refs, up_ref, sem = refs[3 + arrays : -4], refs[-4:-2], refs[-2], refs[-1]
    docs = slots_ref.shape[0]
    tile, width = out_ref.shape
    ends = [ends_ref[d] for d in range(docs)]

    @pl.when(pl.program_id(0) == 0)
    def _():
        copies = load_all(array_refs, held_refs, sem)
        count = at_ref.shape[1]
        span = up_refs[0].shape[0] // count
        for i in range(2):
            for j in range(count):
                start = pl.multiple_of(at_ref[i, j], span)
                copies.append(
                    pltpu.make_async_copy(
                        up_refs[i].at[pl.ds(j * span, span), :],
                        up_ref.at[pl.ds(start, span), :],
                        sem.at[arrays + i * count + j],
                    )
                )
                copies[-1].start()
        for copy in copies:
            copy.wait()
        slots = [slots_ref[d] for d in range(docs)]
        for i, (first, part) in enumerate(parts):
            lay_slabs(rank, part, slots, first, held_refs, rhs_refs[i])

    acc = lax.dot_general(
        token_refs[0][...], rhs_refs[0][...], nt, preferred_element_type=jnp.float32
    )
    acc += lax.dot_general(
        token_refs[1][...], rhs_refs[1][...], nt, preferred_element_type=jnp.float32
    )
    mid = by_document(acc, ends, tile, rank) + mid_refs[0][...] + mid_refs[1][...]
    flat = up_ref.shape[1]
    row = pl.program_id(0) * tile + lax.broadcasted_iota(jnp.int32, (tile, flat), 0)
    slot, low = jnp.zeros((tile, flat), jnp.int32), 0
    for d, end in enumerate(ends):
        slot = jnp.where((row >= low) & (row < end), slots_ref[d], slot)
        low = end
    adapter = lax.broadcasted_iota(jnp.int32, (tile, flat), 1) // rank
    spread = jnp.where(slot == adapter, jnp.concatenate([mid] * (flat // rank), 1), 0.0)
    spread = spread.astype(jnp.bfloat16)
    columns = sum_refs[1].shape[1]
    for n in range(0, width, columns):
        cols = slice(n, n + columns)
        delta = lax.dot_general(spread, up_ref[cols, :], nt, preferred_element_type=jnp.float32)
        base = sum_refs[0][:, cols] + sum_refs[1 + n // columns][...]
        out_ref[:, cols] = (base + adapter_scale * delta).astype(out_ref.dtype)


def last_values(sums, mids, tokens, ups, up_at, arrays, parts, slots, ends):
    rows, width = sums[0].shape
    rank = mids[0].shape[1]
    flat = ups[0].shape[1]
    tile = rows_tile(rows)
    docs = slots.shape[0]
    return pl.pallas_call(
        functools.partial(last_kernel, rank, parts, len(sums), len(arrays)),
        out_shape=jax.ShapeDtypeStruct((rows, width), jnp.bfloat16),
        grid_spec=pltpu.PrefetchScalarGridSpec(
            num_scalar_prefetch=3,
            grid=(rows // tile,),
            in_specs=[tiled(a, tile) for a in (*sums, *mids, *tokens)]
            + [pl.BlockSpec(memory_space=pltpu.HBM)] * (2 + len(arrays)),
            out_specs=pl.BlockSpec((tile, width), lambda i, *_: (i, 0)),
            scratch_shapes=[pltpu.VMEM(a.shape, a.dtype) for a in arrays]
            + [pltpu.VMEM((docs * rank, tokens[0].shape[1]), jnp.bfloat16)] * 2
            + [pltpu.VMEM((width, flat), jnp.bfloat16)]
            + [pltpu.SemaphoreType.DMA((len(arrays) + up_at.size,))],
        ),
        compiler_params=pltpu.CompilerParams(vmem_limit_bytes=34 << 20),
        cost_estimate=light,
    )(slots, ends, up_at, *sums, *mids, *tokens, *ups, *arrays)


def after(value, *earlier):
    return lax.optimization_barrier((value, *earlier))[0]


def make(groups, store):
    depth = store // (rows_y * cores)

    def index(z, y, c):
        return (z * rows_y + y) * cores + c

    def pairs(move):
        return [
            (index(z, y, c), index(*move(z, y, c)))
            for z in range(depth)
            for y in range(rows_y)
            for c in range(cores)
        ]

    def along_z(value, k):
        return lax.ppermute(value, "store", pairs(lambda z, y, c: ((z + k) % depth, y, c)))

    def along_y(value):
        return lax.ppermute(value, "store", pairs(lambda z, y, c: (z, 1 - y, c)))

    def across(value):
        return lax.ppermute(value, "store", pairs(lambda z, y, c: (z, y, 1 - c)))

    def along_x(value):
        return lax.ppermute(value, "groups", [(g, g ^ 1) for g in range(groups)])

    class Line:
        def __init__(self, send, most=2):
            self.send, self.most, self.sent = send, most, []

        def __call__(self, value, *args):
            if len(self.sent) >= self.most:
                value = after(value, self.sent[-self.most])
            self.sent.append(self.send(value, *args))
            return self.sent[-1]

    def per_device(
        tokens,
        input_norm_gain,
        value_matrix,
        adapter_down_factors,
        adapter_up_factors,
        document_lengths,
        document_tenant,
        tenant_adapter_slot,
    ):
        shard, adapters, rank = adapter_down_factors.shape
        flat = adapters * rank
        width = value_matrix.shape[1]
        half, part = shard // 2, 3 * shard // 8
        me = lax.axis_index("store")
        side = lax.axis_index("groups") % 2
        mz, my, mc = me // (rows_y * cores), (me // cores) % rows_y, me % cores
        take = lax.dynamic_slice_in_dim

        down = adapter_down_factors.reshape(shard, flat).T
        up = adapter_up_factors.reshape(flat, -1).T
        bit = up.shape[0] // 2
        cut = part + bit
        rest = half - part
        plan = (
            (0, 0, 0, part, 0, half, 0),
            (1, 0, 0, bit, 0, bit, part),
            (0, 0, 0, rest, part, half + part, cut),
            (0, 0, 0, rest, half + part, part, cut + rest),
            (0, 1, 0, part, half, 0, 0),
            (1, 1, 0, bit, bit, 0, part),
            (2, 2, 1, half, 0, half, 0),
            (2, 3, 1, half, half, 0, 0),
        )
        shapes = [(cut + 2 * rest, width), (cut, width), (flat, half), (flat, half)]
        v_first, v_second, d_first, d_rest = cut_shards(
            [value_matrix, up, down], shapes, plan, side
        )
        v_have, v_miss, d_have = {(0, 0): v_first}, {(0, 0): (v_second, 0)}, {(0, 0): d_first}

        ends = jnp.cumsum(document_lengths, axis=1).astype(jnp.int32)
        slots = jnp.sum(
            (document_tenant[0][:, None] == jnp.arange(adapters, dtype=jnp.int32)[None, :])
            * tenant_adapter_slot[None, :],
            axis=1,
        ).astype(jnp.int32)[None, :]
        near = jnp.concatenate([ends, slots], 0)
        far = across(near)
        ends_both = jnp.concatenate([ends, far[:1]], 0)
        slots_both = jnp.concatenate([slots, far[1:]], 0)
        slots_there = along_x(slots_both)
        d_miss = {(0, 0): (pick_adapters([d_rest], slots_both, rank), 0)}
        chosen = slots_both.size * rank

        order = list(range(depth))
        names = [(k, dy) for k in order for dy in range(rows_y)]
        z, y, x = Line(along_z, 3), Line(along_y, 3), Line(along_x, 3)

        def x_values(names, *earlier):
            got = x(after(jnp.concatenate([v_have[name][:cut] for name in names], 0), *earlier))
            for i, name in enumerate(names):
                v_miss[name] = (got, i * cut)

        def x_down(names, *earlier):
            pieces = [d_have[name] for name in names]
            pieces[0] = after(pieces[0], *earlier)
            got = x(pick_adapters(pieces, slots_there, rank))
            for i, name in enumerate(names):
                d_miss[name] = (got, i * slots_both.size * rank)

        source, up_at = [], []
        for lane_at in (mc, 1 - mc):
            for k, dy in names:
                s = index((mz - k) % depth, my ^ dy, lane_at)
                for c in range(shard // lane):
                    piece = c * lane + jnp.where(c * lane < half, 1, -1) * side * half
                    source.append(s * shard + piece)
                up_at += [(2 * s + side) * bit, (2 * s + 1 - side) * bit]
        source = jnp.stack(source).astype(jnp.int32)
        up_at = jnp.stack(up_at).astype(jnp.int32).reshape(2, -1)
        first, second = names[: len(names) // 2], names[len(names) // 2 :]
        span = len(first) * shard

        def lay():
            arrays = []

            def place(array):
                for i, known in enumerate(arrays):
                    if known is array:
                        return i
                arrays.append(array)
                return len(arrays) - 1

            return arrays, place

        def values(names):
            arrays, place = lay()
            plan = []
            for i, name in enumerate(names):
                h, (m, row) = place(v_have[name]), v_miss[name]
                m, at = place(m), i * shard
                plan += [
                    (h, 0, part, at),
                    (h, cut, cut + half - part, at + part),
                    (m, row, row + part, at + half),
                    (h, cut + half - part, cut + 2 * (half - part), at + half + part),
                ]
            return arrays, tuple(plan)

        def ups(names):
            arrays, place = lay()
            plan = []
            for i, name in enumerate(names):
                h, (m, row) = place(v_have[name]), v_miss[name]
                plan.append((h, part, cut, 2 * i * bit))
                plan.append((place(m), row + part, row + cut, (2 * i + 1) * bit))
            return gather_rows(arrays, tuple(plan))

        def slabs(place, names, have, miss):
            out = []
            for i, name in enumerate(names):
                m, row = miss[name]
                out.append((i * shard, place(have[name]), place(m), row))
            return tuple(out)

        ks = order[1:]
        early, last = ks[:-1], ks[-1]
        own, own_rest, other, other_rest = norm_in_order(
            tokens, input_norm_gain, source, [span] * 4
        )
        partner, partner_rest = across(other), across(other_rest)
        for k in ks:
            v_have[k, 0] = z(v_have[0, 0], k)
        for k in ks:
            d_have[k, 0] = z(d_have[0, 0], k)
        v_have[0, 1] = y(v_have[0, 0])
        d_have[0, 1] = y(d_have[0, 0])
        x_values([(0, 1)], slots_there)
        x_down([(0, 1)])
        for i, k in enumerate(early):
            pins = [partner, partner_rest][: i + 1] + [d_miss[0, 1][0]] * i
            v_have[k, 1] = y(after(v_have[k, 0], *pins))
            x_values([(k, 0)])
        for k in early:
            x_values([(k, 1)])
        v_have[last, 1] = y(v_have[last, 0])
        x_values([(last, 0)])
        for k in early:
            d_have[k, 1] = y(d_have[k, 0])
        arrays, plan = values(first)
        sums = value_sums(
            after(own, v_have[last, 1], *[d_have[k, 0] for k in early], d_have[early[0], 1]), partner, arrays, plan, width
        )
        x_values([(last, 1)], sums[0])
        for k in early:
            x_down([(k, 0)])
        for k in early:
            x_down([(k, 1)])
        d_have[last, 1] = y(d_have[last, 0])
        x_down([(last, 0)])

        arrays, plan = values(second)
        ready = [d_have[last, 1], d_miss[last, 0][0]]
        sum_own, *sum_far = value_sums(
            after(own_rest, *ready), partner_rest, arrays, plan, width, sums, jnp.bfloat16
        )
        sums = (sum_own, *[across(part) for part in sum_far])
        up_lane = ups(names)
        up_both = (up_lane, across(up_lane))

        arrays, place = lay()
        parts = slabs(place, first, d_have, d_miss)
        mid_own, mid_far = mid_partials(own, partner, arrays, parts, ends_both, slots_both, rank)
        mids = (mid_own, across(mid_far))
        x_down([(last, 1)], mids[1], up_both[1])

        arrays, place = lay()
        parts = [(0, slabs(place, second, d_have, d_miss))]
        done = d_have[last, 1]
        far_have = {n: across(after(d_have[n], done)) for n in second}
        far_miss = {n: (across(after(d_miss[n][0], done)), d_miss[n][1]) for n in second}
        parts.append((slots.shape[1], slabs(place, second, far_have, far_miss)))
        return last_values(
            sums,
            mids,
            (own_rest, other_rest),
            up_both,
            up_at,
            arrays,
            tuple(parts),
            slots[0],
            ends[0],
        )

    return per_device


def solution(mesh):
    in_specs = (
        P(("groups", "store"), None),
        P(),
        P("store", None),
        P("store", None, None),
        P(None, None, "store"),
        P(("groups", "store"), None),
        P(("groups", "store"), None),
        P(),
    )
    out_specs = P(("groups", "store"), None)
    groups, store = mesh.shape["groups"], mesh.shape["store"]

    def run(*args):
        shard = args[2].shape[0]
        cut = shard % (4 * lane) == 0 and args[4].shape[2] % 32 == 0 and store > 4 and store % (rows_y * cores) == 0 and groups % 2 == 0
        return (make(groups, store) if cut else plain)(*args)

    return jax.shard_map(
        run, mesh=mesh, in_specs=in_specs, out_specs=out_specs, check_vma=False
    )
```

```python
import functools

import jax
import jax.numpy as jnp
from jax import lax
from jax.experimental import pallas as pl
from jax.experimental.pallas import tpu as pltpu
from jax.sharding import PartitionSpec as P

adapter_scale = 2.0
cores, rows_y, lane = 2, 2, 128
nt = (((1,), (1,)), ((), ()))
light = pl.CostEstimate(flops=0, bytes_accessed=0, transcendentals=0)


def token_slots(lengths, tenants, tenant_adapter_slot, row_count):
    ends = jnp.cumsum(lengths)
    position = jnp.arange(row_count, dtype=jnp.int32)
    doc_index = jnp.sum((position[:, None] >= ends[None, :]).astype(jnp.int32), axis=1)
    doc_pick = (
        doc_index[:, None] == jnp.arange(lengths.shape[0], dtype=jnp.int32)[None, :]
    ).astype(jnp.int32)
    tenant = jnp.sum(doc_pick * tenants[None, :], axis=1)
    tenant_pick = (
        tenant[:, None] == jnp.arange(tenant_adapter_slot.shape[0], dtype=jnp.int32)[None, :]
    ).astype(jnp.int32)
    return jnp.sum(tenant_pick * tenant_adapter_slot[None, :], axis=1)


def pick_rank(rank_total_rows, slots, count_of_adapters, rank_span_width):
    select = (slots[:, None] == jnp.arange(count_of_adapters, dtype=jnp.int32)[None, :]).astype(
        jnp.float32
    )
    shaped = rank_total_rows.reshape(slots.shape[0], count_of_adapters, rank_span_width)
    return jnp.sum(shaped * select[:, :, None], axis=1)


def plain(
    tokens,
    input_norm_gain,
    value_matrix,
    adapter_down_factors,
    adapter_up_factors,
    document_lengths,
    document_tenant,
    tenant_adapter_slot,
):
    row_count = tokens.shape[0]
    count_of_adapters = adapter_down_factors.shape[1]
    rank_span_width = adapter_down_factors.shape[2]
    flat_width = count_of_adapters * rank_span_width
    wide = tokens.astype(jnp.float32)
    meansq = jnp.mean(wide * wide, axis=1, keepdims=True)
    normed = (wide * lax.rsqrt(meansq + 1e-05) * input_norm_gain.astype(jnp.float32)).astype(
        jnp.bfloat16
    )
    slots = token_slots(document_lengths[0], document_tenant[0], tenant_adapter_slot, row_count)
    base_output = jnp.dot(
        normed,
        lax.all_gather(value_matrix, "store", axis=0, tiled=True),
        preferred_element_type=jnp.float32,
    )
    down = lax.all_gather(adapter_down_factors, "store", axis=0, tiled=True)
    rank_total_rows = jnp.dot(
        normed, down.reshape(down.shape[0], flat_width), preferred_element_type=jnp.float32
    )
    mid = pick_rank(rank_total_rows, slots, count_of_adapters, rank_span_width)
    mid = mid.astype(jnp.bfloat16)
    select = (slots[:, None] == jnp.arange(count_of_adapters, dtype=jnp.int32)[None, :]).astype(
        jnp.bfloat16
    )
    expanded_rows = (mid[:, None, :] * select[:, :, None]).reshape(row_count, flat_width)
    up = lax.all_gather(adapter_up_factors, "store", axis=2, tiled=True)
    adapter_update = jnp.dot(
        expanded_rows, up.reshape(flat_width, up.shape[2]), preferred_element_type=jnp.float32
    )
    return (base_output + adapter_scale * adapter_update).astype(jnp.bfloat16)


def norm_kernel(source_ref, tokens_ref, gain_ref, *out_refs):
    width = tokens_ref.shape[1]
    total = jnp.zeros((tokens_ref.shape[0], lane), jnp.float32)
    for i in range(width // lane):
        part = tokens_ref[:, i * lane : (i + 1) * lane].astype(jnp.float32)
        total += part * part
    scale = lax.rsqrt(jnp.sum(total, axis=1, keepdims=True) / width + 1e-05)
    first = 0
    for out_ref in out_refs:
        for i in range(out_ref.shape[1] // lane):
            start = pl.multiple_of(source_ref[first + i], lane)
            part = tokens_ref[:, pl.ds(start, lane)].astype(jnp.float32)
            gain = gain_ref[:, pl.ds(start, lane)].astype(jnp.float32)
            out_ref[:, i * lane : (i + 1) * lane] = (part * scale * gain).astype(jnp.bfloat16)
        first += out_ref.shape[1] // lane


def norm_in_order(tokens, gain, source, widths):
    rows, width = tokens.shape
    block = 128
    return pl.pallas_call(
        norm_kernel,
        out_shape=[jax.ShapeDtypeStruct((rows, w), jnp.bfloat16) for w in widths],
        grid_spec=pltpu.PrefetchScalarGridSpec(
            num_scalar_prefetch=1,
            grid=(rows // block,),
            in_specs=[
                pl.BlockSpec((block, width), lambda i, *_: (i, 0)),
                pl.BlockSpec((1, width), lambda i, *_: (0, 0)),
            ],
            out_specs=[pl.BlockSpec((block, w), lambda i, *_: (i, 0)) for w in widths],
        ),
        compiler_params=pltpu.CompilerParams(vmem_limit_bytes=12 << 20),
        cost_estimate=light,
    )(source, tokens, gain.reshape(1, width))


def far_memory():
    return pl.BlockSpec(memory_space=pl.ANY)


def tiled(array, tile):
    return pl.BlockSpec((tile,) + array.shape[1:], lambda i, *_: (i, 0))


def rows_tile(rows):
    return 256 if rows % 256 == 0 else rows


def pick_kernel(rank, slots_ref, *refs):
    piece_refs, out_ref = refs[:-1], refs[-1]
    sides, docs = slots_ref.shape
    at = 0
    for piece in piece_refs:
        for i in range(sides * docs):
            start = pl.multiple_of(slots_ref[i // docs, i % docs] * rank, rank)
            out_ref[at : at + rank, :] = piece[pl.ds(start, rank), :]
            at += rank


def pick_adapters(pieces, slots, rank):
    count = slots.shape[0] * slots.shape[1] * len(pieces)
    columns = pieces[0].shape[1]
    whole = [pl.BlockSpec(p.shape, lambda i, *_: (0, 0)) for p in pieces]
    return pl.pallas_call(
        functools.partial(pick_kernel, rank),
        out_shape=jax.ShapeDtypeStruct((count * rank, columns), jnp.bfloat16),
        grid_spec=pltpu.PrefetchScalarGridSpec(
            num_scalar_prefetch=1,
            grid=(1,),
            in_specs=whole,
            out_specs=pl.BlockSpec((count * rank, columns), lambda i, *_: (0, 0)),
        ),
        compiler_params=pltpu.CompilerParams(vmem_limit_bytes=12 << 20),
        cost_estimate=light,
    )(slots, *pieces)


def value_kernel(plan, columns, has_sum, arrays, *refs):
    own_ref, far_ref, refs = refs[0], refs[1], refs[2:]
    sum_refs, refs = refs[:has_sum], refs[has_sum:]
    array_refs, out_refs, held_ref, sem = refs[:arrays], refs[arrays:-2], refs[-2], refs[-1]

    @pl.when(pl.program_id(0) == 0)
    def _():
        copies = [
            pltpu.make_async_copy(
                array_refs[i].at[a:b, :], held_ref.at[row : row + b - a, :], sem.at[j]
            )
            for j, (i, a, b, row) in enumerate(plan)
        ]
        for copy in copies:
            copy.start()
        for copy in copies:
            copy.wait()

    tile = own_ref.shape[0]
    both = jnp.concatenate([own_ref[...], far_ref[...]], 0)
    for n in range(0, held_ref.shape[1], columns):
        cols = slice(n, n + columns)
        acc = jnp.dot(both, held_ref[:, cols], preferred_element_type=jnp.float32)
        terms = [acc[:tile], acc[tile:]]
        if has_sum:
            terms[0] += sum_refs[0][:, cols]
            terms[1] += sum_refs[1 + n // columns][...]
        out_refs[0][:, cols] = terms[0]
        out_refs[1 + n // columns][...] = terms[1].astype(out_refs[1].dtype)


def value_sums(own, far, arrays, plan, width, sums=(), far_type=jnp.float32):
    rows, depth = own.shape
    tile, columns = rows_tile(rows), 256
    outs = [jax.ShapeDtypeStruct((rows, width), jnp.float32)]
    outs += [jax.ShapeDtypeStruct((rows, columns), far_type)] * (width // columns)
    return pl.pallas_call(
        functools.partial(value_kernel, plan, columns, len(sums), len(arrays)),
        out_shape=outs,
        grid=(rows // tile,),
        in_specs=[tiled(b, tile) for b in (own, far, *sums)] + [far_memory()] * len(arrays),
        out_specs=[tiled(o, tile) for o in outs],
        scratch_shapes=[
            pltpu.VMEM((depth, width), jnp.bfloat16),
            pltpu.SemaphoreType.DMA((len(plan),)),
        ],
        compiler_params=pltpu.CompilerParams(vmem_limit_bytes=14 << 20),
        cost_estimate=light,
    )(own, far, *sums, *arrays)


def cut_kernel(plan, side_ref, *refs):
    arrays = 1 + max(p[0] for p in plan)
    array_refs, out_refs, sem = refs[:arrays], refs[arrays:-1], refs[-1]
    copies = []
    for j, (i, o, axis, length, even, odd, at) in enumerate(plan):
        start = pl.multiple_of(even + side_ref[0] * (odd - even), 16 if axis == 0 else lane)
        src, dst = [slice(None)] * 2, [slice(None)] * 2
        src[axis], dst[axis] = pl.ds(start, length), slice(at, at + length)
        copies.append(
            pltpu.make_async_copy(
                array_refs[i].at[tuple(src)], out_refs[o].at[tuple(dst)], sem.at[j]
            )
        )
        copies[-1].start()
    for copy in copies:
        copy.wait()


def cut_shards(arrays, shapes, plan, side):
    return pl.pallas_call(
        functools.partial(cut_kernel, plan),
        out_shape=[jax.ShapeDtypeStruct(s, jnp.bfloat16) for s in shapes],
        grid_spec=pltpu.PrefetchScalarGridSpec(
            num_scalar_prefetch=1,
            in_specs=[far_memory()] * len(arrays),
            out_specs=[pl.BlockSpec(memory_space=pltpu.VMEM)] * len(shapes),
            scratch_shapes=[pltpu.SemaphoreType.DMA((len(plan),))],
        ),
        compiler_params=pltpu.CompilerParams(vmem_limit_bytes=12 << 20),
        cost_estimate=light,
    )(side.reshape(1).astype(jnp.int32), *arrays)


def gather_kernel(plan, *refs):
    array_refs, out_ref, sem = refs[:-2], refs[-2], refs[-1]
    copies = [
        pltpu.make_async_copy(array_refs[i].at[a:b, :], out_ref.at[row : row + b - a, :], sem.at[j])
        for j, (i, a, b, row) in enumerate(plan)
    ]
    for copy in copies:
        copy.start()
    for copy in copies:
        copy.wait()


def gather_rows(arrays, plan):
    rows = sum(b - a for _, a, b, _ in plan)
    return pl.pallas_call(
        functools.partial(gather_kernel, plan),
        out_shape=jax.ShapeDtypeStruct((rows, arrays[0].shape[1]), arrays[0].dtype),
        in_specs=[far_memory()] * len(arrays),
        out_specs=pl.BlockSpec(memory_space=pltpu.VMEM),
        scratch_shapes=[pltpu.SemaphoreType.DMA((len(plan),))],
        compiler_params=pltpu.CompilerParams(vmem_limit_bytes=12 << 20),
        cost_estimate=light,
    )(*arrays)


def load_all(array_refs, held_refs, sem, first=0):
    copies = [
        pltpu.make_async_copy(a, h, sem.at[first + i])
        for i, (a, h) in enumerate(zip(array_refs, held_refs))
    ]
    for copy in copies:
        copy.start()
    return copies


def lay_slabs(rank, parts, slots, first, held_refs, rhs_ref):
    for at, have, miss, row in parts:
        for d, slot in enumerate(slots):
            rows = slice(d * rank, (d + 1) * rank)
            start = pl.multiple_of(slot * rank, rank)
            half = held_refs[have].shape[1]
            rhs_ref[rows, at : at + half] = held_refs[have][pl.ds(start, rank), :]
            low = row + (first + d) * rank
            rhs_ref[rows, at + half : at + 2 * half] = held_refs[miss][low : low + rank, :]


def by_document(acc, ends, tile, rank):
    row = pl.program_id(0) * tile + lax.broadcasted_iota(jnp.int32, (tile, rank), 0)
    mid = jnp.zeros((tile, rank), jnp.float32)
    low = 0
    for doc, end in enumerate(ends):
        mid = jnp.where((row >= low) & (row < end), acc[:, doc * rank : (doc + 1) * rank], mid)
        low = end
    return mid


def mid_kernel(rank, parts, arrays, ends_ref, slots_ref, *refs):
    token_refs, array_refs, out_refs = refs[:2], refs[2 : 2 + arrays], refs[2 + arrays : 4 + arrays]
    held_refs, rhs_refs, sem = refs[4 + arrays : -3], refs[-3:-1], refs[-1]
    docs = slots_ref.shape[1]
    tile = out_refs[0].shape[0]

    @pl.when(pl.program_id(0) == 0)
    def _():
        for copy in load_all(array_refs, held_refs, sem):
            copy.wait()
        for side in range(2):
            slots = [slots_ref[side, d] for d in range(docs)]
            lay_slabs(rank, parts, slots, side * docs, held_refs, rhs_refs[side])

    for side in range(2):
        acc = lax.dot_general(
            token_refs[side][...], rhs_refs[side][...], nt, preferred_element_type=jnp.float32
        )
        ends = [ends_ref[side, d] for d in range(docs)]
        out_refs[side][...] = by_document(acc, ends, tile, rank)


def mid_partials(own, far, arrays, parts, ends, slots, rank):
    rows, depth = own.shape
    tile = rows_tile(rows)
    docs = slots.shape[1]
    out = jax.ShapeDtypeStruct((rows, rank), jnp.float32)
    return pl.pallas_call(
        functools.partial(mid_kernel, rank, parts, len(arrays)),
        out_shape=(out, out),
        grid_spec=pltpu.PrefetchScalarGridSpec(
            num_scalar_prefetch=2,
            grid=(rows // tile,),
            in_specs=[tiled(own, tile), tiled(far, tile)] + [far_memory()] * len(arrays),
            out_specs=[pl.BlockSpec((tile, rank), lambda i, *_: (i, 0))] * 2,
            scratch_shapes=[pltpu.VMEM(a.shape, a.dtype) for a in arrays]
            + [pltpu.VMEM((docs * rank, depth), jnp.bfloat16)] * 2
            + [pltpu.SemaphoreType.DMA((len(arrays),))],
        ),
        compiler_params=pltpu.CompilerParams(vmem_limit_bytes=12 << 20),
        cost_estimate=light,
    )(ends, slots, own, far, *arrays)


def last_kernel(rank, parts, sums, arrays, slots_ref, ends_ref, at_ref, *refs):
    sum_refs, refs = refs[:sums], refs[sums:]
    mid_refs, token_refs, refs = refs[:2], refs[2:4], refs[4:]
    up_refs, array_refs, out_ref = refs[:2], refs[2 : 2 + arrays], refs[2 + arrays]
    held_refs, rhs_refs, up_ref, sem = refs[3 + arrays : -4], refs[-4:-2], refs[-2], refs[-1]
    docs = slots_ref.shape[0]
    tile, width = out_ref.shape
    ends = [ends_ref[d] for d in range(docs)]

    @pl.when(pl.program_id(0) == 0)
    def _():
        copies = load_all(array_refs, held_refs, sem)
        count = at_ref.shape[1]
        span = up_refs[0].shape[0] // count
        for i in range(2):
            for j in range(count):
                start = pl.multiple_of(at_ref[i, j], span)
                copies.append(
                    pltpu.make_async_copy(
                        up_refs[i].at[pl.ds(j * span, span), :],
                        up_ref.at[pl.ds(start, span), :],
                        sem.at[arrays + i * count + j],
                    )
                )
                copies[-1].start()
        for copy in copies:
            copy.wait()
        slots = [slots_ref[d] for d in range(docs)]
        for i, (first, part) in enumerate(parts):
            lay_slabs(rank, part, slots, first, held_refs, rhs_refs[i])

    acc = lax.dot_general(
        token_refs[0][...], rhs_refs[0][...], nt, preferred_element_type=jnp.float32
    )
    acc += lax.dot_general(
        token_refs[1][...], rhs_refs[1][...], nt, preferred_element_type=jnp.float32
    )
    mid = by_document(acc, ends, tile, rank) + mid_refs[0][...] + mid_refs[1][...]
    flat = up_ref.shape[1]
    row = pl.program_id(0) * tile + lax.broadcasted_iota(jnp.int32, (tile, flat), 0)
    slot, low = jnp.zeros((tile, flat), jnp.int32), 0
    for d, end in enumerate(ends):
        slot = jnp.where((row >= low) & (row < end), slots_ref[d], slot)
        low = end
    adapter = lax.broadcasted_iota(jnp.int32, (tile, flat), 1) // rank
    spread = jnp.where(slot == adapter, jnp.concatenate([mid] * (flat // rank), 1), 0.0)
    spread = spread.astype(jnp.bfloat16)
    columns = sum_refs[1].shape[1]
    for n in range(0, width, columns):
        cols = slice(n, n + columns)
        delta = lax.dot_general(spread, up_ref[cols, :], nt, preferred_element_type=jnp.float32)
        base = sum_refs[0][:, cols] + sum_refs[1 + n // columns][...]
        out_ref[:, cols] = (base + adapter_scale * delta).astype(out_ref.dtype)


def last_values(sums, mids, tokens, ups, up_at, arrays, parts, slots, ends):
    rows, width = sums[0].shape
    rank = mids[0].shape[1]
    flat = ups[0].shape[1]
    tile = rows_tile(rows)
    docs = slots.shape[0]
    return pl.pallas_call(
        functools.partial(last_kernel, rank, parts, len(sums), len(arrays)),
        out_shape=jax.ShapeDtypeStruct((rows, width), jnp.bfloat16),
        grid_spec=pltpu.PrefetchScalarGridSpec(
            num_scalar_prefetch=3,
            grid=(rows // tile,),
            in_specs=[tiled(a, tile) for a in (*sums, *mids, *tokens)]
            + [far_memory()] * (2 + len(arrays)),
            out_specs=pl.BlockSpec((tile, width), lambda i, *_: (i, 0)),
            scratch_shapes=[pltpu.VMEM(a.shape, a.dtype) for a in arrays]
            + [pltpu.VMEM((docs * rank, tokens[0].shape[1]), jnp.bfloat16)] * 2
            + [pltpu.VMEM((width, flat), jnp.bfloat16)]
            + [pltpu.SemaphoreType.DMA((len(arrays) + up_at.size,))],
        ),
        compiler_params=pltpu.CompilerParams(vmem_limit_bytes=20 << 20),
        cost_estimate=light,
    )(slots, ends, up_at, *sums, *mids, *tokens, *ups, *arrays)


def after(value, *earlier):
    return lax.optimization_barrier((value, *earlier))[0]


def make(groups, store):
    depth = store // (rows_y * cores)

    def index(z, y, c):
        return (z * rows_y + y) * cores + c

    def pairs(move):
        return [
            (index(z, y, c), index(*move(z, y, c)))
            for z in range(depth)
            for y in range(rows_y)
            for c in range(cores)
        ]

    def along_z(value, k):
        return lax.ppermute(value, "store", pairs(lambda z, y, c: ((z + k) % depth, y, c)))

    def along_y(value):
        return lax.ppermute(value, "store", pairs(lambda z, y, c: (z, 1 - y, c)))

    def across(value):
        return lax.ppermute(value, "store", pairs(lambda z, y, c: (z, y, 1 - c)))

    def along_x(value):
        return lax.ppermute(value, "groups", [(g, g ^ 1) for g in range(groups)])

    class Line:
        def __init__(self, send, most=2):
            self.send, self.most, self.sent = send, most, []

        def __call__(self, value, *args):
            if len(self.sent) >= self.most:
                value = after(value, self.sent[-self.most])
            self.sent.append(self.send(value, *args))
            return self.sent[-1]

    def per_device(
        tokens,
        input_norm_gain,
        value_matrix,
        adapter_down_factors,
        adapter_up_factors,
        document_lengths,
        document_tenant,
        tenant_adapter_slot,
    ):
        shard, adapters, rank = adapter_down_factors.shape
        flat = adapters * rank
        width = value_matrix.shape[1]
        half, part = shard // 2, 3 * shard // 8
        me = lax.axis_index("store")
        side = lax.axis_index("groups") % 2
        mz, my, mc = me // (rows_y * cores), (me // cores) % rows_y, me % cores
        take = lax.dynamic_slice_in_dim

        down = adapter_down_factors.reshape(shard, flat).T
        up = adapter_up_factors.reshape(flat, -1).T
        bit = up.shape[0] // 2
        cut = part + bit
        rest = half - part
        plan = (
            (0, 0, 0, part, 0, half, 0),
            (1, 0, 0, bit, 0, bit, part),
            (0, 0, 0, rest, part, half + part, cut),
            (0, 0, 0, rest, half + part, part, cut + rest),
            (0, 1, 0, part, half, 0, 0),
            (1, 1, 0, bit, bit, 0, part),
            (2, 2, 1, half, 0, half, 0),
            (2, 3, 1, half, half, 0, 0),
        )
        shapes = [(cut + 2 * rest, width), (cut, width), (flat, half), (flat, half)]
        v_first, v_second, d_first, d_rest = cut_shards(
            [value_matrix, up, down], shapes, plan, side
        )
        v_have, v_miss, d_have = {(0, 0): v_first}, {(0, 0): (v_second, 0)}, {(0, 0): d_first}

        ends = jnp.cumsum(document_lengths, axis=1).astype(jnp.int32)
        slots = jnp.sum(
            (document_tenant[0][:, None] == jnp.arange(adapters, dtype=jnp.int32)[None, :])
            * tenant_adapter_slot[None, :],
            axis=1,
        ).astype(jnp.int32)[None, :]
        near = jnp.concatenate([ends, slots], 0)
        far = across(near)
        ends_both = jnp.concatenate([ends, far[:1]], 0)
        slots_both = jnp.concatenate([slots, far[1:]], 0)
        slots_there = along_x(slots_both)
        d_miss = {(0, 0): (pick_adapters([d_rest], slots_both, rank), 0)}
        chosen = slots_both.size * rank

        order = list(range(depth))
        names = [(k, dy) for k in order for dy in range(rows_y)]
        z, y, x = Line(along_z, 3), Line(along_y, 3), Line(along_x, 3)

        def x_values(names, *earlier):
            got = x(after(jnp.concatenate([v_have[name][:cut] for name in names], 0), *earlier))
            for i, name in enumerate(names):
                v_miss[name] = (got, i * cut)

        def x_down(names, *earlier):
            pieces = [d_have[name] for name in names]
            pieces[0] = after(pieces[0], *earlier)
            got = x(pick_adapters(pieces, slots_there, rank))
            for i, name in enumerate(names):
                d_miss[name] = (got, i * slots_both.size * rank)

        source, up_at = [], []
        for lane_at in (mc, 1 - mc):
            for k, dy in names:
                s = index((mz - k) % depth, my ^ dy, lane_at)
                for c in range(shard // lane):
                    piece = c * lane + jnp.where(c * lane < half, 1, -1) * side * half
                    source.append(s * shard + piece)
                up_at += [(2 * s + side) * bit, (2 * s + 1 - side) * bit]
        source = jnp.stack(source).astype(jnp.int32)
        up_at = jnp.stack(up_at).astype(jnp.int32).reshape(2, -1)
        first, second = names[: len(names) // 2], names[len(names) // 2 :]
        span = len(first) * shard

        def lay():
            arrays = []

            def place(array):
                for i, known in enumerate(arrays):
                    if known is array:
                        return i
                arrays.append(array)
                return len(arrays) - 1

            return arrays, place

        def values(names):
            arrays, place = lay()
            plan = []
            for i, name in enumerate(names):
                h, (m, row) = place(v_have[name]), v_miss[name]
                m, at = place(m), i * shard
                plan += [
                    (h, 0, part, at),
                    (h, cut, cut + half - part, at + part),
                    (m, row, row + part, at + half),
                    (h, cut + half - part, cut + 2 * (half - part), at + half + part),
                ]
            return arrays, tuple(plan)

        def ups(names):
            arrays, place = lay()
            plan = []
            for i, name in enumerate(names):
                h, (m, row) = place(v_have[name]), v_miss[name]
                plan.append((h, part, cut, 2 * i * bit))
                plan.append((place(m), row + part, row + cut, (2 * i + 1) * bit))
            return gather_rows(arrays, tuple(plan))

        def slabs(place, names, have, miss):
            out = []
            for i, name in enumerate(names):
                m, row = miss[name]
                out.append((i * shard, place(have[name]), place(m), row))
            return tuple(out)

        ks = order[1:]
        early, last = ks[:-1], ks[-1]
        own, own_rest, other, other_rest = norm_in_order(
            tokens, input_norm_gain, source, [span] * 4
        )
        partner = across(other)
        for k in ks:
            v_have[k, 0] = z(v_have[0, 0], k)
        for k in ks:
            d_have[k, 0] = z(d_have[0, 0], k)
        v_have[0, 1] = y(v_have[0, 0])
        d_have[0, 1] = y(d_have[0, 0])
        x_values([(0, 1)], slots_there)
        x_down([(0, 1)])
        for i, k in enumerate(early):
            pins = [partner] + [d_miss[0, 1][0]] * i
            v_have[k, 1] = y(after(v_have[k, 0], *pins))
            x_values([(k, 0)])
        for k in early:
            x_values([(k, 1)])
        v_have[last, 1] = y(v_have[last, 0])
        x_values([(last, 0)])
        for k in early:
            d_have[k, 1] = y(d_have[k, 0])
        arrays, plan = values(first)
        sums = value_sums(
            after(own, v_have[last, 1], d_have[last, 0], d_have[early[0], 1]), partner, arrays, plan, width
        )
        x_values([(last, 1)])
        for k in early:
            x_down([(k, 0)])
        for k in early:
            x_down([(k, 1)])
        d_have[last, 1] = y(d_have[last, 0])
        x_down([(last, 0)], sums[0])

        partner_rest = across(after(other_rest, v_have[last, 1]))
        arrays, plan = values(second)
        ready = [d_have[last, 1], d_miss[early[-1], 1][0]]
        sum_own, *sum_far = value_sums(
            after(own_rest, *ready), partner_rest, arrays, plan, width, sums, jnp.bfloat16
        )
        sums = (sum_own, *[across(part) for part in sum_far])
        v_have[0, 0] = after(v_have[0, 0], d_miss[early[-1], 1][0])
        up_lane = ups(names)
        up_both = (up_lane, across(up_lane))

        arrays, place = lay()
        parts = slabs(place, first, d_have, d_miss)
        mid_own, mid_far = mid_partials(own, partner, arrays, parts, ends_both, slots_both, rank)
        mids = (mid_own, across(mid_far))
        x_down([(last, 1)], mids[1])

        arrays, place = lay()
        parts = [(0, slabs(place, second, d_have, d_miss))]
        done = d_have[last, 1]
        far_have = {n: across(after(d_have[n], done)) for n in second}
        far_miss = {n: (across(after(d_miss[n][0], done)), d_miss[n][1]) for n in second}
        parts.append((slots.shape[1], slabs(place, second, far_have, far_miss)))
        return last_values(
            sums,
            mids,
            (own_rest, other_rest),
            up_both,
            up_at,
            arrays,
            tuple(parts),
            slots[0],
            ends[0],
        )

    return per_device


def solution(mesh):
    in_specs = (
        P(("groups", "store"), None),
        P(),
        P("store", None),
        P("store", None, None),
        P(None, None, "store"),
        P(("groups", "store"), None),
        P(("groups", "store"), None),
        P(),
    )
    out_specs = P(("groups", "store"), None)
    groups, store = mesh.shape["groups"], mesh.shape["store"]

    def run(*args):
        shard = args[2].shape[0]
        cut = shard % (4 * lane) == 0 and args[4].shape[2] % 32 == 0 and store > 4 and store % (rows_y * cores) == 0 and groups % 2 == 0
        return (make(groups, store) if cut else plain)(*args)

    return jax.shard_map(
        run, mesh=mesh, in_specs=in_specs, out_specs=out_specs, check_vma=False
    )
```

```python
import functools

import jax
import jax.numpy as jnp
from jax import lax
from jax.experimental import pallas as pl
from jax.experimental.pallas import tpu as pltpu
from jax.sharding import PartitionSpec as P

adapter_scale = 2.0
cores, rows_y, lane = 2, 2, 128
nt = (((1,), (1,)), ((), ()))
light = pl.CostEstimate(flops=0, bytes_accessed=0, transcendentals=0)


def token_slots(lengths, tenants, tenant_adapter_slot, row_count):
    ends = jnp.cumsum(lengths)
    position = jnp.arange(row_count, dtype=jnp.int32)
    doc_index = jnp.sum((position[:, None] >= ends[None, :]).astype(jnp.int32), axis=1)
    doc_pick = (
        doc_index[:, None] == jnp.arange(lengths.shape[0], dtype=jnp.int32)[None, :]
    ).astype(jnp.int32)
    tenant = jnp.sum(doc_pick * tenants[None, :], axis=1)
    tenant_pick = (
        tenant[:, None] == jnp.arange(tenant_adapter_slot.shape[0], dtype=jnp.int32)[None, :]
    ).astype(jnp.int32)
    return jnp.sum(tenant_pick * tenant_adapter_slot[None, :], axis=1)


def pick_rank(rank_total_rows, slots, count_of_adapters, rank_span_width):
    select = (slots[:, None] == jnp.arange(count_of_adapters, dtype=jnp.int32)[None, :]).astype(
        jnp.float32
    )
    shaped = rank_total_rows.reshape(slots.shape[0], count_of_adapters, rank_span_width)
    return jnp.sum(shaped * select[:, :, None], axis=1)


def plain(
    tokens,
    input_norm_gain,
    value_matrix,
    adapter_down_factors,
    adapter_up_factors,
    document_lengths,
    document_tenant,
    tenant_adapter_slot,
):
    row_count = tokens.shape[0]
    count_of_adapters = adapter_down_factors.shape[1]
    rank_span_width = adapter_down_factors.shape[2]
    flat_width = count_of_adapters * rank_span_width
    wide = tokens.astype(jnp.float32)
    meansq = jnp.mean(wide * wide, axis=1, keepdims=True)
    normed = (wide * lax.rsqrt(meansq + 1e-05) * input_norm_gain.astype(jnp.float32)).astype(
        jnp.bfloat16
    )
    slots = token_slots(document_lengths[0], document_tenant[0], tenant_adapter_slot, row_count)
    base_output = jnp.dot(
        normed,
        lax.all_gather(value_matrix, "store", axis=0, tiled=True),
        preferred_element_type=jnp.float32,
    )
    down = lax.all_gather(adapter_down_factors, "store", axis=0, tiled=True)
    rank_total_rows = jnp.dot(
        normed, down.reshape(down.shape[0], flat_width), preferred_element_type=jnp.float32
    )
    mid = pick_rank(rank_total_rows, slots, count_of_adapters, rank_span_width)
    mid = mid.astype(jnp.bfloat16)
    select = (slots[:, None] == jnp.arange(count_of_adapters, dtype=jnp.int32)[None, :]).astype(
        jnp.bfloat16
    )
    expanded_rows = (mid[:, None, :] * select[:, :, None]).reshape(row_count, flat_width)
    up = lax.all_gather(adapter_up_factors, "store", axis=2, tiled=True)
    adapter_update = jnp.dot(
        expanded_rows, up.reshape(flat_width, up.shape[2]), preferred_element_type=jnp.float32
    )
    return (base_output + adapter_scale * adapter_update).astype(jnp.bfloat16)


def norm_kernel(source_ref, tokens_ref, gain_ref, *out_refs):
    width = tokens_ref.shape[1]
    total = jnp.zeros((tokens_ref.shape[0], lane), jnp.float32)
    for i in range(width // lane):
        part = tokens_ref[:, i * lane : (i + 1) * lane].astype(jnp.float32)
        total += part * part
    scale = lax.rsqrt(jnp.sum(total, axis=1, keepdims=True) / width + 1e-05)
    first = 0
    for out_ref in out_refs:
        for i in range(out_ref.shape[1] // lane):
            start = pl.multiple_of(source_ref[first + i], lane)
            part = tokens_ref[:, pl.ds(start, lane)].astype(jnp.float32)
            gain = gain_ref[:, pl.ds(start, lane)].astype(jnp.float32)
            out_ref[:, i * lane : (i + 1) * lane] = (part * scale * gain).astype(jnp.bfloat16)
        first += out_ref.shape[1] // lane


def norm_in_order(tokens, gain, source, widths):
    rows, width = tokens.shape
    block = 128
    return pl.pallas_call(
        norm_kernel,
        out_shape=[jax.ShapeDtypeStruct((rows, w), jnp.bfloat16) for w in widths],
        grid_spec=pltpu.PrefetchScalarGridSpec(
            num_scalar_prefetch=1,
            grid=(rows // block,),
            in_specs=[
                pl.BlockSpec((block, width), lambda i, *_: (i, 0)),
                pl.BlockSpec((1, width), lambda i, *_: (0, 0)),
            ],
            out_specs=[pl.BlockSpec((block, w), lambda i, *_: (i, 0)) for w in widths],
        ),
        compiler_params=pltpu.CompilerParams(vmem_limit_bytes=58 << 20),
        cost_estimate=light,
    )(source, tokens, gain.reshape(1, width))


def far_memory():
    return pl.BlockSpec(memory_space=pl.ANY)


def tiled(array, tile):
    return pl.BlockSpec((tile,) + array.shape[1:], lambda i, *_: (i, 0))


def rows_tile(rows):
    return 256 if rows % 256 == 0 else rows


def pick_kernel(rank, slots_ref, *refs):
    piece_refs, out_ref = refs[:-1], refs[-1]
    sides, docs = slots_ref.shape
    at = 0
    for piece in piece_refs:
        for i in range(sides * docs):
            start = pl.multiple_of(slots_ref[i // docs, i % docs] * rank, rank)
            out_ref[at : at + rank, :] = piece[pl.ds(start, rank), :]
            at += rank


def pick_adapters(pieces, slots, rank):
    count = slots.shape[0] * slots.shape[1] * len(pieces)
    columns = pieces[0].shape[1]
    whole = [pl.BlockSpec(p.shape, lambda i, *_: (0, 0)) for p in pieces]
    return pl.pallas_call(
        functools.partial(pick_kernel, rank),
        out_shape=jax.ShapeDtypeStruct((count * rank, columns), jnp.bfloat16),
        grid_spec=pltpu.PrefetchScalarGridSpec(
            num_scalar_prefetch=1,
            grid=(1,),
            in_specs=whole,
            out_specs=pl.BlockSpec((count * rank, columns), lambda i, *_: (0, 0)),
        ),
        compiler_params=pltpu.CompilerParams(vmem_limit_bytes=12 << 20),
        cost_estimate=light,
    )(slots, *pieces)


def value_kernel(plan, columns, has_sum, arrays, *refs):
    own_ref, far_ref, refs = refs[0], refs[1], refs[2:]
    sum_refs, refs = refs[:has_sum], refs[has_sum:]
    array_refs, out_refs, held_ref, sem = refs[:arrays], refs[arrays:-2], refs[-2], refs[-1]

    @pl.when(pl.program_id(0) == 0)
    def _():
        copies = [
            pltpu.make_async_copy(
                array_refs[i].at[a:b, :], held_ref.at[row : row + b - a, :], sem.at[j]
            )
            for j, (i, a, b, row) in enumerate(plan)
        ]
        for copy in copies:
            copy.start()
        for copy in copies:
            copy.wait()

    tile = own_ref.shape[0]
    both = jnp.concatenate([own_ref[...], far_ref[...]], 0)
    for n in range(0, held_ref.shape[1], columns):
        cols = slice(n, n + columns)
        acc = jnp.dot(both, held_ref[:, cols], preferred_element_type=jnp.float32)
        terms = [acc[:tile], acc[tile:]]
        if has_sum:
            terms[0] += sum_refs[0][:, cols]
            terms[1] += sum_refs[1 + n // columns][...]
        out_refs[0][:, cols] = terms[0]
        out_refs[1 + n // columns][...] = terms[1].astype(out_refs[1].dtype)


def value_sums(own, far, arrays, plan, width, sums=(), far_type=jnp.float32):
    rows, depth = own.shape
    tile, columns = rows_tile(rows), 256
    outs = [jax.ShapeDtypeStruct((rows, width), jnp.float32)]
    outs += [jax.ShapeDtypeStruct((rows, columns), far_type)] * (width // columns)
    return pl.pallas_call(
        functools.partial(value_kernel, plan, columns, len(sums), len(arrays)),
        out_shape=outs,
        grid=(rows // tile,),
        in_specs=[tiled(b, tile) for b in (own, far, *sums)] + [far_memory()] * len(arrays),
        out_specs=[tiled(o, tile) for o in outs],
        scratch_shapes=[
            pltpu.VMEM((depth, width), jnp.bfloat16),
            pltpu.SemaphoreType.DMA((len(plan),)),
        ],
        compiler_params=pltpu.CompilerParams(vmem_limit_bytes=14 << 20),
        cost_estimate=light,
    )(own, far, *sums, *arrays)


def cut_kernel(plan, side_ref, *refs):
    arrays = 1 + max(p[0] for p in plan)
    array_refs, out_refs, sem = refs[:arrays], refs[arrays:-1], refs[-1]
    copies = []
    for j, (i, o, axis, length, even, odd, at) in enumerate(plan):
        start = pl.multiple_of(even + side_ref[0] * (odd - even), 16 if axis == 0 else lane)
        src, dst = [slice(None)] * 2, [slice(None)] * 2
        src[axis], dst[axis] = pl.ds(start, length), slice(at, at + length)
        copies.append(
            pltpu.make_async_copy(
                array_refs[i].at[tuple(src)], out_refs[o].at[tuple(dst)], sem.at[j]
            )
        )
        copies[-1].start()
    for copy in copies:
        copy.wait()


def cut_shards(arrays, shapes, plan, side):
    return pl.pallas_call(
        functools.partial(cut_kernel, plan),
        out_shape=[jax.ShapeDtypeStruct(s, jnp.bfloat16) for s in shapes],
        grid_spec=pltpu.PrefetchScalarGridSpec(
            num_scalar_prefetch=1,
            in_specs=[far_memory()] * len(arrays),
            out_specs=[pl.BlockSpec(memory_space=pltpu.VMEM)] * len(shapes),
            scratch_shapes=[pltpu.SemaphoreType.DMA((len(plan),))],
        ),
        compiler_params=pltpu.CompilerParams(vmem_limit_bytes=58 << 20),
        cost_estimate=light,
    )(side.reshape(1).astype(jnp.int32), *arrays)


def gather_kernel(plan, *refs):
    array_refs, out_ref, sem = refs[:-2], refs[-2], refs[-1]
    copies = [
        pltpu.make_async_copy(array_refs[i].at[a:b, :], out_ref.at[row : row + b - a, :], sem.at[j])
        for j, (i, a, b, row) in enumerate(plan)
    ]
    for copy in copies:
        copy.start()
    for copy in copies:
        copy.wait()


def gather_rows(arrays, plan):
    rows = sum(b - a for _, a, b, _ in plan)
    return pl.pallas_call(
        functools.partial(gather_kernel, plan),
        out_shape=jax.ShapeDtypeStruct((rows, arrays[0].shape[1]), arrays[0].dtype),
        in_specs=[far_memory()] * len(arrays),
        out_specs=pl.BlockSpec(memory_space=pltpu.VMEM),
        scratch_shapes=[pltpu.SemaphoreType.DMA((len(plan),))],
        compiler_params=pltpu.CompilerParams(vmem_limit_bytes=12 << 20),
        cost_estimate=light,
    )(*arrays)


def load_all(array_refs, held_refs, sem, first=0):
    copies = [
        pltpu.make_async_copy(a, h, sem.at[first + i])
        for i, (a, h) in enumerate(zip(array_refs, held_refs))
    ]
    for copy in copies:
        copy.start()
    return copies


def lay_slabs(rank, parts, slots, first, held_refs, rhs_ref):
    for at, have, miss, row in parts:
        for d, slot in enumerate(slots):
            rows = slice(d * rank, (d + 1) * rank)
            start = pl.multiple_of(slot * rank, rank)
            half = held_refs[have].shape[1]
            rhs_ref[rows, at : at + half] = held_refs[have][pl.ds(start, rank), :]
            low = row + (first + d) * rank
            rhs_ref[rows, at + half : at + 2 * half] = held_refs[miss][low : low + rank, :]


def by_document(acc, ends, tile, rank):
    row = pl.program_id(0) * tile + lax.broadcasted_iota(jnp.int32, (tile, rank), 0)
    mid = jnp.zeros((tile, rank), jnp.float32)
    low = 0
    for doc, end in enumerate(ends):
        mid = jnp.where((row >= low) & (row < end), acc[:, doc * rank : (doc + 1) * rank], mid)
        low = end
    return mid


def mid_kernel(rank, parts, arrays, ends_ref, slots_ref, *refs):
    token_refs, array_refs, out_refs = refs[:2], refs[2 : 2 + arrays], refs[2 + arrays : 4 + arrays]
    held_refs, rhs_refs, sem = refs[4 + arrays : -3], refs[-3:-1], refs[-1]
    docs = slots_ref.shape[1]
    tile = out_refs[0].shape[0]

    @pl.when(pl.program_id(0) == 0)
    def _():
        for copy in load_all(array_refs, held_refs, sem):
            copy.wait()
        for side in range(2):
            slots = [slots_ref[side, d] for d in range(docs)]
            lay_slabs(rank, parts, slots, side * docs, held_refs, rhs_refs[side])

    for side in range(2):
        acc = lax.dot_general(
            token_refs[side][...], rhs_refs[side][...], nt, preferred_element_type=jnp.float32
        )
        ends = [ends_ref[side, d] for d in range(docs)]
        out_refs[side][...] = by_document(acc, ends, tile, rank)


def mid_partials(own, far, arrays, parts, ends, slots, rank):
    rows, depth = own.shape
    tile = rows_tile(rows)
    docs = slots.shape[1]
    out = jax.ShapeDtypeStruct((rows, rank), jnp.float32)
    return pl.pallas_call(
        functools.partial(mid_kernel, rank, parts, len(arrays)),
        out_shape=(out, out),
        grid_spec=pltpu.PrefetchScalarGridSpec(
            num_scalar_prefetch=2,
            grid=(rows // tile,),
            in_specs=[tiled(own, tile), tiled(far, tile)] + [far_memory()] * len(arrays),
            out_specs=[pl.BlockSpec((tile, rank), lambda i, *_: (i, 0))] * 2,
            scratch_shapes=[pltpu.VMEM(a.shape, a.dtype) for a in arrays]
            + [pltpu.VMEM((docs * rank, depth), jnp.bfloat16)] * 2
            + [pltpu.SemaphoreType.DMA((len(arrays),))],
        ),
        compiler_params=pltpu.CompilerParams(vmem_limit_bytes=12 << 20),
        cost_estimate=light,
    )(ends, slots, own, far, *arrays)


def last_kernel(rank, parts, sums, arrays, slots_ref, ends_ref, at_ref, *refs):
    sum_refs, refs = refs[:sums], refs[sums:]
    mid_refs, token_refs, refs = refs[:2], refs[2:4], refs[4:]
    up_refs, array_refs, out_ref = refs[:2], refs[2 : 2 + arrays], refs[2 + arrays]
    held_refs, rhs_refs, up_ref, sem = refs[3 + arrays : -4], refs[-4:-2], refs[-2], refs[-1]
    docs = slots_ref.shape[0]
    tile, width = out_ref.shape
    ends = [ends_ref[d] for d in range(docs)]

    @pl.when(pl.program_id(0) == 0)
    def _():
        copies = load_all(array_refs, held_refs, sem)
        count = at_ref.shape[1]
        span = up_refs[0].shape[0] // count
        for i in range(2):
            for j in range(count):
                start = pl.multiple_of(at_ref[i, j], span)
                copies.append(
                    pltpu.make_async_copy(
                        up_refs[i].at[pl.ds(j * span, span), :],
                        up_ref.at[pl.ds(start, span), :],
                        sem.at[arrays + i * count + j],
                    )
                )
                copies[-1].start()
        for copy in copies:
            copy.wait()
        slots = [slots_ref[d] for d in range(docs)]
        for i, (first, part) in enumerate(parts):
            lay_slabs(rank, part, slots, first, held_refs, rhs_refs[i])

    acc = lax.dot_general(
        token_refs[0][...], rhs_refs[0][...], nt, preferred_element_type=jnp.float32
    )
    acc += lax.dot_general(
        token_refs[1][...], rhs_refs[1][...], nt, preferred_element_type=jnp.float32
    )
    mid = by_document(acc, ends, tile, rank) + mid_refs[0][...] + mid_refs[1][...]
    flat = up_ref.shape[1]
    row = pl.program_id(0) * tile + lax.broadcasted_iota(jnp.int32, (tile, flat), 0)
    slot, low = jnp.zeros((tile, flat), jnp.int32), 0
    for d, end in enumerate(ends):
        slot = jnp.where((row >= low) & (row < end), slots_ref[d], slot)
        low = end
    adapter = lax.broadcasted_iota(jnp.int32, (tile, flat), 1) // rank
    spread = jnp.where(slot == adapter, jnp.concatenate([mid] * (flat // rank), 1), 0.0)
    spread = spread.astype(jnp.bfloat16)
    columns = sum_refs[1].shape[1]
    for n in range(0, width, columns):
        cols = slice(n, n + columns)
        delta = lax.dot_general(spread, up_ref[cols, :], nt, preferred_element_type=jnp.float32)
        base = sum_refs[0][:, cols] + sum_refs[1 + n // columns][...]
        out_ref[:, cols] = (base + adapter_scale * delta).astype(out_ref.dtype)


def last_values(sums, mids, tokens, ups, up_at, arrays, parts, slots, ends):
    rows, width = sums[0].shape
    rank = mids[0].shape[1]
    flat = ups[0].shape[1]
    tile = rows_tile(rows)
    docs = slots.shape[0]
    return pl.pallas_call(
        functools.partial(last_kernel, rank, parts, len(sums), len(arrays)),
        out_shape=jax.ShapeDtypeStruct((rows, width), jnp.bfloat16),
        grid_spec=pltpu.PrefetchScalarGridSpec(
            num_scalar_prefetch=3,
            grid=(rows // tile,),
            in_specs=[tiled(a, tile) for a in (*sums, *mids, *tokens)]
            + [far_memory()] * (2 + len(arrays)),
            out_specs=pl.BlockSpec((tile, width), lambda i, *_: (i, 0)),
            scratch_shapes=[pltpu.VMEM(a.shape, a.dtype) for a in arrays]
            + [pltpu.VMEM((docs * rank, tokens[0].shape[1]), jnp.bfloat16)] * 2
            + [pltpu.VMEM((width, flat), jnp.bfloat16)]
            + [pltpu.SemaphoreType.DMA((len(arrays) + up_at.size,))],
        ),
        compiler_params=pltpu.CompilerParams(vmem_limit_bytes=58 << 20),
        cost_estimate=light,
    )(slots, ends, up_at, *sums, *mids, *tokens, *ups, *arrays)


def after(value, *earlier):
    return lax.optimization_barrier((value, *earlier))[0]


def make(groups, store):
    depth = store // (rows_y * cores)

    def index(z, y, c):
        return (z * rows_y + y) * cores + c

    def pairs(move):
        return [
            (index(z, y, c), index(*move(z, y, c)))
            for z in range(depth)
            for y in range(rows_y)
            for c in range(cores)
        ]

    def along_z(value, k):
        return lax.ppermute(value, "store", pairs(lambda z, y, c: ((z + k) % depth, y, c)))

    def along_y(value):
        return lax.ppermute(value, "store", pairs(lambda z, y, c: (z, 1 - y, c)))

    def across(value):
        return lax.ppermute(value, "store", pairs(lambda z, y, c: (z, y, 1 - c)))

    def along_x(value):
        return lax.ppermute(value, "groups", [(g, g ^ 1) for g in range(groups)])

    class Line:
        def __init__(self, send, most=2):
            self.send, self.most, self.sent = send, most, []

        def __call__(self, value, *args):
            if len(self.sent) >= self.most:
                value = after(value, self.sent[-self.most])
            self.sent.append(self.send(value, *args))
            return self.sent[-1]

    def per_device(
        tokens,
        input_norm_gain,
        value_matrix,
        adapter_down_factors,
        adapter_up_factors,
        document_lengths,
        document_tenant,
        tenant_adapter_slot,
    ):
        shard, adapters, rank = adapter_down_factors.shape
        flat = adapters * rank
        width = value_matrix.shape[1]
        half, part = shard // 2, 3 * shard // 8
        me = lax.axis_index("store")
        side = lax.axis_index("groups") % 2
        mz, my, mc = me // (rows_y * cores), (me // cores) % rows_y, me % cores
        take = lax.dynamic_slice_in_dim

        down = adapter_down_factors.reshape(shard, flat).T
        up = adapter_up_factors.reshape(flat, -1).T
        bit = up.shape[0] // 2
        cut = part + bit
        rest = half - part
        plan = (
            (0, 0, 0, part, 0, half, 0),
            (1, 0, 0, bit, 0, bit, part),
            (0, 0, 0, rest, part, half + part, cut),
            (0, 0, 0, rest, half + part, part, cut + rest),
            (0, 1, 0, part, half, 0, 0),
            (1, 1, 0, bit, bit, 0, part),
            (2, 2, 1, half, 0, half, 0),
            (2, 3, 1, half, half, 0, 0),
        )
        shapes = [(cut + 2 * rest, width), (cut, width), (flat, half), (flat, half)]
        v_first, v_second, d_first, d_rest = cut_shards(
            [value_matrix, up, down], shapes, plan, side
        )
        v_have, v_miss, d_have = {(0, 0): v_first}, {(0, 0): (v_second, 0)}, {(0, 0): d_first}

        ends = jnp.cumsum(document_lengths, axis=1).astype(jnp.int32)
        slots = jnp.sum(
            (document_tenant[0][:, None] == jnp.arange(adapters, dtype=jnp.int32)[None, :])
            * tenant_adapter_slot[None, :],
            axis=1,
        ).astype(jnp.int32)[None, :]
        near = jnp.concatenate([ends, slots], 0)
        far = across(near)
        ends_both = jnp.concatenate([ends, far[:1]], 0)
        slots_both = jnp.concatenate([slots, far[1:]], 0)
        slots_there = along_x(slots_both)
        d_miss = {(0, 0): (pick_adapters([d_rest], slots_both, rank), 0)}
        chosen = slots_both.size * rank

        order = list(range(depth))
        names = [(k, dy) for k in order for dy in range(rows_y)]
        z, y, x = Line(along_z), Line(along_y, 3), Line(along_x, 3)

        def x_values(names, *earlier):
            got = x(after(jnp.concatenate([v_have[name][:cut] for name in names], 0), *earlier))
            for i, name in enumerate(names):
                v_miss[name] = (got, i * cut)

        def x_down(names, *earlier):
            pieces = [d_have[name] for name in names]
            pieces[0] = after(pieces[0], *earlier)
            got = x(pick_adapters(pieces, slots_there, rank))
            for i, name in enumerate(names):
                d_miss[name] = (got, i * slots_both.size * rank)

        source, up_at = [], []
        for lane_at in (mc, 1 - mc):
            for k, dy in names:
                s = index((mz - k) % depth, my ^ dy, lane_at)
                for c in range(shard // lane):
                    piece = c * lane + jnp.where(c * lane < half, 1, -1) * side * half
                    source.append(s * shard + piece)
                up_at += [(2 * s + side) * bit, (2 * s + 1 - side) * bit]
        source = jnp.stack(source).astype(jnp.int32)
        up_at = jnp.stack(up_at).astype(jnp.int32).reshape(2, -1)
        first, second = names[: len(names) // 2], names[len(names) // 2 :]
        span = len(first) * shard

        def lay():
            arrays = []

            def place(array):
                for i, known in enumerate(arrays):
                    if known is array:
                        return i
                arrays.append(array)
                return len(arrays) - 1

            return arrays, place

        def values(names):
            arrays, place = lay()
            plan = []
            for i, name in enumerate(names):
                h, (m, row) = place(v_have[name]), v_miss[name]
                m, at = place(m), i * shard
                plan += [
                    (h, 0, part, at),
                    (h, cut, cut + half - part, at + part),
                    (m, row, row + part, at + half),
                    (h, cut + half - part, cut + 2 * (half - part), at + half + part),
                ]
            return arrays, tuple(plan)

        def ups(names):
            arrays, place = lay()
            plan = []
            for i, name in enumerate(names):
                h, (m, row) = place(v_have[name]), v_miss[name]
                plan.append((h, part, cut, 2 * i * bit))
                plan.append((place(m), row + part, row + cut, (2 * i + 1) * bit))
            return gather_rows(arrays, tuple(plan))

        def slabs(place, names, have, miss):
            out = []
            for i, name in enumerate(names):
                m, row = miss[name]
                out.append((i * shard, place(have[name]), place(m), row))
            return tuple(out)

        ks = order[1:]
        early, last = ks[:-1], ks[-1]
        own, own_rest, other, other_rest = norm_in_order(
            tokens, input_norm_gain, source, [span] * 4
        )
        partner = across(other)
        for k in ks:
            v_have[k, 0] = z(v_have[0, 0], k)
        for k in ks:
            d_have[k, 0] = z(d_have[0, 0], k)
        v_have[0, 1] = y(v_have[0, 0])
        d_have[0, 1] = y(after(d_have[0, 0], v_have[0, 1]))
        x_values([(0, 1)], slots_there)
        x_down([(0, 1)])
        for i, k in enumerate(early):
            pins = [partner] + [d_miss[0, 1][0]] * i
            v_have[k, 1] = y(after(v_have[k, 0], *pins))
            x_values([(k, 0)])
        for k in early:
            x_values([(k, 1)])
        v_have[last, 1] = y(v_have[last, 0])
        x_values([(last, 0)])
        for k in early:
            d_have[k, 1] = y(d_have[k, 0])
        arrays, plan = values(first)
        sums = value_sums(
            after(own, v_have[last, 1], *[d_have[k, 0] for k in early], d_have[early[0], 1]), partner, arrays, plan, width
        )
        x_values([(last, 1)], sums[0])
        for k in early:
            x_down([(k, 0)])
        for k in early:
            x_down([(k, 1)])
        d_have[last, 1] = y(d_have[last, 0])
        x_down([(last, 0)])

        partner_rest = across(after(other_rest, v_have[last, 1]))
        arrays, plan = values(second)
        ready = [d_have[last, 1], d_miss[last, 0][0]]
        sum_own, *sum_far = value_sums(
            after(own_rest, *ready), partner_rest, arrays, plan, width, sums, jnp.bfloat16
        )
        sums = (sum_own, *[across(part) for part in sum_far])
        v_have[0, 0] = after(v_have[0, 0], d_miss[early[-1], 1][0])
        up_lane = ups(names)
        up_both = (up_lane, across(up_lane))

        arrays, place = lay()
        parts = slabs(place, first, d_have, d_miss)
        mid_own, mid_far = mid_partials(own, partner, arrays, parts, ends_both, slots_both, rank)
        mids = (mid_own, across(mid_far))
        x_down([(last, 1)])

        arrays, place = lay()
        parts = [(0, slabs(place, second, d_have, d_miss))]
        done = d_have[last, 1]
        far_have = {n: across(after(d_have[n], done)) for n in second}
        far_miss = {n: (across(after(d_miss[n][0], done)), d_miss[n][1]) for n in second}
        parts.append((slots.shape[1], slabs(place, second, far_have, far_miss)))
        return last_values(
            sums,
            mids,
            (own_rest, other_rest),
            up_both,
            up_at,
            arrays,
            tuple(parts),
            slots[0],
            ends[0],
        )

    return per_device


def solution(mesh):
    in_specs = (
        P(("groups", "store"), None),
        P(),
        P("store", None),
        P("store", None, None),
        P(None, None, "store"),
        P(("groups", "store"), None),
        P(("groups", "store"), None),
        P(),
    )
    out_specs = P(("groups", "store"), None)
    groups, store = mesh.shape["groups"], mesh.shape["store"]

    def run(*args):
        shard = args[2].shape[0]
        cut = shard % (4 * lane) == 0 and args[4].shape[2] % 32 == 0 and store > 4 and store % (rows_y * cores) == 0 and groups % 2 == 0
        return (make(groups, store) if cut else plain)(*args)

    return jax.shard_map(
        run, mesh=mesh, in_specs=in_specs, out_specs=out_specs, check_vma=False
    )
```

```python
import functools

import jax
import jax.numpy as jnp
from jax import lax
from jax.experimental import pallas as pl
from jax.experimental.pallas import tpu as pltpu
from jax.sharding import PartitionSpec as P

adapter_scale = 2.0
cores, rows_y, lane = 2, 2, 128
nt = (((1,), (1,)), ((), ()))
light = pl.CostEstimate(flops=0, bytes_accessed=0, transcendentals=0)


def token_slots(lengths, tenants, tenant_adapter_slot, row_count):
    ends = jnp.cumsum(lengths)
    position = jnp.arange(row_count, dtype=jnp.int32)
    doc_index = jnp.sum((position[:, None] >= ends[None, :]).astype(jnp.int32), axis=1)
    doc_pick = (
        doc_index[:, None] == jnp.arange(lengths.shape[0], dtype=jnp.int32)[None, :]
    ).astype(jnp.int32)
    tenant = jnp.sum(doc_pick * tenants[None, :], axis=1)
    tenant_pick = (
        tenant[:, None] == jnp.arange(tenant_adapter_slot.shape[0], dtype=jnp.int32)[None, :]
    ).astype(jnp.int32)
    return jnp.sum(tenant_pick * tenant_adapter_slot[None, :], axis=1)


def pick_rank(rank_total_rows, slots, count_of_adapters, rank_span_width):
    select = (slots[:, None] == jnp.arange(count_of_adapters, dtype=jnp.int32)[None, :]).astype(
        jnp.float32
    )
    shaped = rank_total_rows.reshape(slots.shape[0], count_of_adapters, rank_span_width)
    return jnp.sum(shaped * select[:, :, None], axis=1)


def plain(
    tokens,
    input_norm_gain,
    value_matrix,
    adapter_down_factors,
    adapter_up_factors,
    document_lengths,
    document_tenant,
    tenant_adapter_slot,
):
    row_count = tokens.shape[0]
    count_of_adapters = adapter_down_factors.shape[1]
    rank_span_width = adapter_down_factors.shape[2]
    flat_width = count_of_adapters * rank_span_width
    wide = tokens.astype(jnp.float32)
    meansq = jnp.mean(wide * wide, axis=1, keepdims=True)
    normed = (wide * lax.rsqrt(meansq + 1e-05) * input_norm_gain.astype(jnp.float32)).astype(
        jnp.bfloat16
    )
    slots = token_slots(document_lengths[0], document_tenant[0], tenant_adapter_slot, row_count)
    base_output = jnp.dot(
        normed,
        lax.all_gather(value_matrix, "store", axis=0, tiled=True),
        preferred_element_type=jnp.float32,
    )
    down = lax.all_gather(adapter_down_factors, "store", axis=0, tiled=True)
    rank_total_rows = jnp.dot(
        normed, down.reshape(down.shape[0], flat_width), preferred_element_type=jnp.float32
    )
    mid = pick_rank(rank_total_rows, slots, count_of_adapters, rank_span_width)
    mid = mid.astype(jnp.bfloat16)
    select = (slots[:, None] == jnp.arange(count_of_adapters, dtype=jnp.int32)[None, :]).astype(
        jnp.bfloat16
    )
    expanded_rows = (mid[:, None, :] * select[:, :, None]).reshape(row_count, flat_width)
    up = lax.all_gather(adapter_up_factors, "store", axis=2, tiled=True)
    adapter_update = jnp.dot(
        expanded_rows, up.reshape(flat_width, up.shape[2]), preferred_element_type=jnp.float32
    )
    return (base_output + adapter_scale * adapter_update).astype(jnp.bfloat16)


def norm_kernel(source_ref, tokens_ref, gain_ref, *out_refs):
    width = tokens_ref.shape[1]
    total = jnp.zeros((tokens_ref.shape[0], lane), jnp.float32)
    for i in range(width // lane):
        part = tokens_ref[:, i * lane : (i + 1) * lane].astype(jnp.float32)
        total += part * part
    scale = lax.rsqrt(jnp.sum(total, axis=1, keepdims=True) / width + 1e-05)
    first = 0
    for out_ref in out_refs:
        for i in range(out_ref.shape[1] // lane):
            start = pl.multiple_of(source_ref[first + i], lane)
            part = tokens_ref[:, pl.ds(start, lane)].astype(jnp.float32)
            gain = gain_ref[:, pl.ds(start, lane)].astype(jnp.float32)
            out_ref[:, i * lane : (i + 1) * lane] = (part * scale * gain).astype(jnp.bfloat16)
        first += out_ref.shape[1] // lane


def norm_in_order(tokens, gain, source, widths):
    rows, width = tokens.shape
    block = 128
    return pl.pallas_call(
        norm_kernel,
        out_shape=[jax.ShapeDtypeStruct((rows, w), jnp.bfloat16) for w in widths],
        grid_spec=pltpu.PrefetchScalarGridSpec(
            num_scalar_prefetch=1,
            grid=(rows // block,),
            in_specs=[
                pl.BlockSpec((block, width), lambda i, *_: (i, 0)),
                pl.BlockSpec((1, width), lambda i, *_: (0, 0)),
            ],
            out_specs=[pl.BlockSpec((block, w), lambda i, *_: (i, 0)) for w in widths],
        ),
        compiler_params=pltpu.CompilerParams(vmem_limit_bytes=58 << 20),
        cost_estimate=light,
    )(source, tokens, gain.reshape(1, width))


def far_memory():
    return pl.BlockSpec(memory_space=pl.ANY)


def tiled(array, tile):
    return pl.BlockSpec((tile,) + array.shape[1:], lambda i, *_: (i, 0))


def rows_tile(rows):
    return 256 if rows % 256 == 0 else rows


def pick_kernel(rank, slots_ref, *refs):
    piece_refs, out_ref = refs[:-1], refs[-1]
    sides, docs = slots_ref.shape
    at = 0
    for piece in piece_refs:
        for i in range(sides * docs):
            start = pl.multiple_of(slots_ref[i // docs, i % docs] * rank, rank)
            out_ref[at : at + rank, :] = piece[pl.ds(start, rank), :]
            at += rank


def pick_adapters(pieces, slots, rank):
    count = slots.shape[0] * slots.shape[1] * len(pieces)
    columns = pieces[0].shape[1]
    whole = [pl.BlockSpec(p.shape, lambda i, *_: (0, 0)) for p in pieces]
    return pl.pallas_call(
        functools.partial(pick_kernel, rank),
        out_shape=jax.ShapeDtypeStruct((count * rank, columns), jnp.bfloat16),
        grid_spec=pltpu.PrefetchScalarGridSpec(
            num_scalar_prefetch=1,
            grid=(1,),
            in_specs=whole,
            out_specs=pl.BlockSpec((count * rank, columns), lambda i, *_: (0, 0)),
        ),
        compiler_params=pltpu.CompilerParams(vmem_limit_bytes=12 << 20),
        cost_estimate=light,
    )(slots, *pieces)


def value_kernel(plan, columns, has_sum, arrays, *refs):
    own_ref, far_ref, refs = refs[0], refs[1], refs[2:]
    sum_refs, refs = refs[:has_sum], refs[has_sum:]
    array_refs, out_refs, held_ref, sem = refs[:arrays], refs[arrays:-2], refs[-2], refs[-1]

    @pl.when(pl.program_id(0) == 0)
    def _():
        copies = [
            pltpu.make_async_copy(
                array_refs[i].at[a:b, :], held_ref.at[row : row + b - a, :], sem.at[j]
            )
            for j, (i, a, b, row) in enumerate(plan)
        ]
        for copy in copies:
            copy.start()
        for copy in copies:
            copy.wait()

    tile = own_ref.shape[0]
    both = jnp.concatenate([own_ref[...], far_ref[...]], 0)
    for n in range(0, held_ref.shape[1], columns):
        cols = slice(n, n + columns)
        acc = jnp.dot(both, held_ref[:, cols], preferred_element_type=jnp.float32)
        terms = [acc[:tile], acc[tile:]]
        if has_sum:
            terms[0] += sum_refs[0][:, cols]
            terms[1] += sum_refs[1 + n // columns][...]
        out_refs[0][:, cols] = terms[0]
        out_refs[1 + n // columns][...] = terms[1].astype(out_refs[1].dtype)


def value_sums(own, far, arrays, plan, width, sums=(), far_type=jnp.float32):
    rows, depth = own.shape
    tile, columns = rows_tile(rows), 256
    outs = [jax.ShapeDtypeStruct((rows, width), jnp.float32)]
    outs += [jax.ShapeDtypeStruct((rows, columns), far_type)] * (width // columns)
    return pl.pallas_call(
        functools.partial(value_kernel, plan, columns, len(sums), len(arrays)),
        out_shape=outs,
        grid=(rows // tile,),
        in_specs=[tiled(b, tile) for b in (own, far, *sums)] + [far_memory()] * len(arrays),
        out_specs=[tiled(o, tile) for o in outs],
        scratch_shapes=[
            pltpu.VMEM((depth, width), jnp.bfloat16),
            pltpu.SemaphoreType.DMA((len(plan),)),
        ],
        compiler_params=pltpu.CompilerParams(vmem_limit_bytes=14 << 20),
        cost_estimate=light,
    )(own, far, *sums, *arrays)


def cut_kernel(plan, side_ref, *refs):
    arrays = 1 + max(p[0] for p in plan)
    array_refs, out_refs, sem = refs[:arrays], refs[arrays:-1], refs[-1]
    copies = []
    for j, (i, o, axis, length, even, odd, at) in enumerate(plan):
        start = pl.multiple_of(even + side_ref[0] * (odd - even), 16 if axis == 0 else lane)
        src, dst = [slice(None)] * 2, [slice(None)] * 2
        src[axis], dst[axis] = pl.ds(start, length), slice(at, at + length)
        copies.append(
            pltpu.make_async_copy(
                array_refs[i].at[tuple(src)], out_refs[o].at[tuple(dst)], sem.at[j]
            )
        )
        copies[-1].start()
    for copy in copies:
        copy.wait()


def cut_shards(arrays, shapes, plan, side):
    return pl.pallas_call(
        functools.partial(cut_kernel, plan),
        out_shape=[jax.ShapeDtypeStruct(s, jnp.bfloat16) for s in shapes],
        grid_spec=pltpu.PrefetchScalarGridSpec(
            num_scalar_prefetch=1,
            in_specs=[far_memory()] * len(arrays),
            out_specs=[pl.BlockSpec(memory_space=pltpu.VMEM)] * len(shapes),
            scratch_shapes=[pltpu.SemaphoreType.DMA((len(plan),))],
        ),
        compiler_params=pltpu.CompilerParams(vmem_limit_bytes=58 << 20),
        cost_estimate=light,
    )(side.reshape(1).astype(jnp.int32), *arrays)


def gather_kernel(plan, *refs):
    array_refs, out_ref, sem = refs[:-2], refs[-2], refs[-1]
    copies = [
        pltpu.make_async_copy(array_refs[i].at[a:b, :], out_ref.at[row : row + b - a, :], sem.at[j])
        for j, (i, a, b, row) in enumerate(plan)
    ]
    for copy in copies:
        copy.start()
    for copy in copies:
        copy.wait()


def gather_rows(arrays, plan):
    rows = sum(b - a for _, a, b, _ in plan)
    return pl.pallas_call(
        functools.partial(gather_kernel, plan),
        out_shape=jax.ShapeDtypeStruct((rows, arrays[0].shape[1]), arrays[0].dtype),
        in_specs=[far_memory()] * len(arrays),
        out_specs=pl.BlockSpec(memory_space=pltpu.VMEM),
        scratch_shapes=[pltpu.SemaphoreType.DMA((len(plan),))],
        compiler_params=pltpu.CompilerParams(vmem_limit_bytes=12 << 20),
        cost_estimate=light,
    )(*arrays)


def load_all(array_refs, held_refs, sem, first=0):
    copies = [
        pltpu.make_async_copy(a, h, sem.at[first + i])
        for i, (a, h) in enumerate(zip(array_refs, held_refs))
    ]
    for copy in copies:
        copy.start()
    return copies


def lay_slabs(rank, parts, slots, first, held_refs, rhs_ref):
    for at, have, miss, row in parts:
        for d, slot in enumerate(slots):
            rows = slice(d * rank, (d + 1) * rank)
            start = pl.multiple_of(slot * rank, rank)
            half = held_refs[have].shape[1]
            rhs_ref[rows, at : at + half] = held_refs[have][pl.ds(start, rank), :]
            low = row + (first + d) * rank
            rhs_ref[rows, at + half : at + 2 * half] = held_refs[miss][low : low + rank, :]


def by_document(acc, ends, tile, rank):
    row = pl.program_id(0) * tile + lax.broadcasted_iota(jnp.int32, (tile, rank), 0)
    mid = jnp.zeros((tile, rank), jnp.float32)
    low = 0
    for doc, end in enumerate(ends):
        mid = jnp.where((row >= low) & (row < end), acc[:, doc * rank : (doc + 1) * rank], mid)
        low = end
    return mid


def mid_kernel(rank, parts, arrays, ends_ref, slots_ref, *refs):
    token_refs, array_refs, out_refs = refs[:2], refs[2 : 2 + arrays], refs[2 + arrays : 4 + arrays]
    held_refs, rhs_refs, sem = refs[4 + arrays : -3], refs[-3:-1], refs[-1]
    docs = slots_ref.shape[1]
    tile = out_refs[0].shape[0]

    @pl.when(pl.program_id(0) == 0)
    def _():
        for copy in load_all(array_refs, held_refs, sem):
            copy.wait()
        for side in range(2):
            slots = [slots_ref[side, d] for d in range(docs)]
            lay_slabs(rank, parts, slots, side * docs, held_refs, rhs_refs[side])

    for side in range(2):
        acc = lax.dot_general(
            token_refs[side][...], rhs_refs[side][...], nt, preferred_element_type=jnp.float32
        )
        ends = [ends_ref[side, d] for d in range(docs)]
        out_refs[side][...] = by_document(acc, ends, tile, rank)


def mid_partials(own, far, arrays, parts, ends, slots, rank):
    rows, depth = own.shape
    tile = rows_tile(rows)
    docs = slots.shape[1]
    out = jax.ShapeDtypeStruct((rows, rank), jnp.float32)
    return pl.pallas_call(
        functools.partial(mid_kernel, rank, parts, len(arrays)),
        out_shape=(out, out),
        grid_spec=pltpu.PrefetchScalarGridSpec(
            num_scalar_prefetch=2,
            grid=(rows // tile,),
            in_specs=[tiled(own, tile), tiled(far, tile)] + [far_memory()] * len(arrays),
            out_specs=[pl.BlockSpec((tile, rank), lambda i, *_: (i, 0))] * 2,
            scratch_shapes=[pltpu.VMEM(a.shape, a.dtype) for a in arrays]
            + [pltpu.VMEM((docs * rank, depth), jnp.bfloat16)] * 2
            + [pltpu.SemaphoreType.DMA((len(arrays),))],
        ),
        compiler_params=pltpu.CompilerParams(vmem_limit_bytes=12 << 20),
        cost_estimate=light,
    )(ends, slots, own, far, *arrays)


def last_kernel(rank, parts, sums, arrays, slots_ref, ends_ref, at_ref, *refs):
    sum_refs, refs = refs[:sums], refs[sums:]
    mid_refs, token_refs, refs = refs[:2], refs[2:4], refs[4:]
    up_refs, array_refs, out_ref = refs[:2], refs[2 : 2 + arrays], refs[2 + arrays]
    held_refs, rhs_refs, up_ref, sem = refs[3 + arrays : -4], refs[-4:-2], refs[-2], refs[-1]
    docs = slots_ref.shape[0]
    tile, width = out_ref.shape
    ends = [ends_ref[d] for d in range(docs)]

    @pl.when(pl.program_id(0) == 0)
    def _():
        copies = load_all(array_refs, held_refs, sem)
        count = at_ref.shape[1]
        span = up_refs[0].shape[0] // count
        for i in range(2):
            for j in range(count):
                start = pl.multiple_of(at_ref[i, j], span)
                copies.append(
                    pltpu.make_async_copy(
                        up_refs[i].at[pl.ds(j * span, span), :],
                        up_ref.at[pl.ds(start, span), :],
                        sem.at[arrays + i * count + j],
                    )
                )
                copies[-1].start()
        for copy in copies:
            copy.wait()
        slots = [slots_ref[d] for d in range(docs)]
        for i, (first, part) in enumerate(parts):
            lay_slabs(rank, part, slots, first, held_refs, rhs_refs[i])

    acc = lax.dot_general(
        token_refs[0][...], rhs_refs[0][...], nt, preferred_element_type=jnp.float32
    )
    acc += lax.dot_general(
        token_refs[1][...], rhs_refs[1][...], nt, preferred_element_type=jnp.float32
    )
    mid = by_document(acc, ends, tile, rank) + mid_refs[0][...] + mid_refs[1][...]
    flat = up_ref.shape[1]
    row = pl.program_id(0) * tile + lax.broadcasted_iota(jnp.int32, (tile, flat), 0)
    slot, low = jnp.zeros((tile, flat), jnp.int32), 0
    for d, end in enumerate(ends):
        slot = jnp.where((row >= low) & (row < end), slots_ref[d], slot)
        low = end
    adapter = lax.broadcasted_iota(jnp.int32, (tile, flat), 1) // rank
    spread = jnp.where(slot == adapter, jnp.concatenate([mid] * (flat // rank), 1), 0.0)
    spread = spread.astype(jnp.bfloat16)
    columns = sum_refs[1].shape[1]
    for n in range(0, width, columns):
        cols = slice(n, n + columns)
        delta = lax.dot_general(spread, up_ref[cols, :], nt, preferred_element_type=jnp.float32)
        base = sum_refs[0][:, cols] + sum_refs[1 + n // columns][...]
        out_ref[:, cols] = (base + adapter_scale * delta).astype(out_ref.dtype)


def last_values(sums, mids, tokens, ups, up_at, arrays, parts, slots, ends):
    rows, width = sums[0].shape
    rank = mids[0].shape[1]
    flat = ups[0].shape[1]
    tile = rows_tile(rows)
    docs = slots.shape[0]
    return pl.pallas_call(
        functools.partial(last_kernel, rank, parts, len(sums), len(arrays)),
        out_shape=jax.ShapeDtypeStruct((rows, width), jnp.bfloat16),
        grid_spec=pltpu.PrefetchScalarGridSpec(
            num_scalar_prefetch=3,
            grid=(rows // tile,),
            in_specs=[tiled(a, tile) for a in (*sums, *mids, *tokens)]
            + [far_memory()] * (2 + len(arrays)),
            out_specs=pl.BlockSpec((tile, width), lambda i, *_: (i, 0)),
            scratch_shapes=[pltpu.VMEM(a.shape, a.dtype) for a in arrays]
            + [pltpu.VMEM((docs * rank, tokens[0].shape[1]), jnp.bfloat16)] * 2
            + [pltpu.VMEM((width, flat), jnp.bfloat16)]
            + [pltpu.SemaphoreType.DMA((len(arrays) + up_at.size,))],
        ),
        compiler_params=pltpu.CompilerParams(vmem_limit_bytes=58 << 20),
        cost_estimate=light,
    )(slots, ends, up_at, *sums, *mids, *tokens, *ups, *arrays)


def after(value, *earlier):
    return lax.optimization_barrier((value, *earlier))[0]


def make(groups, store):
    depth = store // (rows_y * cores)

    def index(z, y, c):
        return (z * rows_y + y) * cores + c

    def pairs(move):
        return [
            (index(z, y, c), index(*move(z, y, c)))
            for z in range(depth)
            for y in range(rows_y)
            for c in range(cores)
        ]

    def along_z(value, k):
        return lax.ppermute(value, "store", pairs(lambda z, y, c: ((z + k) % depth, y, c)))

    def along_y(value):
        return lax.ppermute(value, "store", pairs(lambda z, y, c: (z, 1 - y, c)))

    def across(value):
        return lax.ppermute(value, "store", pairs(lambda z, y, c: (z, y, 1 - c)))

    def along_x(value):
        return lax.ppermute(value, "groups", [(g, g ^ 1) for g in range(groups)])

    class Line:
        def __init__(self, send, most=2):
            self.send, self.most, self.sent = send, most, []

        def __call__(self, value, *args):
            if len(self.sent) >= self.most:
                value = after(value, self.sent[-self.most])
            self.sent.append(self.send(value, *args))
            return self.sent[-1]

    def per_device(
        tokens,
        input_norm_gain,
        value_matrix,
        adapter_down_factors,
        adapter_up_factors,
        document_lengths,
        document_tenant,
        tenant_adapter_slot,
    ):
        shard, adapters, rank = adapter_down_factors.shape
        flat = adapters * rank
        width = value_matrix.shape[1]
        half, part = shard // 2, shard // 4
        me = lax.axis_index("store")
        side = lax.axis_index("groups") % 2
        mz, my, mc = me // (rows_y * cores), (me // cores) % rows_y, me % cores
        take = lax.dynamic_slice_in_dim

        down = adapter_down_factors.reshape(shard, flat).T
        up = adapter_up_factors.reshape(flat, -1).T
        bit = up.shape[0] // 2
        cut = part + bit
        rest = half - part
        plan = (
            (0, 0, 0, part, 0, half, 0),
            (1, 0, 0, bit, 0, bit, part),
            (0, 0, 0, rest, part, half + part, cut),
            (0, 0, 0, rest, half + part, part, cut + rest),
            (0, 1, 0, part, half, 0, 0),
            (1, 1, 0, bit, bit, 0, part),
            (2, 2, 1, half, 0, half, 0),
            (2, 3, 1, half, half, 0, 0),
        )
        shapes = [(cut + 2 * rest, width), (cut, width), (flat, half), (flat, half)]
        v_first, v_second, d_first, d_rest = cut_shards(
            [value_matrix, up, down], shapes, plan, side
        )
        v_have, v_miss, d_have = {(0, 0): v_first}, {(0, 0): (v_second, 0)}, {(0, 0): d_first}

        ends = jnp.cumsum(document_lengths, axis=1).astype(jnp.int32)
        slots = jnp.sum(
            (document_tenant[0][:, None] == jnp.arange(adapters, dtype=jnp.int32)[None, :])
            * tenant_adapter_slot[None, :],
            axis=1,
        ).astype(jnp.int32)[None, :]
        near = jnp.concatenate([ends, slots], 0)
        far = across(near)
        ends_both = jnp.concatenate([ends, far[:1]], 0)
        slots_both = jnp.concatenate([slots, far[1:]], 0)
        slots_there = along_x(slots_both)
        d_miss = {(0, 0): (pick_adapters([d_rest], slots_both, rank), 0)}
        chosen = slots_both.size * rank

        order = list(range(depth))
        names = [(k, dy) for k in order for dy in range(rows_y)]
        z, y, x = Line(along_z), Line(along_y, 3), Line(along_x, 3)

        def x_values(names, *earlier):
            got = x(after(jnp.concatenate([v_have[name][:cut] for name in names], 0), *earlier))
            for i, name in enumerate(names):
                v_miss[name] = (got, i * cut)

        def x_down(names, *earlier):
            pieces = [d_have[name] for name in names]
            pieces[0] = after(pieces[0], *earlier)
            got = x(pick_adapters(pieces, slots_there, rank))
            for i, name in enumerate(names):
                d_miss[name] = (got, i * slots_both.size * rank)

        source, up_at = [], []
        for lane_at in (mc, 1 - mc):
            for k, dy in names:
                s = index((mz - k) % depth, my ^ dy, lane_at)
                for c in range(shard // lane):
                    piece = c * lane + jnp.where(c * lane < half, 1, -1) * side * half
                    source.append(s * shard + piece)
                up_at += [(2 * s + side) * bit, (2 * s + 1 - side) * bit]
        source = jnp.stack(source).astype(jnp.int32)
        up_at = jnp.stack(up_at).astype(jnp.int32).reshape(2, -1)
        first, second = names[: len(names) // 2], names[len(names) // 2 :]
        span = len(first) * shard

        def lay():
            arrays = []

            def place(array):
                for i, known in enumerate(arrays):
                    if known is array:
                        return i
                arrays.append(array)
                return len(arrays) - 1

            return arrays, place

        def values(names):
            arrays, place = lay()
            plan = []
            for i, name in enumerate(names):
                h, (m, row) = place(v_have[name]), v_miss[name]
                m, at = place(m), i * shard
                plan += [
                    (h, 0, part, at),
                    (h, cut, cut + half - part, at + part),
                    (m, row, row + part, at + half),
                    (h, cut + half - part, cut + 2 * (half - part), at + half + part),
                ]
            return arrays, tuple(plan)

        def ups(names):
            arrays, place = lay()
            plan = []
            for i, name in enumerate(names):
                h, (m, row) = place(v_have[name]), v_miss[name]
                plan.append((h, part, cut, 2 * i * bit))
                plan.append((place(m), row + part, row + cut, (2 * i + 1) * bit))
            return gather_rows(arrays, tuple(plan))

        def slabs(place, names, have, miss):
            out = []
            for i, name in enumerate(names):
                m, row = miss[name]
                out.append((i * shard, place(have[name]), place(m), row))
            return tuple(out)

        ks = order[1:]
        early, last = ks[:-1], ks[-1]
        own, own_rest, other, other_rest = norm_in_order(
            tokens, input_norm_gain, source, [span] * 4
        )
        partner = across(other)
        for k in ks:
            v_have[k, 0] = z(v_have[0, 0], k)
        for k in ks:
            d_have[k, 0] = z(d_have[0, 0], k)
        v_have[0, 1] = y(v_have[0, 0])
        d_have[0, 1] = y(after(d_have[0, 0], v_have[0, 1]))
        x_values([(0, 1)], partner)
        x_down([(0, 1)])
        for i, k in enumerate(early):
            pins = [partner] + [d_miss[0, 1][0]] * i
            v_have[k, 1] = y(after(v_have[k, 0], *pins))
            x_values([(k, 0)])
        for k in early:
            x_values([(k, 1)])
        v_have[last, 1] = y(v_have[last, 0])
        x_values([(last, 0)])
        for k in early:
            d_have[k, 1] = y(d_have[k, 0])
        arrays, plan = values(first)
        sums = value_sums(
            after(own, v_have[last, 1], *[d_have[k, 0] for k in early], d_have[early[0], 1]), partner, arrays, plan, width
        )
        x_values([(last, 1)], sums[0])
        for k in early:
            x_down([(k, 0)])
        for k in early[:-1]:
            x_down([(k, 1)])
        partner_rest = across(after(other_rest, v_have[last, 1]))
        arrays, plan = values(second)
        ready = [d_have[last, 0], d_have[early[0], 1]]
        sum_own, *sum_far = value_sums(
            after(own_rest, *ready), partner_rest, arrays, plan, width, sums, jnp.bfloat16
        )
        x_down([(early[-1], 1)], sum_own)
        d_have[last, 1] = y(d_have[last, 0])
        x_down([(last, 0)])

        sums = (sum_own, *[across(part) for part in sum_far])
        v_have[0, 0] = after(v_have[0, 0], d_miss[early[-1], 1][0])
        up_lane = ups(names)
        up_both = (up_lane, across(up_lane))

        arrays, place = lay()
        parts = slabs(place, first, d_have, d_miss)
        mid_own, mid_far = mid_partials(own, partner, arrays, parts, ends_both, slots_both, rank)
        mids = (mid_own, across(mid_far))
        x_down([(last, 1)], mid_own)

        arrays, place = lay()
        parts = [(0, slabs(place, second, d_have, d_miss))]
        done = d_have[last, 1]
        far_have = {n: across(after(d_have[n], done)) for n in second}
        far_miss = {n: (across(after(d_miss[n][0], done)), d_miss[n][1]) for n in second}
        parts.append((slots.shape[1], slabs(place, second, far_have, far_miss)))
        return last_values(
            sums,
            mids,
            (own_rest, other_rest),
            up_both,
            up_at,
            arrays,
            tuple(parts),
            slots[0],
            ends[0],
        )

    return per_device


def solution(mesh):
    in_specs = (
        P(("groups", "store"), None),
        P(),
        P("store", None),
        P("store", None, None),
        P(None, None, "store"),
        P(("groups", "store"), None),
        P(("groups", "store"), None),
        P(),
    )
    out_specs = P(("groups", "store"), None)
    groups, store = mesh.shape["groups"], mesh.shape["store"]

    def run(*args):
        shard = args[2].shape[0]
        cut = shard % (4 * lane) == 0 and args[4].shape[2] % 32 == 0 and store > 4 and store % (rows_y * cores) == 0 and groups % 2 == 0
        return (make(groups, store) if cut else plain)(*args)

    return jax.shard_map(
        run, mesh=mesh, in_specs=in_specs, out_specs=out_specs, check_vma=False
    )
```

```python
import functools

import jax
import jax.numpy as jnp
from jax import lax
from jax.experimental import pallas as pl
from jax.experimental.pallas import tpu as pltpu
from jax.sharding import PartitionSpec as P

adapter_scale = 2.0
cores, rows_y, lane = 2, 2, 128
nt = (((1,), (1,)), ((), ()))
light = pl.CostEstimate(flops=0, bytes_accessed=0, transcendentals=0)


def token_slots(lengths, tenants, tenant_adapter_slot, row_count):
    ends = jnp.cumsum(lengths)
    position = jnp.arange(row_count, dtype=jnp.int32)
    doc_index = jnp.sum((position[:, None] >= ends[None, :]).astype(jnp.int32), axis=1)
    doc_pick = (
        doc_index[:, None] == jnp.arange(lengths.shape[0], dtype=jnp.int32)[None, :]
    ).astype(jnp.int32)
    tenant = jnp.sum(doc_pick * tenants[None, :], axis=1)
    tenant_pick = (
        tenant[:, None] == jnp.arange(tenant_adapter_slot.shape[0], dtype=jnp.int32)[None, :]
    ).astype(jnp.int32)
    return jnp.sum(tenant_pick * tenant_adapter_slot[None, :], axis=1)


def pick_rank(rank_total_rows, slots, count_of_adapters, rank_span_width):
    select = (slots[:, None] == jnp.arange(count_of_adapters, dtype=jnp.int32)[None, :]).astype(
        jnp.float32
    )
    shaped = rank_total_rows.reshape(slots.shape[0], count_of_adapters, rank_span_width)
    return jnp.sum(shaped * select[:, :, None], axis=1)


def plain(
    tokens,
    input_norm_gain,
    value_matrix,
    adapter_down_factors,
    adapter_up_factors,
    document_lengths,
    document_tenant,
    tenant_adapter_slot,
):
    row_count = tokens.shape[0]
    count_of_adapters = adapter_down_factors.shape[1]
    rank_span_width = adapter_down_factors.shape[2]
    flat_width = count_of_adapters * rank_span_width
    wide = tokens.astype(jnp.float32)
    meansq = jnp.mean(wide * wide, axis=1, keepdims=True)
    normed = (wide * lax.rsqrt(meansq + 1e-05) * input_norm_gain.astype(jnp.float32)).astype(
        jnp.bfloat16
    )
    slots = token_slots(document_lengths[0], document_tenant[0], tenant_adapter_slot, row_count)
    base_output = jnp.dot(
        normed,
        lax.all_gather(value_matrix, "store", axis=0, tiled=True),
        preferred_element_type=jnp.float32,
    )
    down = lax.all_gather(adapter_down_factors, "store", axis=0, tiled=True)
    rank_total_rows = jnp.dot(
        normed, down.reshape(down.shape[0], flat_width), preferred_element_type=jnp.float32
    )
    mid = pick_rank(rank_total_rows, slots, count_of_adapters, rank_span_width)
    mid = mid.astype(jnp.bfloat16)
    select = (slots[:, None] == jnp.arange(count_of_adapters, dtype=jnp.int32)[None, :]).astype(
        jnp.bfloat16
    )
    expanded_rows = (mid[:, None, :] * select[:, :, None]).reshape(row_count, flat_width)
    up = lax.all_gather(adapter_up_factors, "store", axis=2, tiled=True)
    adapter_update = jnp.dot(
        expanded_rows, up.reshape(flat_width, up.shape[2]), preferred_element_type=jnp.float32
    )
    return (base_output + adapter_scale * adapter_update).astype(jnp.bfloat16)


def norm_kernel(source_ref, tokens_ref, gain_ref, *out_refs):
    width = tokens_ref.shape[1]
    total = jnp.zeros((tokens_ref.shape[0], lane), jnp.float32)
    for i in range(width // lane):
        part = tokens_ref[:, i * lane : (i + 1) * lane].astype(jnp.float32)
        total += part * part
    scale = lax.rsqrt(jnp.sum(total, axis=1, keepdims=True) / width + 1e-05)
    first = 0
    for out_ref in out_refs:
        for i in range(out_ref.shape[1] // lane):
            start = pl.multiple_of(source_ref[first + i], lane)
            part = tokens_ref[:, pl.ds(start, lane)].astype(jnp.float32)
            gain = gain_ref[:, pl.ds(start, lane)].astype(jnp.float32)
            out_ref[:, i * lane : (i + 1) * lane] = (part * scale * gain).astype(jnp.bfloat16)
        first += out_ref.shape[1] // lane


def norm_in_order(tokens, gain, source, widths):
    rows, width = tokens.shape
    block = 128
    return pl.pallas_call(
        norm_kernel,
        out_shape=[jax.ShapeDtypeStruct((rows, w), jnp.bfloat16) for w in widths],
        grid_spec=pltpu.PrefetchScalarGridSpec(
            num_scalar_prefetch=1,
            grid=(rows // block,),
            in_specs=[
                pl.BlockSpec((block, width), lambda i, *_: (i, 0)),
                pl.BlockSpec((1, width), lambda i, *_: (0, 0)),
            ],
            out_specs=[pl.BlockSpec((block, w), lambda i, *_: (i, 0)) for w in widths],
        ),
        compiler_params=pltpu.CompilerParams(vmem_limit_bytes=20 << 20),
        cost_estimate=light,
    )(source, tokens, gain.reshape(1, width))


def far_memory():
    return pl.BlockSpec(memory_space=pl.ANY)


def tiled(array, tile):
    return pl.BlockSpec((tile,) + array.shape[1:], lambda i, *_: (i, 0))


def rows_tile(rows):
    return 256 if rows % 256 == 0 else rows


def pick_kernel(rank, slots_ref, *refs):
    piece_refs, out_ref = refs[:-1], refs[-1]
    sides, docs = slots_ref.shape
    at = 0
    for piece in piece_refs:
        for i in range(sides * docs):
            start = pl.multiple_of(slots_ref[i // docs, i % docs] * rank, rank)
            out_ref[at : at + rank, :] = piece[pl.ds(start, rank), :]
            at += rank


def pick_adapters(pieces, slots, rank):
    count = slots.shape[0] * slots.shape[1] * len(pieces)
    columns = pieces[0].shape[1]
    whole = [pl.BlockSpec(p.shape, lambda i, *_: (0, 0)) for p in pieces]
    return pl.pallas_call(
        functools.partial(pick_kernel, rank),
        out_shape=jax.ShapeDtypeStruct((count * rank, columns), jnp.bfloat16),
        grid_spec=pltpu.PrefetchScalarGridSpec(
            num_scalar_prefetch=1,
            grid=(1,),
            in_specs=whole,
            out_specs=pl.BlockSpec((count * rank, columns), lambda i, *_: (0, 0)),
        ),
        compiler_params=pltpu.CompilerParams(vmem_limit_bytes=12 << 20),
        cost_estimate=light,
    )(slots, *pieces)


def value_kernel(plan, columns, has_sum, arrays, *refs):
    own_ref, far_ref, refs = refs[0], refs[1], refs[2:]
    sum_refs, refs = refs[:has_sum], refs[has_sum:]
    array_refs, out_refs, held_ref, sem = refs[:arrays], refs[arrays:-2], refs[-2], refs[-1]

    @pl.when(pl.program_id(0) == 0)
    def _():
        copies = [
            pltpu.make_async_copy(
                array_refs[i].at[a:b, :], held_ref.at[row : row + b - a, :], sem.at[j]
            )
            for j, (i, a, b, row) in enumerate(plan)
        ]
        for copy in copies:
            copy.start()
        for copy in copies:
            copy.wait()

    tile = own_ref.shape[0]
    both = jnp.concatenate([own_ref[...], far_ref[...]], 0)
    for n in range(0, held_ref.shape[1], columns):
        cols = slice(n, n + columns)
        acc = jnp.dot(both, held_ref[:, cols], preferred_element_type=jnp.float32)
        terms = [acc[:tile], acc[tile:]]
        if has_sum:
            terms[0] += sum_refs[0][:, cols]
            terms[1] += sum_refs[1 + n // columns][...]
        out_refs[0][:, cols] = terms[0]
        out_refs[1 + n // columns][...] = terms[1].astype(out_refs[1].dtype)


def value_sums(own, far, arrays, plan, width, sums=(), far_type=jnp.float32):
    rows, depth = own.shape
    tile, columns = rows_tile(rows), 256
    outs = [jax.ShapeDtypeStruct((rows, width), jnp.float32)]
    outs += [jax.ShapeDtypeStruct((rows, columns), far_type)] * (width // columns)
    return pl.pallas_call(
        functools.partial(value_kernel, plan, columns, len(sums), len(arrays)),
        out_shape=outs,
        grid=(rows // tile,),
        in_specs=[tiled(b, tile) for b in (own, far, *sums)] + [far_memory()] * len(arrays),
        out_specs=[tiled(o, tile) for o in outs],
        scratch_shapes=[
            pltpu.VMEM((depth, width), jnp.bfloat16),
            pltpu.SemaphoreType.DMA((len(plan),)),
        ],
        compiler_params=pltpu.CompilerParams(vmem_limit_bytes=24 << 20),
        cost_estimate=light,
    )(own, far, *sums, *arrays)


def cut_kernel(plan, side_ref, *refs):
    arrays = 1 + max(p[0] for p in plan)
    array_refs, out_refs, sem = refs[:arrays], refs[arrays:-1], refs[-1]
    copies = []
    for j, (i, o, axis, length, even, odd, at) in enumerate(plan):
        start = pl.multiple_of(even + side_ref[0] * (odd - even), 16 if axis == 0 else lane)
        src, dst = [slice(None)] * 2, [slice(None)] * 2
        src[axis], dst[axis] = pl.ds(start, length), slice(at, at + length)
        copies.append(
            pltpu.make_async_copy(
                array_refs[i].at[tuple(src)], out_refs[o].at[tuple(dst)], sem.at[j]
            )
        )
        copies[-1].start()
    for copy in copies:
        copy.wait()


def cut_shards(arrays, shapes, plan, side):
    return pl.pallas_call(
        functools.partial(cut_kernel, plan),
        out_shape=[jax.ShapeDtypeStruct(s, jnp.bfloat16) for s in shapes],
        grid_spec=pltpu.PrefetchScalarGridSpec(
            num_scalar_prefetch=1,
            in_specs=[far_memory()] * len(arrays),
            out_specs=[pl.BlockSpec(memory_space=pltpu.VMEM)] * len(shapes),
            scratch_shapes=[pltpu.SemaphoreType.DMA((len(plan),))],
        ),
        compiler_params=pltpu.CompilerParams(vmem_limit_bytes=12 << 20),
        cost_estimate=light,
    )(side.reshape(1).astype(jnp.int32), *arrays)


def gather_kernel(plan, *refs):
    array_refs, out_ref, sem = refs[:-2], refs[-2], refs[-1]
    copies = [
        pltpu.make_async_copy(array_refs[i].at[a:b, :], out_ref.at[row : row + b - a, :], sem.at[j])
        for j, (i, a, b, row) in enumerate(plan)
    ]
    for copy in copies:
        copy.start()
    for copy in copies:
        copy.wait()


def gather_rows(arrays, plan):
    rows = sum(b - a for _, a, b, _ in plan)
    return pl.pallas_call(
        functools.partial(gather_kernel, plan),
        out_shape=jax.ShapeDtypeStruct((rows, arrays[0].shape[1]), arrays[0].dtype),
        in_specs=[far_memory()] * len(arrays),
        out_specs=pl.BlockSpec(memory_space=pltpu.VMEM),
        scratch_shapes=[pltpu.SemaphoreType.DMA((len(plan),))],
        compiler_params=pltpu.CompilerParams(vmem_limit_bytes=12 << 20),
        cost_estimate=light,
    )(*arrays)


def load_all(array_refs, held_refs, sem, first=0):
    copies = [
        pltpu.make_async_copy(a, h, sem.at[first + i])
        for i, (a, h) in enumerate(zip(array_refs, held_refs))
    ]
    for copy in copies:
        copy.start()
    return copies


def lay_slabs(rank, parts, slots, first, held_refs, rhs_ref):
    for at, have, miss, row in parts:
        for d, slot in enumerate(slots):
            rows = slice(d * rank, (d + 1) * rank)
            start = pl.multiple_of(slot * rank, rank)
            half = held_refs[have].shape[1]
            rhs_ref[rows, at : at + half] = held_refs[have][pl.ds(start, rank), :]
            low = row + (first + d) * rank
            rhs_ref[rows, at + half : at + 2 * half] = held_refs[miss][low : low + rank, :]


def by_document(acc, ends, tile, rank):
    row = pl.program_id(0) * tile + lax.broadcasted_iota(jnp.int32, (tile, rank), 0)
    mid = jnp.zeros((tile, rank), jnp.float32)
    low = 0
    for doc, end in enumerate(ends):
        mid = jnp.where((row >= low) & (row < end), acc[:, doc * rank : (doc + 1) * rank], mid)
        low = end
    return mid


def mid_kernel(rank, parts, arrays, ends_ref, slots_ref, *refs):
    token_refs, array_refs, out_refs = refs[:2], refs[2 : 2 + arrays], refs[2 + arrays : 4 + arrays]
    held_refs, rhs_refs, sem = refs[4 + arrays : -3], refs[-3:-1], refs[-1]
    docs = slots_ref.shape[1]
    tile = out_refs[0].shape[0]

    @pl.when(pl.program_id(0) == 0)
    def _():
        for copy in load_all(array_refs, held_refs, sem):
            copy.wait()
        for side in range(2):
            slots = [slots_ref[side, d] for d in range(docs)]
            lay_slabs(rank, parts, slots, side * docs, held_refs, rhs_refs[side])

    for side in range(2):
        acc = lax.dot_general(
            token_refs[side][...], rhs_refs[side][...], nt, preferred_element_type=jnp.float32
        )
        ends = [ends_ref[side, d] for d in range(docs)]
        out_refs[side][...] = by_document(acc, ends, tile, rank)


def mid_partials(own, far, arrays, parts, ends, slots, rank):
    rows, depth = own.shape
    tile = rows_tile(rows)
    docs = slots.shape[1]
    out = jax.ShapeDtypeStruct((rows, rank), jnp.float32)
    return pl.pallas_call(
        functools.partial(mid_kernel, rank, parts, len(arrays)),
        out_shape=(out, out),
        grid_spec=pltpu.PrefetchScalarGridSpec(
            num_scalar_prefetch=2,
            grid=(rows // tile,),
            in_specs=[tiled(own, tile), tiled(far, tile)] + [far_memory()] * len(arrays),
            out_specs=[pl.BlockSpec((tile, rank), lambda i, *_: (i, 0))] * 2,
            scratch_shapes=[pltpu.VMEM(a.shape, a.dtype) for a in arrays]
            + [pltpu.VMEM((docs * rank, depth), jnp.bfloat16)] * 2
            + [pltpu.SemaphoreType.DMA((len(arrays),))],
        ),
        compiler_params=pltpu.CompilerParams(vmem_limit_bytes=20 << 20),
        cost_estimate=light,
    )(ends, slots, own, far, *arrays)


def last_kernel(rank, parts, sums, arrays, slots_ref, ends_ref, at_ref, *refs):
    sum_refs, refs = refs[:sums], refs[sums:]
    mid_refs, token_refs, refs = refs[:2], refs[2:4], refs[4:]
    up_refs, array_refs, out_ref = refs[:2], refs[2 : 2 + arrays], refs[2 + arrays]
    held_refs, rhs_refs, up_ref, sem = refs[3 + arrays : -4], refs[-4:-2], refs[-2], refs[-1]
    docs = slots_ref.shape[0]
    tile, width = out_ref.shape
    ends = [ends_ref[d] for d in range(docs)]

    @pl.when(pl.program_id(0) == 0)
    def _():
        copies = load_all(array_refs, held_refs, sem)
        count = at_ref.shape[1]
        span = up_refs[0].shape[0] // count
        for i in range(2):
            for j in range(count):
                start = pl.multiple_of(at_ref[i, j], span)
                copies.append(
                    pltpu.make_async_copy(
                        up_refs[i].at[pl.ds(j * span, span), :],
                        up_ref.at[pl.ds(start, span), :],
                        sem.at[arrays + i * count + j],
                    )
                )
                copies[-1].start()
        for copy in copies:
            copy.wait()
        slots = [slots_ref[d] for d in range(docs)]
        for i, (first, part) in enumerate(parts):
            lay_slabs(rank, part, slots, first, held_refs, rhs_refs[i])

    acc = lax.dot_general(
        token_refs[0][...], rhs_refs[0][...], nt, preferred_element_type=jnp.float32
    )
    acc += lax.dot_general(
        token_refs[1][...], rhs_refs[1][...], nt, preferred_element_type=jnp.float32
    )
    mid = by_document(acc, ends, tile, rank) + mid_refs[0][...] + mid_refs[1][...]
    flat = up_ref.shape[1]
    row = pl.program_id(0) * tile + lax.broadcasted_iota(jnp.int32, (tile, flat), 0)
    slot, low = jnp.zeros((tile, flat), jnp.int32), 0
    for d, end in enumerate(ends):
        slot = jnp.where((row >= low) & (row < end), slots_ref[d], slot)
        low = end
    adapter = lax.broadcasted_iota(jnp.int32, (tile, flat), 1) // rank
    spread = jnp.where(slot == adapter, jnp.concatenate([mid] * (flat // rank), 1), 0.0)
    spread = spread.astype(jnp.bfloat16)
    columns = sum_refs[1].shape[1]
    for n in range(0, width, columns):
        cols = slice(n, n + columns)
        delta = lax.dot_general(spread, up_ref[cols, :], nt, preferred_element_type=jnp.float32)
        base = sum_refs[0][:, cols] + sum_refs[1 + n // columns][...]
        out_ref[:, cols] = (base + adapter_scale * delta).astype(out_ref.dtype)


def last_values(sums, mids, tokens, ups, up_at, arrays, parts, slots, ends):
    rows, width = sums[0].shape
    rank = mids[0].shape[1]
    flat = ups[0].shape[1]
    tile = rows_tile(rows)
    docs = slots.shape[0]
    return pl.pallas_call(
        functools.partial(last_kernel, rank, parts, len(sums), len(arrays)),
        out_shape=jax.ShapeDtypeStruct((rows, width), jnp.bfloat16),
        grid_spec=pltpu.PrefetchScalarGridSpec(
            num_scalar_prefetch=3,
            grid=(rows // tile,),
            in_specs=[tiled(a, tile) for a in (*sums, *mids, *tokens)]
            + [far_memory()] * (2 + len(arrays)),
            out_specs=pl.BlockSpec((tile, width), lambda i, *_: (i, 0)),
            scratch_shapes=[pltpu.VMEM(a.shape, a.dtype) for a in arrays]
            + [pltpu.VMEM((docs * rank, tokens[0].shape[1]), jnp.bfloat16)] * 2
            + [pltpu.VMEM((width, flat), jnp.bfloat16)]
            + [pltpu.SemaphoreType.DMA((len(arrays) + up_at.size,))],
        ),
        compiler_params=pltpu.CompilerParams(vmem_limit_bytes=58 << 20),
        cost_estimate=light,
    )(slots, ends, up_at, *sums, *mids, *tokens, *ups, *arrays)


def after(value, *earlier):
    return lax.optimization_barrier((value, *earlier))[0]


def make(groups, store):
    depth = store // (rows_y * cores)

    def index(z, y, c):
        return (z * rows_y + y) * cores + c

    def pairs(move):
        return [
            (index(z, y, c), index(*move(z, y, c)))
            for z in range(depth)
            for y in range(rows_y)
            for c in range(cores)
        ]

    def along_z(value, k):
        return lax.ppermute(value, "store", pairs(lambda z, y, c: ((z + k) % depth, y, c)))

    def along_y(value):
        return lax.ppermute(value, "store", pairs(lambda z, y, c: (z, 1 - y, c)))

    def across(value):
        return lax.ppermute(value, "store", pairs(lambda z, y, c: (z, y, 1 - c)))

    def along_x(value):
        return lax.ppermute(value, "groups", [(g, g ^ 1) for g in range(groups)])

    class Line:
        def __init__(self, send, most=2):
            self.send, self.most, self.sent = send, most, []

        def __call__(self, value, *args):
            if len(self.sent) >= self.most:
                value = after(value, self.sent[-self.most])
            self.sent.append(self.send(value, *args))
            return self.sent[-1]

    def per_device(
        tokens,
        input_norm_gain,
        value_matrix,
        adapter_down_factors,
        adapter_up_factors,
        document_lengths,
        document_tenant,
        tenant_adapter_slot,
    ):
        shard, adapters, rank = adapter_down_factors.shape
        flat = adapters * rank
        width = value_matrix.shape[1]
        half, part = shard // 2, 3 * shard // 8
        me = lax.axis_index("store")
        side = lax.axis_index("groups") % 2
        mz, my, mc = me // (rows_y * cores), (me // cores) % rows_y, me % cores
        take = lax.dynamic_slice_in_dim

        down = adapter_down_factors.reshape(shard, flat).T
        up = adapter_up_factors.reshape(flat, -1).T
        bit = up.shape[0] // 2
        cut = part + bit
        rest = half - part
        plan = (
            (0, 0, 0, part, 0, half, 0),
            (1, 0, 0, bit, 0, bit, part),
            (0, 0, 0, rest, part, half + part, cut),
            (0, 0, 0, rest, half + part, part, cut + rest),
            (0, 1, 0, part, half, 0, 0),
            (1, 1, 0, bit, bit, 0, part),
            (2, 2, 1, half, 0, half, 0),
            (2, 3, 1, half, half, 0, 0),
        )
        shapes = [(cut + 2 * rest, width), (cut, width), (flat, half), (flat, half)]
        v_first, v_second, d_first, d_rest = cut_shards(
            [value_matrix, up, down], shapes, plan, side
        )
        v_have, v_miss, d_have = {(0, 0): v_first}, {(0, 0): (v_second, 0)}, {(0, 0): d_first}

        ends = jnp.cumsum(document_lengths, axis=1).astype(jnp.int32)
        slots = jnp.sum(
            (document_tenant[0][:, None] == jnp.arange(adapters, dtype=jnp.int32)[None, :])
            * tenant_adapter_slot[None, :],
            axis=1,
        ).astype(jnp.int32)[None, :]
        near = jnp.concatenate([ends, slots], 0)
        far = across(near)
        ends_both = jnp.concatenate([ends, far[:1]], 0)
        slots_both = jnp.concatenate([slots, far[1:]], 0)
        slots_there = along_x(slots_both)
        d_miss = {(0, 0): (pick_adapters([d_rest], slots_both, rank), 0)}
        chosen = slots_both.size * rank

        order = list(range(depth))
        names = [(k, dy) for k in order for dy in range(rows_y)]
        z, y, x = Line(along_z, 2), Line(along_y, 2), Line(along_x, 2)

        def x_values(names, *earlier):
            got = x(after(jnp.concatenate([v_have[name][:cut] for name in names], 0), *earlier))
            for i, name in enumerate(names):
                v_miss[name] = (got, i * cut)

        def x_down(names, *earlier):
            pieces = [d_have[name] for name in names]
            pieces[0] = after(pieces[0], *earlier)
            got = x(pick_adapters(pieces, slots_there, rank))
            for i, name in enumerate(names):
                d_miss[name] = (got, i * slots_both.size * rank)

        source, up_at = [], []
        for lane_at in (mc, 1 - mc):
            for k, dy in names:
                s = index((mz - k) % depth, my ^ dy, lane_at)
                for c in range(shard // lane):
                    piece = c * lane + jnp.where(c * lane < half, 1, -1) * side * half
                    source.append(s * shard + piece)
                up_at += [(2 * s + side) * bit, (2 * s + 1 - side) * bit]
        source = jnp.stack(source).astype(jnp.int32)
        up_at = jnp.stack(up_at).astype(jnp.int32).reshape(2, -1)
        first, second = names[: len(names) // 2], names[len(names) // 2 :]
        span = len(first) * shard

        def lay():
            arrays = []

            def place(array):
                for i, known in enumerate(arrays):
                    if known is array:
                        return i
                arrays.append(array)
                return len(arrays) - 1

            return arrays, place

        def values(names):
            arrays, place = lay()
            plan = []
            for i, name in enumerate(names):
                h, (m, row) = place(v_have[name]), v_miss[name]
                m, at = place(m), i * shard
                plan += [
                    (h, 0, part, at),
                    (h, cut, cut + half - part, at + part),
                    (m, row, row + part, at + half),
                    (h, cut + half - part, cut + 2 * (half - part), at + half + part),
                ]
            return arrays, tuple(plan)

        def ups(names):
            arrays, place = lay()
            plan = []
            for i, name in enumerate(names):
                h, (m, row) = place(v_have[name]), v_miss[name]
                plan.append((h, part, cut, 2 * i * bit))
                plan.append((place(m), row + part, row + cut, (2 * i + 1) * bit))
            return gather_rows(arrays, tuple(plan))

        def slabs(place, names, have, miss):
            out = []
            for i, name in enumerate(names):
                m, row = miss[name]
                out.append((i * shard, place(have[name]), place(m), row))
            return tuple(out)

        ks = order[1:]
        early, last = ks[:-1], ks[-1]
        own, own_rest, other, other_rest = norm_in_order(
            tokens, input_norm_gain, source, [span] * 4
        )
        partner, partner_rest = across(other), across(other_rest)
        for k in ks:
            v_have[k, 0] = z(v_have[0, 0], k)
        for k in ks:
            d_have[k, 0] = z(d_have[0, 0], k)
        v_have[0, 1] = y(v_have[0, 0])
        d_have[0, 1] = y(d_have[0, 0])
        x_values([(0, 1)], slots_there)
        x_down([(0, 1)])
        for i, k in enumerate(early):
            pins = [partner, partner_rest][: i + 1] + [d_miss[0, 1][0]] * i
            v_have[k, 1] = y(after(v_have[k, 0], *pins))
            x_values([(k, 0)])
        for k in early:
            x_values([(k, 1)])
        v_have[last, 1] = y(v_have[last, 0])
        x_values([(last, 0)])
        for k in early:
            d_have[k, 1] = y(d_have[k, 0])
        arrays, plan = values(first)
        sums = value_sums(
            after(own, v_have[last, 1], d_have[early[0], 1]), partner, arrays, plan, width
        )
        x_values([(last, 1)], sums[0])
        for k in early:
            x_down([(k, 0)])
        for k in early:
            x_down([(k, 1)])
        d_have[last, 1] = y(d_have[last, 0])
        x_down([(last, 0)])

        arrays, plan = values(second)
        ready = [d_have[last, 0], *[d_have[k, 1] for k in early]]
        sum_own, *sum_far = value_sums(
            after(own_rest, *ready), partner_rest, arrays, plan, width, sums, jnp.bfloat16
        )
        sums = (sum_own, *[across(part) for part in sum_far])
        up_lane = ups(names)
        up_both = (up_lane, across(up_lane))

        arrays, place = lay()
        parts = slabs(place, first, d_have, d_miss)
        mid_own, mid_far = mid_partials(own, partner, arrays, parts, ends_both, slots_both, rank)
        mids = (mid_own, across(mid_far))
        x_down([(last, 1)])

        arrays, place = lay()
        parts = [(0, slabs(place, second, d_have, d_miss))]
        done = d_have[last, 1]
        far_have = {n: across(after(d_have[n], done)) for n in second}
        far_miss = {n: (across(after(d_miss[n][0], done)), d_miss[n][1]) for n in second}
        parts.append((slots.shape[1], slabs(place, second, far_have, far_miss)))
        return last_values(
            sums,
            mids,
            (own_rest, other_rest),
            up_both,
            up_at,
            arrays,
            tuple(parts),
            slots[0],
            ends[0],
        )

    return per_device


def solution(mesh):
    in_specs = (
        P(("groups", "store"), None),
        P(),
        P("store", None),
        P("store", None, None),
        P(None, None, "store"),
        P(("groups", "store"), None),
        P(("groups", "store"), None),
        P(),
    )
    out_specs = P(("groups", "store"), None)
    groups, store = mesh.shape["groups"], mesh.shape["store"]

    def run(*args):
        shard = args[2].shape[0]
        cut = shard % (4 * lane) == 0 and args[4].shape[2] % 32 == 0 and store > 4 and store % (rows_y * cores) == 0 and groups % 2 == 0
        return (make(groups, store) if cut else plain)(*args)

    return jax.shard_map(
        run, mesh=mesh, in_specs=in_specs, out_specs=out_specs, check_vma=False
    )
```
